128 devices in a mesh: rep: 2 (over core), dp: 8 (over y_hi, x), tensor: 8 (over z, y_lo).
Axes of the slice: x: 4, y: 4 (y_hi: 2, y_lo: 2; y = y_hi * 2 + y_lo), z: 4, core: 2. Of those that a mesh axis runs over, the one named last changes fastest.
Arguments:
- frames: bfloat16 [64, 384, 8, 128], P(('rep', 'dp'), 'tensor'), may hold values from -6 to 6
- weight: bfloat16 [384, 3, 3, 3, 384], P('tensor'), may hold values from -0.0625 to 0.0625
- cotangent: bfloat16 [64, 384, 8, 128], P(('rep', 'dp'), 'tensor'), may hold values from -6 to 6
- prev_owner: int32 [16], replicated, may hold values from -1 to 15, as said below
- lengths: int32 [16], replicated, may hold values from 1 to 4, as said below
Outputs:
- output: bfloat16 [64, 384, 8, 128], P(('rep', 'dp'), 'tensor')
- input_grad: float32 [64, 384, 8, 128], P(('rep', 'dp'), 'tensor')
- weight_grad: float32 [384, 3, 3, 3, 384], P('tensor')
The draws below stay inside these ranges and needn't reach their ends.
Inputs may be any that keep to these rules, and one draw needn't show every extreme that they name: `prev_owner`: each segment index appears at most once; segment 0 of every clip has -1; clips form chains without loops. A segment named in prev_owner has lengths 4; only a clip's last segment may be shorter.
All inputs are finite; a program needn't handle non-finite values.
Results may differ from the reference program's by a relative error of at most 0.0034.
Values may be sent and summed in bfloat16 or wider, within the bound.
No kernel may reach another device: no remote copies, remote signals or barrier semaphores. Data moves between devices by JAX's collectives and lax.ppermute only.
A program may use at most 128 MiB of HBM per device.

```python
import jax
import jax.numpy as jnp
from jax import lax

C = 384
SEG_FRAMES = 4
TILE_H = 8
TILE_W = 128
SEGMENTS = 16
FRAMES = 64


def clip_layout(key):
    rest = jax.random.permutation(jax.random.fold_in(key, 11), SEGMENTS - 1).astype(jnp.int32)
    order = jnp.concatenate([jnp.array([SEGMENTS - 1], jnp.int32), rest])
    starts = jax.random.randint(jax.random.fold_in(key, 12), (SEGMENTS,), 0, 3) == 0
    starts = starts.at[0].set(True).at[1].set(False)
    before = jnp.roll(order, 1)
    prev_in_order = jnp.where(starts, -1, before).astype(jnp.int32)
    next_starts = jnp.concatenate([starts[1:], jnp.array([True])])
    short = jax.random.randint(jax.random.fold_in(key, 13), (SEGMENTS,), 1, SEG_FRAMES + 1)
    length_in_order = jnp.where(next_starts, short, SEG_FRAMES).astype(jnp.int32)
    prev_owner = jnp.zeros((SEGMENTS,), jnp.int32).at[order].set(prev_in_order)
    lengths = jnp.zeros((SEGMENTS,), jnp.int32).at[order].set(length_in_order)
    return (prev_owner, lengths)


def draw_prev_owner(key, part):
    return clip_layout(key)[0]


def draw_lengths(key, part):
    return clip_layout(key)[1]


def steps_of(rng, dims, cuts, low, largest):
    gain = 1.0
    for position, shards_of in cuts:
        draws = jax.random.uniform(jax.random.fold_in(jax.random.fold_in(rng, 6), position), (shards_of,), jnp.float32, low / len(cuts), largest / len(cuts))
        gain = gain * jnp.repeat(jnp.exp(draws), dims[position] // shards_of).reshape((-1,) + (1,) * (len(dims) - 1 - position))
    return gain


def bell_draw(rng, extent, scale, bound, split=(), kind=jnp.bfloat16):
    result = scale * jax.random.normal(rng, extent, jnp.float32)
    if split:
        result = result * steps_of(rng, extent, split, -0.22, 0.18)
    return jnp.clip(result, -bound, bound).astype(kind)


def setup_inputs(seed: int = 0) -> dict:
    key_list = jax.random.split(jax.random.key(seed), 6)
    return {
        "frames": bell_draw(key_list[0], (FRAMES, C, TILE_H, TILE_W), 1.0, 6.0, ((0, 16), (1, 8))),
        "weight": bell_draw(key_list[1], (C, 3, 3, 3, C), (27 * C) ** -0.5, 0.0625, ((0, 8),)),
        "cotangent": bell_draw(key_list[2], (FRAMES, C, TILE_H, TILE_W), 1.0, 6.0, ((0, 16), (1, 8))),
        "prev_owner": draw_prev_owner(jax.random.fold_in(key_list[5], 71), 0),
        "lengths": draw_lengths(jax.random.fold_in(key_list[5], 71), 0),
    }


def convolve(padded, weight):
    seg_len = padded.shape[0] - 2
    height = padded.shape[2] - 2
    tile_width = padded.shape[3] - 2
    summed = jnp.zeros((seg_len, weight.shape[0], height, tile_width), jnp.float32)
    for tap_t in range(3):
        for tap_h in range(3):
            for tap_w in range(3):
                window = padded[tap_t:tap_t + seg_len, :, tap_h:tap_h + height, tap_w:tap_w + tile_width]
                summed = summed + jnp.einsum('fchw,oc->fohw', window, weight[:, tap_t, tap_h, tap_w, :], precision=lax.Precision.HIGHEST)
    return summed

def reference(frames, weight, cotangent, prev_owner, lengths):
    segments = frames.reshape(SEGMENTS, SEG_FRAMES, C, TILE_H, TILE_W)
    cotangents = cotangent.reshape(SEGMENTS, SEG_FRAMES, C, TILE_H, TILE_W)
    tail_rows = segments[:, SEG_FRAMES - 2:]
    source = jnp.maximum(prev_owner, 0).astype(jnp.int32)
    cached = jnp.where((prev_owner >= 0)[:, None, None, None, None], tail_rows[source], jnp.zeros_like(tail_rows))
    extended = jnp.concatenate([cached, segments], 1).astype(jnp.float32)
    frame_mask = (jnp.arange(SEG_FRAMES)[None, :] < lengths[:, None]).astype(jnp.float32)[:, :, None, None, None]
    weight_wide = weight.astype(jnp.float32)

    def per_segment(carry, segment_items):
        extended_one, grad_one, keep_one = segment_items
        padded = jnp.pad(extended_one, ((0, 0), (0, 0), (1, 1), (1, 1)))
        convolved, pullback = jax.vjp(convolve, padded, weight_wide)
        masked = grad_one.astype(jnp.float32) * keep_one
        grad_padded, grad_weight = pullback(masked)
        return (carry + grad_weight, ((convolved * keep_one).astype(jnp.bfloat16), grad_padded[:, :, 1:-1, 1:-1]))
    start = jnp.zeros((C, 3, 3, 3, C), jnp.float32)
    weight_total, (outputs, grad_extended) = lax.scan(per_segment, start, (extended, cotangents, frame_mask))
    grad_cached = grad_extended[:, :2]
    matches = (prev_owner[None, :] == jnp.arange(SEGMENTS, dtype=jnp.int32)[:, None]).astype(jnp.float32)
    received = jnp.tensordot(matches, grad_cached, axes=1, precision=lax.Precision.HIGHEST)
    input_grad = grad_extended[:, 2:].at[:, SEG_FRAMES - 2:].add(received)
    scale = 1.0 / jnp.sqrt(jnp.float32(FRAMES * TILE_H * TILE_W))
    return (outputs.reshape(FRAMES, C, TILE_H, TILE_W), input_grad.reshape(FRAMES, C, TILE_H, TILE_W), weight_total * scale)
```

```python
import math

import jax
import jax.numpy as jnp
from jax import lax
from jax.experimental import pallas as pl
from jax.experimental.pallas import tpu as pltpu
from jax.sharding import PartitionSpec as P

BF16 = jnp.bfloat16
F32 = jnp.float32
VMEM_LIMIT = 56 * 1024 * 1024
ANY = pl.BlockSpec(memory_space=pl.ANY)
VMEM = pl.BlockSpec(memory_space=pltpu.VMEM)
SMEM = pl.BlockSpec(memory_space=pltpu.SMEM)

PLACES = ((0, 0), (0, 1), (1, 0), (3, 0), (1, 1), (3, 1), (2, 0), (2, 1))


def tensor_index(ring, pair):
    return ring * 2 + pair


def dp_index(ring, pair):
    return pair * 4 + ring


class Group:
    def __init__(self, name, index_of, coords):
        self.name = name
        self.index_of = index_of
        me = lax.axis_index(name)
        self.ring, self.pair = coords(me)
        cells = [(r, p) for r in range(4) for p in range(2)]
        self.perm_up = [(index_of(r, p), index_of((r + 1) % 4, p)) for r, p in cells]
        self.perm_down = [(index_of(r, p), index_of((r + 3) % 4, p)) for r, p in cells]
        self.perm_swap = [(index_of(r, p), index_of(r, 1 - p)) for r, p in cells]

    def up(self, x):
        return lax.ppermute(x, self.name, self.perm_up)

    def down(self, x):
        return lax.ppermute(x, self.name, self.perm_down)

    def swap(self, x):
        return lax.ppermute(x, self.name, self.perm_swap)

    def absolute(self):
        return [self.index_of((self.ring + dr) % 4, self.pair ^ dp) for dr, dp in PLACES]

    def gather(self, x):
        half = x.shape[0] // 2
        pair, prev, following = self.swap(x), self.up(x), self.down(x)
        pair_next = self.swap(following)
        pair_prev = self.up(pair)
        second = self.down(following)
        far_a = self.down(pair_next[:half])
        far_b = self.up(pair_prev[half:])
        return [x, pair, following, prev, pair_next, pair_prev, second, far_a, far_b]

    def scatter_sum(self, parts):
        own, pair, following, prev, pair_next, pair_prev, second, far = parts
        half = far.shape[0] // 2
        add = lambda a, b: (a.astype(F32) + b.astype(F32)).astype(BF16)
        in_a = self.up(far[:half])
        in_b = self.down(far[half:])
        from_prev_last = self.down(prev)
        pair_next = jnp.concatenate([add(pair_next[:half], in_a), pair_next[half:]], 0)
        pair_prev = jnp.concatenate([pair_prev[:half], add(pair_prev[half:], in_b)], 0)
        got_swap = self.swap(pair_next)
        got_down = self.down(pair_prev)
        got_up = self.up(second)
        following = (following.astype(F32) + got_swap.astype(F32) + got_up.astype(F32)).astype(BF16)
        pair = add(pair, got_down)
        last_up = self.up(following)
        last_swap = self.swap(pair)
        return own.astype(F32) + from_prev_last.astype(F32) + last_up.astype(F32) + last_swap.astype(F32)


def shifted(x, by):
    lanes = x.shape[-1]
    column = lax.broadcasted_iota(jnp.int32, x.shape, x.ndim - 1) % 128
    rolled = pltpu.roll(x, by % lanes, x.ndim - 1)
    edge = 0 if by == 1 else 127
    return jnp.where(column == edge, 0.0, rolled)


def fill_taps(m_ref, head_ref, taps):
    rows, width = m_ref.shape[0], m_ref.shape[1]
    taps[0] = jnp.zeros(taps.shape[1:], BF16)
    taps[rows + 1] = jnp.zeros(taps.shape[1:], BF16)
    for h in range(rows):
        plain = jnp.concatenate([m_ref[h], head_ref[h]], 1)
        wide = plain.astype(F32)
        taps[h + 1, 0:width] = shifted(wide, -1).astype(BF16)
        taps[h + 1, width : 2 * width] = plain
        taps[h + 1, 2 * width : 3 * width] = shifted(wide, 1).astype(BF16)


def input_grad_kernel(place_ref, m_ref, head_ref, w_ref, *rest):
    outs, (taps, wt, parts, sems) = rest[:8], rest[8:]
    rows, width, lanes = m_ref.shape
    channels = w_ref.shape[2]
    fill_taps(m_ref, head_ref, taps)
    depth = 3 * 3 * width
    for a in range(3):
        block = jnp.concatenate([w_ref[a * 3 + b] for b in range(3)], 0)
        wt[:, a * depth : (a + 1) * depth] = block.T

    @pl.loop(0, rows)
    def _(h):
        stack = jnp.reshape(taps[pl.ds(h, 3)], (depth, taps.shape[2]))
        for start in range(0, lanes, 256):
            rhs = jnp.concatenate(
                [stack[:, (2 - a) * 128 + start : (2 - a) * 128 + start + 256] for a in range(3)], 0
            )
            total = jnp.dot(wt[...], rhs, preferred_element_type=F32).astype(BF16)
            for t in range(8):
                parts[t, h, :, start : start + 256] = total[t * width : (t + 1) * width]

    copies = [
        pltpu.make_async_copy(parts.at[place_ref[r]], outs[r], sems.at[r]) for r in range(8)
    ]
    for copy in copies:
        copy.start()
    for copy in copies:
        copy.wait()


def load_channels(place_ref, blocks, x, sems):
    rows, width = blocks[0].shape[0], blocks[0].shape[1]
    half = rows // 2
    x[0] = jnp.zeros(x.shape[1:], BF16)
    x[rows + 1] = jnp.zeros(x.shape[1:], BF16)
    copies = []
    for r, block in enumerate(blocks):
        place = place_ref[min(r, 7)]
        channel = pl.ds(pl.multiple_of(place * width, 16), width)
        if r < 7:
            target = x.at[pl.ds(1, rows), channel]
        else:
            target = x.at[pl.ds(1 + (r - 7) * half, half), channel]
        copies.append(pltpu.make_async_copy(block, target, sems.at[r]))
    for copy in copies:
        copy.start()
    for copy in copies:
        copy.wait()


def forward_kernel(place_ref, *rest):
    blocks, (w_ref, out_ref, carry_ref, x, sems) = rest[:9], rest[9:]
    rows, width, lanes = out_ref.shape
    load_channels(place_ref, blocks, x, sems)
    zero = jnp.zeros((width, 128), F32)

    @pl.loop(0, rows)
    def _(h):
        stack = jnp.reshape(x[pl.ds(h, 3)], (3 * x.shape[1], lanes))
        lhs = jnp.concatenate(
            [
                jnp.concatenate([w_ref[a * 3 + 2 - b] for a in range(3)], 0)
                for b in range(3)
            ],
            1,
        )
        y = jnp.dot(lhs, stack, preferred_element_type=F32)
        sums = []
        for e in range(3):
            frames = []
            for g in range(lanes // 128 + 2):
                terms = []
                for a in range(3):
                    f = g + a - 2
                    if 0 <= f < lanes // 128:
                        row = (a * 3 + e) * width
                        terms.append(y[row : row + width, f * 128 : f * 128 + 128])
                total = terms[0]
                for term in terms[1:]:
                    total = total + term
                frames.append(total)
            sums.append(jnp.concatenate(frames, 1))
        result = sums[1] + shifted(sums[0], 1) + shifted(sums[2], -1)
        out_ref[h] = result[:, :lanes]
        carry_ref[h] = result[:, lanes:].astype(BF16)


def kernel_grad_kernel(place_ref, *rest):
    blocks, (m_ref, head_ref, out_ref, x, taps, total, sems) = rest[:9], rest[9:]
    rows, width, lanes = m_ref.shape
    load_channels(place_ref, blocks, x, sems)
    fill_taps(m_ref, head_ref, taps)
    depth = 9 * width
    total[...] = jnp.zeros(total.shape, F32)

    @pl.loop(0, rows)
    def _(h):
        stack = jnp.reshape(taps[pl.ds(h, 3)], (depth, taps.shape[2]))
        right = x[h + 1]
        for a in range(3):
            left = stack[:, (2 - a) * 128 : (2 - a) * 128 + lanes]
            total[a] += lax.dot_general(
                left, right, (((1,), (1,)), ((), ())), preferred_element_type=F32
            )

    out_ref[9 * depth :, :] = jnp.zeros((out_ref.shape[0] - 9 * depth, 128), F32)
    for a in range(3):
        for block in range(3):
            row = (a * 3 + block) * depth
            out_ref[row : row + depth, :] = total[a, :, block * 128 : block * 128 + 128]


def params():
    return pltpu.CompilerParams(vmem_limit_bytes=VMEM_LIMIT)


def cost(flops, size):
    return pl.CostEstimate(flops=flops, bytes_accessed=size, transcendentals=0)


FLOPS = 2 * 27 * 48 * 384 * 4096


def input_partials(place, m, head, weight):
    rows, width, lanes = m.shape
    channels = weight.shape[2]
    return pl.pallas_call(
        input_grad_kernel,
        out_shape=[jax.ShapeDtypeStruct((rows, width, lanes), BF16)] * 8,
        in_specs=[SMEM, VMEM, VMEM, VMEM],
        out_specs=[ANY] * 8,
        scratch_shapes=[
            pltpu.VMEM((rows + 2, 3 * width, lanes + 256), BF16),
            pltpu.VMEM((channels, 27 * width), BF16),
            pltpu.VMEM((8, rows, width, lanes), BF16),
            pltpu.SemaphoreType.DMA((8,)),
        ],
        compiler_params=params(),
        cost_estimate=cost(FLOPS, 5_000_000),
        name="input_partials",
    )(place, m, head, weight)


def forward(place, blocks, weight):
    rows, width, lanes = blocks[0].shape
    channels = weight.shape[2]
    return pl.pallas_call(
        forward_kernel,
        out_shape=[
            jax.ShapeDtypeStruct((rows, width, lanes), F32),
            jax.ShapeDtypeStruct((rows, width, 256), BF16),
        ],
        in_specs=[SMEM] + [ANY] * 9 + [VMEM],
        out_specs=[VMEM, VMEM],
        scratch_shapes=[
            pltpu.VMEM((rows + 2, channels, lanes), BF16),
            pltpu.SemaphoreType.DMA((9,)),
        ],
        compiler_params=params(),
        cost_estimate=cost(FLOPS, 5_000_000),
        name="forward",
    )(place, *blocks, weight)


def kernel_grad(place, blocks, m, head):
    rows, width, lanes = m.shape
    channels = 8 * width
    return pl.pallas_call(
        kernel_grad_kernel,
        out_shape=jax.ShapeDtypeStruct((4096, 128), F32),
        in_specs=[SMEM] + [ANY] * 9 + [VMEM, VMEM],
        out_specs=VMEM,
        scratch_shapes=[
            pltpu.VMEM((rows + 2, channels, lanes), BF16),
            pltpu.VMEM((rows + 2, 3 * width, lanes + 256), BF16),
            pltpu.VMEM((3, 9 * width, channels), F32),
            pltpu.SemaphoreType.DMA((9,)),
        ],
        compiler_params=params(),
        cost_estimate=cost(FLOPS, 6_000_000),
        name="kernel_grad",
    )(place, *blocks, m, head)


def to_rows(x):
    f, c, h, w = x.shape
    return x.transpose(2, 1, 0, 3).reshape(h, c, f * w)


def from_rows(x):
    h, c, lanes = x.shape
    return x.reshape(h, c, lanes // 128, 128).transpose(2, 1, 0, 3)


def core_swap(x):
    return lax.ppermute(x, "rep", [(0, 1), (1, 0)])


def route(dp, payload, source):
    rep, me = lax.axis_index("rep"), lax.axis_index("dp")
    blocks = dp.gather(payload)
    blocks = blocks[:7] + [jnp.concatenate(blocks[7:], 0)]
    places = dp.absolute()

    def pick(wanted):
        result = jnp.zeros_like(payload)
        for place, block in zip(places, blocks):
            result = jnp.where(wanted == place, block, result)
        return result

    mine = source[rep * 8 + me]
    other = source[(1 - rep) * 8 + me]
    crossed = core_swap(pick(jnp.maximum(other, 0) % 8))
    direct = pick(jnp.maximum(mine, 0) % 8)
    result = jnp.where(jnp.maximum(mine, 0) // 8 == rep, direct, crossed)
    return jnp.where(mine >= 0, result, jnp.zeros_like(result))


def summed_kernel_grad(dp, local, scale):
    rep = lax.axis_index("rep")
    halves = local.reshape(2, 2048, 128)
    mine = lax.dynamic_index_in_dim(halves, rep, 0, False)
    theirs = lax.dynamic_index_in_dim(halves, 1 - rep, 0, False)
    pair = mine + core_swap(theirs)
    spread = lax.all_to_all(pair.astype(BF16).reshape(8, 256, 128), "dp", 0, 0, tiled=True)
    share = (jnp.sum(spread.astype(F32), 0) * scale).astype(BF16)
    blocks = dp.gather(share)
    blocks = blocks[:7] + [jnp.concatenate(blocks[7:], 0)]
    half = jnp.zeros((8, 256, 128), BF16)
    for place, block in zip(dp.absolute(), blocks):
        half = lax.dynamic_update_slice(half, block[None], (place, 0, 0))
    half = half.reshape(2048, 128)
    there = core_swap(half)
    low = jnp.where(rep == 0, half, there)
    high = jnp.where(rep == 0, there, half)
    return jnp.concatenate([low, high], 0)


def per_device(frames, weight, cotangent, prev_owner, lengths):
    seg_len, width, height, columns = frames.shape
    channels = weight.shape[4]
    rep, me = lax.axis_index("rep"), lax.axis_index("dp")
    member = rep * 8 + me
    tensor = Group("tensor", tensor_index, lambda i: (i // 2, i % 2))
    dp = Group("dp", dp_index, lambda i: (i % 4, i // 4))
    place = jnp.stack(tensor.absolute()).astype(jnp.int32)
    segments = jnp.arange(prev_owner.shape[0], dtype=jnp.int32)
    follows = prev_owner[None, :] == segments[:, None]
    follower = jnp.max(jnp.where(follows, segments[None, :], -1), 1)

    keep = jnp.arange(seg_len) < lengths[member]
    x = to_rows(frames)
    m = to_rows(jnp.where(keep[:, None, None, None], cotangent, jnp.zeros_like(cotangent)))
    rows = weight.transpose(1, 2, 3, 0, 4)[:, ::-1].reshape(9, 3 * width, channels)

    head = route(dp, m[:, :, :256], follower)
    blocks = tensor.gather(x)
    partials = input_partials(place, m, head, rows)
    input_grad = from_rows(tensor.scatter_sum(partials))

    local = kernel_grad(place, blocks, m, head)
    cells = prev_owner.shape[0] * seg_len * height * columns
    total = summed_kernel_grad(dp, local, 1.0 / math.sqrt(cells))
    total = total[: 81 * width].reshape(3, 3, 3, 3, width, 128)
    weight_grad = total[:, :, ::-1].transpose(4, 0, 2, 3, 1, 5).reshape(weight.shape).astype(F32)

    conv, carry = forward(place, blocks, rows)
    received = route(dp, carry, prev_owner)
    conv = conv + jnp.pad(received.astype(F32), ((0, 0), (0, 0), (0, 256)))
    live = jnp.repeat(keep, columns)[None, None, :]
    output = from_rows(jnp.where(live, conv, 0.0).astype(BF16))
    return (output, input_grad, weight_grad)


def solution(mesh):
    split = P(("rep", "dp"), "tensor", None, None)
    kernel = P("tensor", None, None, None, None)
    return jax.shard_map(
        per_device,
        mesh=mesh,
        in_specs=(split, kernel, split, P(), P()),
        out_specs=(split, split, kernel),
        check_vma=False,
    )
```

```python
import math

import jax
import jax.numpy as jnp
from jax import lax
from jax.experimental import pallas as pl
from jax.experimental.pallas import tpu as pltpu
from jax.sharding import PartitionSpec as P

BF16 = jnp.bfloat16
F32 = jnp.float32
VMEM_LIMIT = 56 * 1024 * 1024
ANY = pl.BlockSpec(memory_space=pl.ANY)
VMEM = pl.BlockSpec(memory_space=pltpu.VMEM)
SMEM = pl.BlockSpec(memory_space=pltpu.SMEM)

PLACES = ((0, 0), (0, 1), (1, 0), (3, 0), (1, 1), (3, 1), (2, 0), (2, 1))


def tensor_index(ring, pair):
    return ring * 2 + pair


class Group:
    def __init__(self, name, index_of, coords):
        self.name = name
        self.index_of = index_of
        me = lax.axis_index(name)
        self.ring, self.pair = coords(me)
        cells = [(r, p) for r in range(4) for p in range(2)]
        self.perm_up = [(index_of(r, p), index_of((r + 1) % 4, p)) for r, p in cells]
        self.perm_down = [(index_of(r, p), index_of((r + 3) % 4, p)) for r, p in cells]
        self.perm_swap = [(index_of(r, p), index_of(r, 1 - p)) for r, p in cells]

    def up(self, x):
        return lax.ppermute(x, self.name, self.perm_up)

    def down(self, x):
        return lax.ppermute(x, self.name, self.perm_down)

    def swap(self, x):
        return lax.ppermute(x, self.name, self.perm_swap)

    def absolute(self):
        return [self.index_of((self.ring + dr) % 4, self.pair ^ dp) for dr, dp in PLACES]

    def gather(self, x):
        half = x.shape[0] // 2
        pair, prev, following = self.swap(x), self.up(x), self.down(x)
        pair_next = self.swap(following)
        pair_prev = self.up(pair)
        second = self.down(following)
        far_a = self.down(pair_next[:half])
        far_b = self.up(pair_prev[half:])
        return [x, pair, following, prev, pair_next, pair_prev, second, far_a, far_b]


def shifted(x, by):
    lanes = x.shape[-1]
    column = lax.broadcasted_iota(jnp.int32, x.shape, x.ndim - 1) % 128
    rolled = pltpu.roll(x, by % lanes, x.ndim - 1)
    edge = 0 if by == 1 else 127
    return jnp.where(column == edge, 0.0, rolled)


def fill_taps(m_ref, head_ref, taps):
    rows, width = m_ref.shape[0], m_ref.shape[1]
    taps[0] = jnp.zeros(taps.shape[1:], BF16)
    taps[rows + 1] = jnp.zeros(taps.shape[1:], BF16)
    for h in range(rows):
        plain = jnp.concatenate([m_ref[h], head_ref[h]], 1)
        wide = plain.astype(F32)
        taps[h + 1, 0:width] = shifted(wide, -1).astype(BF16)
        taps[h + 1, width : 2 * width] = plain
        taps[h + 1, 2 * width : 3 * width] = shifted(wide, 1).astype(BF16)


def input_grad_kernel(m_ref, head_ref, w_ref, out_ref, taps, wt, parts, sems):
    rows, width, lanes = m_ref.shape
    fill_taps(m_ref, head_ref, taps)
    depth = 3 * 3 * width
    for a in range(3):
        block = jnp.concatenate([w_ref[a * 3 + b] for b in range(3)], 0)
        wt[:, a * depth : (a + 1) * depth] = block.T

    copies = []
    for h in range(rows):
        stack = jnp.reshape(taps[h : h + 3], (depth, taps.shape[2]))
        for start in range(0, lanes, 256):
            rhs = jnp.concatenate(
                [stack[:, (2 - a) * 128 + start : (2 - a) * 128 + start + 256] for a in range(3)], 0
            )
            total = jnp.dot(wt[...], rhs, preferred_element_type=F32).astype(BF16)
            for t in range(8):
                parts[t, h, :, start : start + 256] = total[t * width : (t + 1) * width]
        copies.append(pltpu.make_async_copy(parts.at[:, h], out_ref.at[:, h], sems.at[h]))
        copies[-1].start()
    for copy in copies:
        copy.wait()


def pick_kernel(row_ref, from_ref, own_ref, other_ref, out_ref):
    for d in range(out_ref.shape[0]):
        own, other = own_ref[row_ref[d]], other_ref[row_ref[d]]
        chosen = jnp.where(from_ref[d] == 1, own, other)
        out_ref[d] = jnp.where(from_ref[d] == 0, jnp.zeros_like(chosen), chosen)


def load_channels(place_ref, blocks, x, sems):
    rows, width = blocks[0].shape[0], blocks[0].shape[1]
    half = rows // 2
    x[0] = jnp.zeros(x.shape[1:], BF16)
    x[rows + 1] = jnp.zeros(x.shape[1:], BF16)
    copies = []
    for r, block in enumerate(blocks):
        place = place_ref[min(r, 7)]
        channel = pl.ds(pl.multiple_of(place * width, 16), width)
        if r < 7:
            target = x.at[pl.ds(1, rows), channel]
        else:
            target = x.at[pl.ds(1 + (r - 7) * half, half), channel]
        copies.append(pltpu.make_async_copy(block, target, sems.at[r]))
    for copy in copies:
        copy.start()
    for copy in copies:
        copy.wait()


def forward_kernel(place_ref, *rest):
    blocks, (w_ref, out_ref, carry_ref, x, sems) = rest[:9], rest[9:]
    rows, width, lanes = out_ref.shape
    load_channels(place_ref, blocks, x, sems)
    lhs = jnp.concatenate(
        [jnp.concatenate([w_ref[a * 3 + 2 - b] for a in range(3)], 0) for b in range(3)], 1
    )
    for h in range(rows):
        stack = jnp.reshape(x[h : h + 3], (3 * x.shape[1], lanes))
        y = jnp.dot(lhs, stack, preferred_element_type=F32)
        sums = []
        for e in range(3):
            frames = []
            for g in range(lanes // 128 + 2):
                terms = []
                for a in range(3):
                    f = g + a - 2
                    if 0 <= f < lanes // 128:
                        row = (a * 3 + e) * width
                        terms.append(y[row : row + width, f * 128 : f * 128 + 128])
                total = terms[0]
                for term in terms[1:]:
                    total = total + term
                frames.append(total)
            sums.append(jnp.concatenate(frames, 1))
        result = sums[1] + shifted(sums[0], 1) + shifted(sums[2], -1)
        out_ref[h] = result[:, :lanes]
        carry_ref[h] = result[:, lanes:].astype(BF16)


def kernel_grad_kernel(place_ref, *rest):
    blocks, (m_ref, head_ref, out_ref, x, taps, total, sems) = rest[:9], rest[9:]
    rows, width, lanes = m_ref.shape
    load_channels(place_ref, blocks, x, sems)
    fill_taps(m_ref, head_ref, taps)
    depth = 9 * width
    total[...] = jnp.zeros(total.shape, F32)

    @pl.loop(0, rows)
    def _(h):
        stack = jnp.reshape(taps[pl.ds(h, 3)], (depth, taps.shape[2]))
        right = x[h + 1]
        for a in range(3):
            left = stack[:, (2 - a) * 128 : (2 - a) * 128 + lanes]
            total[a] += lax.dot_general(
                left, right, (((1,), (1,)), ((), ())), preferred_element_type=F32
            )

    out_ref[9 * depth :, :] = jnp.zeros((out_ref.shape[0] - 9 * depth, 128), F32)
    for a in range(3):
        for block in range(3):
            row = (a * 3 + block) * depth
            out_ref[row : row + depth, :] = total[a, :, block * 128 : block * 128 + 128]


def params():
    return pltpu.CompilerParams(vmem_limit_bytes=VMEM_LIMIT)


def cost(flops, size):
    return pl.CostEstimate(flops=flops, bytes_accessed=size, transcendentals=0)


FLOPS = 2 * 27 * 48 * 384 * 4096


def input_partials(m, head, weight):
    rows, width, lanes = m.shape
    channels = weight.shape[2]
    return pl.pallas_call(
        input_grad_kernel,
        out_shape=jax.ShapeDtypeStruct((8, rows, width, lanes), BF16),
        in_specs=[VMEM, VMEM, VMEM],
        out_specs=ANY,
        scratch_shapes=[
            pltpu.VMEM((rows + 2, 3 * width, lanes + 256), BF16),
            pltpu.VMEM((channels, 27 * width), BF16),
            pltpu.VMEM((8, rows, width, lanes), BF16),
            pltpu.SemaphoreType.DMA((rows,)),
        ],
        compiler_params=params(),
        cost_estimate=cost(FLOPS, 5_000_000),
        name="input_partials",
    )(m, head, weight)


def pick(row, origin, own, other):
    return pl.pallas_call(
        pick_kernel,
        out_shape=jax.ShapeDtypeStruct(own.shape, own.dtype),
        in_specs=[SMEM, SMEM, VMEM, VMEM],
        out_specs=VMEM,
        compiler_params=params(),
        name="pick",
    )(row, origin, own, other)


def forward(place, blocks, weight):
    rows, width, lanes = blocks[0].shape
    channels = weight.shape[2]
    return pl.pallas_call(
        forward_kernel,
        out_shape=[
            jax.ShapeDtypeStruct((rows, width, lanes), F32),
            jax.ShapeDtypeStruct((rows, width, 256), BF16),
        ],
        in_specs=[SMEM] + [ANY] * 9 + [VMEM],
        out_specs=[VMEM, VMEM],
        scratch_shapes=[
            pltpu.VMEM((rows + 2, channels, lanes), BF16),
            pltpu.SemaphoreType.DMA((9,)),
        ],
        compiler_params=params(),
        cost_estimate=cost(FLOPS, 5_000_000),
        name="forward",
    )(place, *blocks, weight)


def kernel_grad(place, blocks, m, head):
    rows, width, lanes = m.shape
    channels = 8 * width
    return pl.pallas_call(
        kernel_grad_kernel,
        out_shape=jax.ShapeDtypeStruct((4096, 128), F32),
        in_specs=[SMEM] + [ANY] * 9 + [VMEM, VMEM],
        out_specs=VMEM,
        scratch_shapes=[
            pltpu.VMEM((rows + 2, channels, lanes), BF16),
            pltpu.VMEM((rows + 2, 3 * width, lanes + 256), BF16),
            pltpu.VMEM((3, 9 * width, channels), F32),
            pltpu.SemaphoreType.DMA((9,)),
        ],
        compiler_params=params(),
        cost_estimate=cost(FLOPS, 6_000_000),
        name="kernel_grad",
    )(place, *blocks, m, head)


def to_rows(x):
    f, c, h, w = x.shape
    return x.transpose(2, 1, 0, 3).reshape(h, c, f * w)


def from_rows(x):
    h, c, lanes = x.shape
    return x.reshape(h, c, lanes // 128, 128).transpose(2, 1, 0, 3)


def core_swap(x):
    return lax.ppermute(x, "rep", [(0, 1), (1, 0)])


def exchange(x, axis):
    return lax.all_to_all(x, axis, 0, 0, tiled=True)


def route(payload, source):
    rep = lax.axis_index("rep")
    own = exchange(payload, "dp")
    other = core_swap(own)
    wanted = lax.dynamic_slice_in_dim(source, rep * 8, 8, 0)
    row = jnp.maximum(wanted, 0) % 8
    origin = jnp.where(wanted < 0, 0, jnp.where(wanted // 8 == rep, 1, 2)).astype(jnp.int32)
    return exchange(pick(row, origin, own, other), "dp")


def summed_kernel_grad(local, scale):
    rep = lax.axis_index("rep")
    halves = local.reshape(2, 2048, 128)
    mine = lax.dynamic_index_in_dim(halves, rep, 0, False)
    theirs = lax.dynamic_index_in_dim(halves, 1 - rep, 0, False)
    pair = mine + core_swap(theirs)
    spread = exchange(pair.astype(BF16).reshape(8, 256, 128), "dp")
    share = (jnp.sum(spread.astype(F32), 0) * scale).astype(BF16)
    half = exchange(jnp.broadcast_to(share[None], (8, 256, 128)), "dp").reshape(2048, 128)
    there = core_swap(half)
    low = jnp.where(rep == 0, half, there)
    high = jnp.where(rep == 0, there, half)
    return jnp.concatenate([low, high], 0)


def per_device(frames, weight, cotangent, prev_owner, lengths):
    seg_len, width, height, columns = frames.shape
    channels = weight.shape[4]
    rep, me = lax.axis_index("rep"), lax.axis_index("dp")
    member = rep * 8 + me
    tensor = Group("tensor", tensor_index, lambda i: (i // 2, i % 2))
    place = jnp.stack(tensor.absolute()).astype(jnp.int32)
    segments = jnp.arange(prev_owner.shape[0], dtype=jnp.int32)
    follows = prev_owner[None, :] == segments[:, None]
    follower = jnp.max(jnp.where(follows, segments[None, :], -1), 1)

    keep = jnp.arange(seg_len) < lengths[member]
    x = to_rows(frames)
    m = to_rows(jnp.where(keep[:, None, None, None], cotangent, jnp.zeros_like(cotangent)))
    rows = weight.transpose(1, 2, 3, 0, 4)[:, ::-1].reshape(9, 3 * width, channels)

    head = route(m[:, :, :256], follower)
    blocks = tensor.gather(x)
    partials = exchange(input_partials(m, head, rows), "tensor")
    input_grad = from_rows(jnp.sum(partials.astype(F32), 0))

    local = kernel_grad(place, blocks, m, head)
    cells = prev_owner.shape[0] * seg_len * height * columns
    total = summed_kernel_grad(local, 1.0 / math.sqrt(cells))
    total = total[: 81 * width].reshape(3, 3, 3, 3, width, 128)
    weight_grad = total[:, :, ::-1].transpose(4, 0, 2, 3, 1, 5).reshape(weight.shape).astype(F32)

    conv, carry = forward(place, blocks, rows)
    received = route(carry, prev_owner)
    conv = conv + jnp.pad(received.astype(F32), ((0, 0), (0, 0), (0, 256)))
    live = jnp.repeat(keep, columns)[None, None, :]
    output = from_rows(jnp.where(live, conv, 0.0).astype(BF16))
    return (output, input_grad, weight_grad)


def solution(mesh):
    split = P(("rep", "dp"), "tensor", None, None)
    kernel = P("tensor", None, None, None, None)
    return jax.shard_map(
        per_device,
        mesh=mesh,
        in_specs=(split, kernel, split, P(), P()),
        out_specs=(split, split, kernel),
        check_vma=False,
    )
```

```python
import math

import jax
import jax.numpy as jnp
from jax import lax
from jax.experimental import pallas as pl
from jax.experimental.pallas import tpu as pltpu
from jax.sharding import PartitionSpec as P

BF16 = jnp.bfloat16
F32 = jnp.float32
VMEM_LIMIT = 56 * 1024 * 1024
ANY = pl.BlockSpec(memory_space=pl.ANY)
VMEM = pl.BlockSpec(memory_space=pltpu.VMEM)
SMEM = pl.BlockSpec(memory_space=pltpu.SMEM)

PLACES = ((0, 0), (0, 1), (1, 0), (3, 0), (1, 1), (3, 1), (2, 0), (2, 1))


def tensor_index(ring, pair):
    return ring * 2 + pair


class Group:
    def __init__(self, name, index_of, coords):
        self.name = name
        self.index_of = index_of
        me = lax.axis_index(name)
        self.ring, self.pair = coords(me)
        cells = [(r, p) for r in range(4) for p in range(2)]
        self.perm_up = [(index_of(r, p), index_of((r + 1) % 4, p)) for r, p in cells]
        self.perm_down = [(index_of(r, p), index_of((r + 3) % 4, p)) for r, p in cells]
        self.perm_swap = [(index_of(r, p), index_of(r, 1 - p)) for r, p in cells]

    def up(self, x):
        return lax.ppermute(x, self.name, self.perm_up)

    def down(self, x):
        return lax.ppermute(x, self.name, self.perm_down)

    def swap(self, x):
        return lax.ppermute(x, self.name, self.perm_swap)

    def absolute(self):
        return [self.index_of((self.ring + dr) % 4, self.pair ^ dp) for dr, dp in PLACES]

    def gather(self, x):
        half = x.shape[0] // 2
        pair, prev, following = self.swap(x), self.up(x), self.down(x)
        pair_next = self.swap(following)
        pair_prev = self.up(pair)
        second = self.down(following)
        far_a = self.down(pair_next[:half])
        far_b = self.up(pair_prev[half:])
        return [x, pair, following, prev, pair_next, pair_prev, second, far_a, far_b]

    def scatter_sum(self, parts):
        own, pair, following, prev, pair_next, pair_prev, second, far_a, far_b = parts
        from_prev = self.down(prev)
        in_a = self.up(far_a)
        in_b = self.down(far_b)
        pair_next = added(pair_next, jnp.concatenate([in_a, jnp.zeros_like(in_a)], 0))
        pair_prev = added(pair_prev, jnp.concatenate([jnp.zeros_like(in_b), in_b], 0))
        got_up = self.up(second)
        got_swap = self.swap(pair_next)
        got_down = self.down(pair_prev)
        last_up = self.up(added(following, got_swap, got_up))
        last_swap = self.swap(added(pair, got_down))
        return sum(x.astype(F32) for x in (own, from_prev, last_up, last_swap))


def added(*terms):
    return sum(x.astype(F32) for x in terms).astype(BF16)


def shifted(x, by):
    lanes = x.shape[-1]
    column = lax.broadcasted_iota(jnp.int32, x.shape, x.ndim - 1) % 128
    rolled = pltpu.roll(x, by % lanes, x.ndim - 1)
    edge = 0 if by == 1 else 127
    return jnp.where(column == edge, 0.0, rolled)


def fill_taps(m_ref, head_ref, taps):
    rows, width = m_ref.shape[0], m_ref.shape[1]
    taps[0] = jnp.zeros(taps.shape[1:], BF16)
    taps[rows + 1] = jnp.zeros(taps.shape[1:], BF16)
    for h in range(rows):
        plain = jnp.concatenate([m_ref[h], head_ref[h]], 1)
        wide = plain.astype(F32)
        taps[h + 1, 0:width] = shifted(wide, -1).astype(BF16)
        taps[h + 1, width : 2 * width] = plain
        taps[h + 1, 2 * width : 3 * width] = shifted(wide, 1).astype(BF16)


def input_grad_kernel(place_ref, after_ref, m_ref, head_ref, w_ref, *rest):
    del after_ref
    outs, (taps, wt, parts, sems) = rest[:9], rest[9:]
    rows, width, lanes = m_ref.shape
    half = rows // 2
    fill_taps(m_ref, head_ref, taps)
    depth = 3 * 3 * width
    for a in range(3):
        block = jnp.concatenate([w_ref[a * 3 + b] for b in range(3)], 0)
        wt[:, a * depth : (a + 1) * depth] = block.T

    copies = []
    for h in range(rows):
        stack = jnp.reshape(taps[h : h + 3], (depth, taps.shape[2]))
        for start in range(0, lanes, 256):
            rhs = jnp.concatenate(
                [stack[:, (2 - a) * 128 + start : (2 - a) * 128 + start + 256] for a in range(3)], 0
            )
            total = jnp.dot(wt[...], rhs, preferred_element_type=F32).astype(BF16)
            for t in range(8):
                parts[t, h, :, start : start + 256] = total[t * width : (t + 1) * width]
        if h % half == half - 1:
            part, first = h // half, h + 1 - half
            for r in range(8):
                source = parts.at[place_ref[r], first : first + half]
                target = outs[r].at[first : first + half] if r < 7 else outs[7 + part]
                copies.append(pltpu.make_async_copy(source, target, sems.at[part, r]))
                copies[-1].start()
    for copy in copies:
        copy.wait()


def pick_kernel(row_ref, from_ref, own_ref, other_ref, out_ref):
    for d in range(out_ref.shape[0]):
        own, other = own_ref[row_ref[d]], other_ref[row_ref[d]]
        chosen = jnp.where(from_ref[d] == 1, own, other)
        out_ref[d] = jnp.where(from_ref[d] == 0, jnp.zeros_like(chosen), chosen)


def load_channels(place_ref, blocks, x, sems):
    rows, width = blocks[0].shape[0], blocks[0].shape[1]
    half = rows // 2
    x[0] = jnp.zeros(x.shape[1:], BF16)
    x[rows + 1] = jnp.zeros(x.shape[1:], BF16)
    copies = []
    for r, block in enumerate(blocks):
        place = place_ref[min(r, 7)]
        channel = pl.ds(pl.multiple_of(place * width, 16), width)
        if r < 7:
            target = x.at[pl.ds(1, rows), channel]
        else:
            target = x.at[pl.ds(1 + (r - 7) * half, half), channel]
        copies.append(pltpu.make_async_copy(block, target, sems.at[r]))
    for copy in copies:
        copy.start()
    for copy in copies:
        copy.wait()


def forward_kernel(place_ref, *rest):
    blocks, (w_ref, out_ref, carry_ref, x, sems) = rest[:9], rest[9:]
    rows, width, lanes = out_ref.shape
    load_channels(place_ref, blocks, x, sems)
    lhs = jnp.concatenate(
        [jnp.concatenate([w_ref[a * 3 + 2 - b] for a in range(3)], 0) for b in range(3)], 1
    )
    for h in range(rows):
        stack = jnp.reshape(x[h : h + 3], (3 * x.shape[1], lanes))
        y = jnp.dot(lhs, stack, preferred_element_type=F32)
        sums = []
        for e in range(3):
            frames = []
            for g in range(lanes // 128 + 2):
                terms = []
                for a in range(3):
                    f = g + a - 2
                    if 0 <= f < lanes // 128:
                        row = (a * 3 + e) * width
                        terms.append(y[row : row + width, f * 128 : f * 128 + 128])
                total = terms[0]
                for term in terms[1:]:
                    total = total + term
                frames.append(total)
            sums.append(jnp.concatenate(frames, 1))
        result = sums[1] + shifted(sums[0], 1) + shifted(sums[2], -1)
        out_ref[h] = result[:, :lanes]
        carry_ref[h, :width] = result[:, lanes : lanes + 128].astype(BF16)
        carry_ref[h, width:] = result[:, lanes + 128 :].astype(BF16)


def kernel_grad_kernel(place_ref, *rest):
    blocks, (after_ref, m_ref, head_ref, out_ref, x, taps, total, sems) = rest[:9], rest[9:]
    rows, width, lanes = m_ref.shape
    del after_ref
    load_channels(place_ref, blocks, x, sems)
    fill_taps(m_ref, head_ref, taps)
    depth = 9 * width
    total[...] = jnp.zeros(total.shape, F32)

    @pl.loop(0, rows)
    def _(h):
        stack = jnp.reshape(taps[pl.ds(h, 3)], (depth, taps.shape[2]))
        right = x[h + 1]
        for a in range(3):
            left = stack[:, (2 - a) * 128 : (2 - a) * 128 + lanes]
            total[a] += lax.dot_general(
                left, right, (((1,), (1,)), ((), ())), preferred_element_type=F32
            )

    out_ref[9 * depth :, :] = jnp.zeros((out_ref.shape[0] - 9 * depth, 128), F32)
    for a in range(3):
        for block in range(3):
            row = (a * 3 + block) * depth
            out_ref[row : row + depth, :] = total[a, :, block * 128 : block * 128 + 128]


def params():
    return pltpu.CompilerParams(vmem_limit_bytes=VMEM_LIMIT)


def cost(flops, size):
    return pl.CostEstimate(flops=flops, bytes_accessed=size, transcendentals=0)


FLOPS = 2 * 27 * 48 * 384 * 4096


def input_partials(place, after, m, head, weight):
    rows, width, lanes = m.shape
    channels = weight.shape[2]
    whole = jax.ShapeDtypeStruct((rows, width, lanes), BF16)
    half = jax.ShapeDtypeStruct((rows // 2, width, lanes), BF16)
    return pl.pallas_call(
        input_grad_kernel,
        out_shape=[whole] * 7 + [half] * 2,
        in_specs=[SMEM, ANY, VMEM, VMEM, VMEM],
        out_specs=[ANY] * 9,
        scratch_shapes=[
            pltpu.VMEM((rows + 2, 3 * width, lanes + 256), BF16),
            pltpu.VMEM((channels, 27 * width), BF16),
            pltpu.VMEM((8, rows, width, lanes), BF16),
            pltpu.SemaphoreType.DMA((2, 8)),
        ],
        compiler_params=params(),
        cost_estimate=cost(FLOPS, 5_000_000),
        name="input_partials",
    )(place, after, m, head, weight)


def pick(row, origin, own, other):
    return pl.pallas_call(
        pick_kernel,
        out_shape=jax.ShapeDtypeStruct(own.shape, own.dtype),
        in_specs=[SMEM, SMEM, VMEM, VMEM],
        out_specs=VMEM,
        compiler_params=params(),
        name="pick",
    )(row, origin, own, other)


def forward(place, blocks, weight):
    rows, width, lanes = blocks[0].shape
    channels = weight.shape[2]
    return pl.pallas_call(
        forward_kernel,
        out_shape=[
            jax.ShapeDtypeStruct((rows, width, lanes), F32),
            jax.ShapeDtypeStruct((rows, 2 * width, 128), BF16),
        ],
        in_specs=[SMEM] + [ANY] * 9 + [VMEM],
        out_specs=[VMEM, VMEM],
        scratch_shapes=[
            pltpu.VMEM((rows + 2, channels, lanes), BF16),
            pltpu.SemaphoreType.DMA((9,)),
        ],
        compiler_params=params(),
        cost_estimate=cost(FLOPS, 5_000_000),
        name="forward",
    )(place, *blocks, weight)


def kernel_grad(place, blocks, after, m, head):
    rows, width, lanes = m.shape
    channels = 8 * width
    return pl.pallas_call(
        kernel_grad_kernel,
        out_shape=jax.ShapeDtypeStruct((4096, 128), F32),
        in_specs=[SMEM] + [ANY] * 10 + [VMEM, VMEM],
        out_specs=VMEM,
        scratch_shapes=[
            pltpu.VMEM((rows + 2, channels, lanes), BF16),
            pltpu.VMEM((rows + 2, 3 * width, lanes + 256), BF16),
            pltpu.VMEM((3, 9 * width, channels), F32),
            pltpu.SemaphoreType.DMA((9,)),
        ],
        compiler_params=params(),
        cost_estimate=cost(FLOPS, 6_000_000),
        name="kernel_grad",
    )(place, *blocks, after, m, head)


def to_rows(x):
    f, c, h, w = x.shape
    return x.transpose(2, 1, 0, 3).reshape(h, c, f * w)


def from_rows(x):
    h, c, lanes = x.shape
    return x.reshape(h, c, lanes // 128, 128).transpose(2, 1, 0, 3)


def core_swap(x):
    return lax.ppermute(x, "rep", [(0, 1), (1, 0)])


def exchange(x):
    return lax.all_to_all(x, "dp", 0, 0, tiled=True)


def handed_on(own, source):
    rep = lax.axis_index("rep")
    wanted = lax.dynamic_slice_in_dim(source, rep * 8, 8, 0)
    row = jnp.maximum(wanted, 0) % 8
    origin = jnp.where(wanted < 0, 0, jnp.where(wanted // 8 == rep, 1, 2)).astype(jnp.int32)
    return pick(row, origin, own, core_swap(own))


def route(payload, source):
    return exchange(handed_on(exchange(payload), source))


def sum_and_route(local, scale, payload, source):
    rep = lax.axis_index("rep")
    halves = local.reshape(2, 2048, 128)
    mine = lax.dynamic_index_in_dim(halves, rep, 0, False)
    theirs = lax.dynamic_index_in_dim(halves, 1 - rep, 0, False)
    pair = (mine + core_swap(theirs)).astype(BF16).reshape(8, 256, 128)
    spread = exchange(jnp.concatenate([pair, payload], 1))
    handed = handed_on(spread[:, 256:], source)
    share = (jnp.sum(spread[:, :256].astype(F32), 0) * scale).astype(BF16)
    share = jnp.broadcast_to(share[None], (8, 256, 128))
    spread = exchange(jnp.concatenate([share, handed], 1))
    half = spread[:, :256].reshape(2048, 128)
    there = core_swap(half)
    low = jnp.where(rep == 0, half, there)
    high = jnp.where(rep == 0, there, half)
    return jnp.concatenate([low, high], 0), spread[:, 256:]


def per_device(frames, weight, cotangent, prev_owner, lengths):
    seg_len, width, height, columns = frames.shape
    channels = weight.shape[4]
    rep, me = lax.axis_index("rep"), lax.axis_index("dp")
    member = rep * 8 + me
    tensor = Group("tensor", tensor_index, lambda i: (i // 2, i % 2))
    place = jnp.stack(tensor.absolute()).astype(jnp.int32)
    segments = jnp.arange(prev_owner.shape[0], dtype=jnp.int32)
    follows = prev_owner[None, :] == segments[:, None]
    follower = jnp.max(jnp.where(follows, segments[None, :], -1), 1)

    keep = jnp.arange(seg_len) < lengths[member]
    x = to_rows(frames)
    m = to_rows(jnp.where(keep[:, None, None, None], cotangent, jnp.zeros_like(cotangent)))
    rows = weight.transpose(1, 2, 3, 0, 4)[:, ::-1].reshape(9, 3 * width, channels)

    payload, x = lax.optimization_barrier((m[:, :, :256], x))
    head = route(payload, follower)
    blocks = tensor.gather(x)

    conv, carry = forward(place, blocks, rows)
    local = kernel_grad(place, blocks, carry, m, head)
    partials = input_partials(place, local, m, head, rows)
    input_grad = from_rows(tensor.scatter_sum(partials))

    cells = prev_owner.shape[0] * seg_len * height * columns
    total, received = sum_and_route(local, 1.0 / math.sqrt(cells), carry, prev_owner)
    total = total[: 81 * width].reshape(3, 3, 3, 3, width, 128)
    weight_grad = total[:, :, ::-1].transpose(4, 0, 2, 3, 1, 5).reshape(weight.shape).astype(F32)

    conv = conv.reshape(height, width, seg_len, columns).transpose(2, 1, 0, 3)
    received = received.reshape(height, 2, width, columns).transpose(1, 2, 0, 3).astype(F32)
    conv = conv + jnp.concatenate([received, jnp.zeros_like(received)], 0)
    output = jnp.where(keep[:, None, None, None], conv, 0.0).astype(BF16)
    return (output, input_grad, weight_grad)


def solution(mesh):
    split = P(("rep", "dp"), "tensor", None, None)
    kernel = P("tensor", None, None, None, None)
    return jax.shard_map(
        per_device,
        mesh=mesh,
        in_specs=(split, kernel, split, P(), P()),
        out_specs=(split, split, kernel),
        check_vma=False,
    )
```

```python
import math

import jax
import jax.numpy as jnp
from jax import lax
from jax.experimental import pallas as pl
from jax.experimental.pallas import tpu as pltpu
from jax.sharding import PartitionSpec as P

BF16 = jnp.bfloat16
F32 = jnp.float32
VMEM_LIMIT = 56 * 1024 * 1024
ANY = pl.BlockSpec(memory_space=pl.ANY)
VMEM = pl.BlockSpec(memory_space=pltpu.VMEM)
SMEM = pl.BlockSpec(memory_space=pltpu.SMEM)

PLACES = ((0, 0), (0, 1), (1, 0), (3, 0), (1, 1), (3, 1), (2, 0), (2, 1))


def tensor_index(ring, pair):
    return ring * 2 + pair


class Group:
    def __init__(self, name, index_of, coords):
        self.name = name
        self.index_of = index_of
        me = lax.axis_index(name)
        self.ring, self.pair = coords(me)
        cells = [(r, p) for r in range(4) for p in range(2)]
        self.perm_up = [(index_of(r, p), index_of((r + 1) % 4, p)) for r, p in cells]
        self.perm_down = [(index_of(r, p), index_of((r + 3) % 4, p)) for r, p in cells]
        self.perm_swap = [(index_of(r, p), index_of(r, 1 - p)) for r, p in cells]

    def up(self, x):
        return lax.ppermute(x, self.name, self.perm_up)

    def down(self, x):
        return lax.ppermute(x, self.name, self.perm_down)

    def swap(self, x):
        return lax.ppermute(x, self.name, self.perm_swap)

    def absolute(self):
        return [self.index_of((self.ring + dr) % 4, self.pair ^ dp) for dr, dp in PLACES]

    def gather(self, x, tie):
        half = x.shape[0] // 2
        following, prev, pair = self.down(x), self.up(x), self.swap(x)
        tie, following, prev, pair = lax.optimization_barrier((tie, following, prev, pair))
        pair_next = self.swap(following)
        pair_prev = self.up(pair)
        second = self.down(following)
        far_a = self.down(pair_next[:half])
        far_b = self.up(pair_prev[half:])
        return [x, pair, following, prev, pair_next, pair_prev, second, far_a, far_b], tie

    def scatter_sum(self, parts):
        own, pair, following, prev, pair_next, pair_prev, second, far_a, far_b = parts
        from_prev = self.down(prev)
        in_a = self.up(far_a)
        in_b = self.down(far_b)
        pair_next = added(pair_next, jnp.concatenate([in_a, jnp.zeros_like(in_a)], 0))
        pair_prev = added(pair_prev, jnp.concatenate([jnp.zeros_like(in_b), in_b], 0))
        got_up = self.up(second)
        got_swap = self.swap(pair_next)
        got_down = self.down(pair_prev)
        last_up = self.up(added(following, got_swap, got_up))
        last_swap = self.swap(added(pair, got_down))
        return sum(x.astype(F32) for x in (own, from_prev, last_up, last_swap))


def added(*terms):
    return sum(x.astype(F32) for x in terms).astype(BF16)


def shifted(x, by):
    lanes = x.shape[-1]
    column = lax.broadcasted_iota(jnp.int32, x.shape, x.ndim - 1) % 128
    rolled = pltpu.roll(x, by % lanes, x.ndim - 1)
    edge = 0 if by == 1 else 127
    return jnp.where(column == edge, 0.0, rolled)


def fill_taps(live_ref, m_ref, head_ref, taps):
    rows, width, lanes = m_ref.shape
    frames = taps.shape[2] // 128
    taps[0] = jnp.zeros(taps.shape[1:], BF16)
    taps[rows + 1] = jnp.zeros(taps.shape[1:], BF16)
    for h in range(rows):
        whole = jnp.concatenate([m_ref[h], head_ref[h]], 1).astype(F32)
        wide = jnp.concatenate(
            [
                jnp.where(live_ref[f] > 0, whole[:, f * 128 : f * 128 + 128], 0.0)
                for f in range(frames)
            ],
            1,
        )
        taps[h + 1, 0:width] = shifted(wide, -1).astype(BF16)
        taps[h + 1, width : 2 * width] = wide.astype(BF16)
        taps[h + 1, 2 * width : 3 * width] = shifted(wide, 1).astype(BF16)


def input_grad_kernel(place_ref, live_ref, after_ref, m_ref, head_ref, w_ref, *rest):
    del after_ref
    outs, (taps, wt, parts, sems) = rest[:9], rest[9:]
    rows, width, lanes = m_ref.shape
    half = rows // 2
    fill_taps(live_ref, m_ref, head_ref, taps)
    depth = 3 * 3 * width
    for a in range(3):
        block = jnp.concatenate([w_ref[a * 3 + b] for b in range(3)], 0)
        wt[:, a * depth : (a + 1) * depth] = block.T

    copies = []
    for h in range(rows):
        stack = jnp.reshape(taps[h : h + 3], (depth, taps.shape[2]))
        for start in range(0, lanes, 256):
            rhs = jnp.concatenate(
                [stack[:, (2 - a) * 128 + start : (2 - a) * 128 + start + 256] for a in range(3)], 0
            )
            total = jnp.dot(wt[...], rhs, preferred_element_type=F32).astype(BF16)
            for t in range(8):
                parts[t, h, :, start : start + 256] = total[t * width : (t + 1) * width]
        if h % half == half - 1:
            part, first = h // half, h + 1 - half
            for r in range(8):
                source = parts.at[place_ref[r], first : first + half]
                target = outs[r].at[first : first + half] if r < 7 else outs[7 + part]
                copies.append(pltpu.make_async_copy(source, target, sems.at[part, r]))
                copies[-1].start()
    for copy in copies:
        copy.wait()


def pick_kernel(row_ref, from_ref, own_ref, other_ref, out_ref):
    for d in range(out_ref.shape[0]):
        own, other = own_ref[row_ref[d]], other_ref[row_ref[d]]
        chosen = jnp.where(from_ref[d] == 1, own, other)
        out_ref[d] = jnp.where(from_ref[d] == 0, jnp.zeros_like(chosen), chosen)


CHUNK = 2


def start_loads(place_ref, blocks, x, sems):
    rows, width = blocks[0].shape[0], blocks[0].shape[1]
    half = rows // 2
    x[0] = jnp.zeros(x.shape[1:], BF16)
    x[rows + 1] = jnp.zeros(x.shape[1:], BF16)
    lists = []
    for part in range(rows // CHUNK):
        first = part * CHUNK
        copies = []
        for r in range(8):
            channel = pl.ds(pl.multiple_of(place_ref[r] * width, 16), width)
            block, skip = (blocks[r], 0) if r < 7 else (blocks[7 + first // half], first // half * half)
            copies.append(
                pltpu.make_async_copy(
                    block.at[first - skip : first - skip + CHUNK],
                    x.at[first + 1 : first + 1 + CHUNK, channel],
                    sems.at[part, r],
                )
            )
            copies[-1].start()
        lists.append(copies)
    return lists


def wait_for(copies):
    for copy in copies:
        copy.wait()


def forward_kernel(place_ref, after_ref, *rest):
    del after_ref
    blocks, (w_ref, out_ref, carry_ref, x, sems) = rest[:9], rest[9:]
    rows, width, lanes = out_ref.shape
    loads = start_loads(place_ref, blocks, x, sems)
    lhs = jnp.concatenate(
        [jnp.concatenate([w_ref[a * 3 + 2 - b] for a in range(3)], 0) for b in range(3)], 1
    )
    wait_for(loads[0])
    for h in range(rows):
        if (h + 1) % CHUNK == 0 and h + 1 < rows:
            wait_for(loads[(h + 1) // CHUNK])
        stack = jnp.reshape(x[h : h + 3], (3 * x.shape[1], lanes))
        y = jnp.dot(lhs, stack, preferred_element_type=F32)
        sums = []
        for e in range(3):
            frames = []
            for g in range(lanes // 128 + 2):
                terms = []
                for a in range(3):
                    f = g + a - 2
                    if 0 <= f < lanes // 128:
                        row = (a * 3 + e) * width
                        terms.append(y[row : row + width, f * 128 : f * 128 + 128])
                total = terms[0]
                for term in terms[1:]:
                    total = total + term
                frames.append(total)
            sums.append(jnp.concatenate(frames, 1))
        result = sums[1] + shifted(sums[0], 1) + shifted(sums[2], -1)
        out_ref[h] = result[:, :lanes]
        carry_ref[h, :width] = result[:, lanes : lanes + 128].astype(BF16)
        carry_ref[h, width:] = result[:, lanes + 128 :].astype(BF16)


def kernel_grad_kernel(place_ref, live_ref, rep_ref, *rest):
    blocks, (m_ref, head_ref, mine_ref, theirs_ref, x, taps, total, result, sems, out_sems) = rest[:9], rest[9:]
    rows, width, lanes = m_ref.shape
    loads = start_loads(place_ref, blocks, x, sems)
    fill_taps(live_ref, m_ref, head_ref, taps)
    depth = 9 * width
    result[9 * depth :, :] = jnp.zeros((result.shape[0] - 9 * depth, 128), F32)
    for h in range(rows):
        if h % CHUNK == 0:
            wait_for(loads[h // CHUNK])
        stack = jnp.reshape(taps[h : h + 3], (depth, taps.shape[2]))
        right = x[h + 1]
        for a in range(3):
            left = stack[:, (2 - a) * 128 : (2 - a) * 128 + lanes]
            product = lax.dot_general(
                left, right, (((1,), (1,)), ((), ())), preferred_element_type=F32
            )
            if h == 0:
                total[a] = product
            elif h < rows - 1:
                total[a] += product
            else:
                product = total[a] + product
                for block in range(3):
                    row = (a * 3 + block) * depth
                    result[row : row + depth, :] = product[:, block * 128 : block * 128 + 128]
    half = result.shape[0] // 2
    copies = []
    for slot, (target, rep) in enumerate(((theirs_ref, 1 - rep_ref[0]), (mine_ref, rep_ref[0]))):
        source = result.at[pl.ds(pl.multiple_of(rep * half, 16), half)]
        copies.append(pltpu.make_async_copy(source, target, out_sems.at[slot]))
        copies[-1].start()
    wait_for(copies)


def params():
    return pltpu.CompilerParams(vmem_limit_bytes=VMEM_LIMIT)


def cost(flops, size):
    return pl.CostEstimate(flops=flops, bytes_accessed=size, transcendentals=0)


FLOPS = 2 * 27 * 48 * 384 * 4096


def input_partials(place, live, after, m, head, weight):
    rows, width, lanes = m.shape
    channels = weight.shape[2]
    whole = jax.ShapeDtypeStruct((rows, width, lanes), BF16)
    half = jax.ShapeDtypeStruct((rows // 2, width, lanes), BF16)
    return pl.pallas_call(
        input_grad_kernel,
        out_shape=[whole] * 7 + [half] * 2,
        in_specs=[SMEM, SMEM, ANY, VMEM, VMEM, VMEM],
        out_specs=[ANY] * 9,
        scratch_shapes=[
            pltpu.VMEM((rows + 2, 3 * width, lanes + 256), BF16),
            pltpu.VMEM((channels, 27 * width), BF16),
            pltpu.VMEM((8, rows, width, lanes), BF16),
            pltpu.SemaphoreType.DMA((2, 8)),
        ],
        compiler_params=params(),
        cost_estimate=cost(FLOPS, 5_000_000),
        name="input_partials",
    )(place, live, after, m, head, weight)


def pick(row, origin, own, other):
    return pl.pallas_call(
        pick_kernel,
        out_shape=jax.ShapeDtypeStruct(own.shape, own.dtype),
        in_specs=[SMEM, SMEM, VMEM, VMEM],
        out_specs=VMEM,
        compiler_params=params(),
        name="pick",
    )(row, origin, own, other)


def forward(place, after, blocks, weight):
    rows, width, lanes = blocks[0].shape
    channels = weight.shape[2]
    return pl.pallas_call(
        forward_kernel,
        out_shape=[
            jax.ShapeDtypeStruct((rows, width, lanes), F32),
            jax.ShapeDtypeStruct((rows, 2 * width, 128), BF16),
        ],
        in_specs=[SMEM] + [ANY] * 10 + [VMEM],
        out_specs=[VMEM, VMEM],
        scratch_shapes=[
            pltpu.VMEM((rows + 2, channels, lanes), BF16),
            pltpu.SemaphoreType.DMA((rows // CHUNK, 8)),
        ],
        compiler_params=params(),
        cost_estimate=cost(FLOPS, 5_000_000),
        name="forward",
    )(place, after, *blocks, weight)


def kernel_grad(place, live, rep, blocks, m, head):
    rows, width, lanes = m.shape
    channels = 8 * width
    return pl.pallas_call(
        kernel_grad_kernel,
        out_shape=[jax.ShapeDtypeStruct((2048, 128), F32)] * 2,
        in_specs=[SMEM] * 3 + [ANY] * 9 + [VMEM, VMEM],
        out_specs=[ANY, ANY],
        scratch_shapes=[
            pltpu.VMEM((rows + 2, channels, lanes), BF16),
            pltpu.VMEM((rows + 2, 3 * width, lanes + 256), BF16),
            pltpu.VMEM((3, 9 * width, channels), F32),
            pltpu.VMEM((4096, 128), F32),
            pltpu.SemaphoreType.DMA((rows // CHUNK, 8)),
            pltpu.SemaphoreType.DMA((2,)),
        ],
        compiler_params=params(),
        cost_estimate=cost(FLOPS, 6_000_000),
        name="kernel_grad",
    )(place, live, rep, *blocks, m, head)


def to_rows(x):
    f, c, h, w = x.shape
    return x.transpose(2, 1, 0, 3).reshape(h, c, f * w)


def from_rows(x):
    h, c, lanes = x.shape
    return x.reshape(h, c, lanes // 128, 128).transpose(2, 1, 0, 3)


def core_swap(x):
    return lax.ppermute(x, "rep", [(0, 1), (1, 0)])


def exchange(x):
    return lax.all_to_all(x, "dp", 0, 0, tiled=True)


def handed_on(own, source):
    rep = lax.axis_index("rep")
    wanted = lax.dynamic_slice_in_dim(source, rep * 8, 8, 0)
    row = jnp.maximum(wanted, 0) % 8
    origin = jnp.where(wanted < 0, 0, jnp.where(wanted // 8 == rep, 1, 2)).astype(jnp.int32)
    return pick(row, origin, own, core_swap(own))


def first_exchange(mine, theirs, payload):
    pair = (mine + core_swap(theirs)).astype(BF16).reshape(8, 256, 128)
    return jnp.concatenate([pair, payload], 1)


def second_exchange(spread, scale, source):
    rep = lax.axis_index("rep")
    spread = exchange(spread)
    handed = handed_on(spread[:, 256:], source)
    share = (jnp.sum(spread[:, :256].astype(F32), 0) * scale).astype(BF16)
    share = jnp.broadcast_to(share[None], (8, 256, 128))
    spread = exchange(jnp.concatenate([share, handed], 1))
    half = spread[:, :256].reshape(2048, 128)
    there = core_swap(half)
    low = jnp.where(rep == 0, half, there)
    high = jnp.where(rep == 0, there, half)
    return jnp.concatenate([low, high], 0), spread[:, 256:]


def per_device(frames, weight, cotangent, prev_owner, lengths):
    seg_len, width, height, columns = frames.shape
    channels = weight.shape[4]
    rep, me = lax.axis_index("rep"), lax.axis_index("dp")
    member = rep * 8 + me
    tensor = Group("tensor", tensor_index, lambda i: (i // 2, i % 2))
    place = jnp.stack(tensor.absolute()).astype(jnp.int32)
    segments = jnp.arange(prev_owner.shape[0], dtype=jnp.int32)
    follows = prev_owner[None, :] == segments[:, None]
    follower = jnp.max(jnp.where(follows, segments[None, :], -1), 1)

    x = to_rows(frames)
    m = to_rows(cotangent)
    rows = weight.transpose(1, 2, 3, 0, 4)[:, ::-1].reshape(9, 3 * width, channels)

    payload, x = lax.optimization_barrier((m[:, :, :256], x))
    blocks, payload = tensor.gather(x, exchange(payload))
    head = exchange(handed_on(payload, follower))
    keep = jnp.arange(seg_len) < lengths[member]
    keep_head = jnp.arange(2) < lengths[jnp.maximum(follower[member], 0)]
    live = jnp.concatenate([keep, keep_head]).astype(jnp.int32)

    mine, theirs = kernel_grad(place, live, rep.astype(jnp.int32)[None], blocks, m, head)
    conv, carry = forward(place, theirs, blocks, rows)
    spread = first_exchange(mine, theirs, carry)
    partials = input_partials(place, live, spread, m, head, rows)
    input_grad = from_rows(tensor.scatter_sum(partials))

    cells = prev_owner.shape[0] * seg_len * height * columns
    total, received = second_exchange(spread, 1.0 / math.sqrt(cells), prev_owner)
    total = total[: 81 * width].reshape(3, 3, 3, 3, width, 128)
    weight_grad = total[:, :, ::-1].transpose(4, 0, 2, 3, 1, 5).reshape(weight.shape).astype(F32)

    conv = conv.reshape(height, width, seg_len, columns).transpose(2, 1, 0, 3)
    received = received.reshape(height, 2, width, columns).transpose(1, 2, 0, 3).astype(F32)
    conv = conv + jnp.concatenate([received, jnp.zeros_like(received)], 0)
    output = jnp.where(keep[:, None, None, None], conv, 0.0).astype(BF16)
    return (output, input_grad, weight_grad)


def solution(mesh):
    split = P(("rep", "dp"), "tensor", None, None)
    kernel = P("tensor", None, None, None, None)
    return jax.shard_map(
        per_device,
        mesh=mesh,
        in_specs=(split, kernel, split, P(), P()),
        out_specs=(split, split, kernel),
        check_vma=False,
    )
```

```python
import math

import jax
import jax.numpy as jnp
from jax import lax
from jax.experimental import pallas as pl
from jax.experimental.pallas import tpu as pltpu
from jax.sharding import PartitionSpec as P

BF16 = jnp.bfloat16
F32 = jnp.float32
VMEM_LIMIT = 56 * 1024 * 1024
ANY = pl.BlockSpec(memory_space=pl.ANY)
VMEM = pl.BlockSpec(memory_space=pltpu.VMEM)
SMEM = pl.BlockSpec(memory_space=pltpu.SMEM)

PLACES = ((0, 0), (0, 1), (1, 0), (3, 0), (1, 1), (3, 1), (2, 0), (2, 1))


def tensor_index(ring, pair):
    return ring * 2 + pair


class Group:
    def __init__(self, name, index_of, coords):
        self.name = name
        self.index_of = index_of
        me = lax.axis_index(name)
        self.ring, self.pair = coords(me)
        cells = [(r, p) for r in range(4) for p in range(2)]
        self.perm_up = [(index_of(r, p), index_of((r + 1) % 4, p)) for r, p in cells]
        self.perm_down = [(index_of(r, p), index_of((r + 3) % 4, p)) for r, p in cells]
        self.perm_swap = [(index_of(r, p), index_of(r, 1 - p)) for r, p in cells]

    def up(self, x):
        return lax.ppermute(x, self.name, self.perm_up)

    def down(self, x):
        return lax.ppermute(x, self.name, self.perm_down)

    def swap(self, x):
        return lax.ppermute(x, self.name, self.perm_swap)

    def absolute(self):
        return [self.index_of((self.ring + dr) % 4, self.pair ^ dp) for dr, dp in PLACES]

    def gather(self, x):
        half = x.shape[0] // 2
        following, prev, pair = lax.optimization_barrier((self.down(x), self.up(x), self.swap(x)))
        pair_next = self.swap(following)
        pair_prev = self.up(pair)
        second = self.down(following)
        far_a = self.down(pair_next[:half])
        far_b = self.up(pair_prev[half:])
        return [x, pair, following, prev, pair_next, pair_prev, second, far_a, far_b]

    def scatter_sum(self, parts):
        own, pair, following, prev, pair_next, pair_prev, second, far_a, far_b = parts
        from_prev = self.down(prev)
        in_a = self.up(far_a)
        in_b = self.down(far_b)
        pair_next = added(pair_next, jnp.concatenate([in_a, jnp.zeros_like(in_a)], 0))
        pair_prev = added(pair_prev, jnp.concatenate([jnp.zeros_like(in_b), in_b], 0))
        got_up = self.up(second)
        got_swap = self.swap(pair_next)
        got_down = self.down(pair_prev)
        last_up = self.up(added(following, got_swap, got_up))
        last_swap = self.swap(added(pair, got_down))
        return sum(x.astype(F32) for x in (own, from_prev, last_up, last_swap))


def added(*terms):
    return sum(x.astype(F32) for x in terms).astype(BF16)


def shifted(x, by):
    lanes = x.shape[-1]
    column = lax.broadcasted_iota(jnp.int32, x.shape, x.ndim - 1) % 128
    rolled = pltpu.roll(x, by % lanes, x.ndim - 1)
    edge = 0 if by == 1 else 127
    return jnp.where(column == edge, 0.0, rolled)


def fill_taps(live_ref, m_ref, head_ref, taps):
    rows, width, lanes = m_ref.shape
    frames = taps.shape[2] // 128
    taps[0] = jnp.zeros(taps.shape[1:], BF16)
    taps[rows + 1] = jnp.zeros(taps.shape[1:], BF16)
    for h in range(rows):
        whole = jnp.concatenate([m_ref[h], head_ref[h]], 1).astype(F32)
        wide = jnp.concatenate(
            [
                jnp.where(live_ref[f] > 0, whole[:, f * 128 : f * 128 + 128], 0.0)
                for f in range(frames)
            ],
            1,
        )
        taps[h + 1, 0:width] = shifted(wide, -1).astype(BF16)
        taps[h + 1, width : 2 * width] = wide.astype(BF16)
        taps[h + 1, 2 * width : 3 * width] = shifted(wide, 1).astype(BF16)


def input_grad_kernel(place_ref, live_ref, m_ref, head_ref, w_ref, *rest):
    outs, (taps, wt, parts, sems) = rest[:9], rest[9:]
    rows, width, lanes = m_ref.shape
    half = rows // 2
    fill_taps(live_ref, m_ref, head_ref, taps)
    depth = 3 * 3 * width
    for a in range(3):
        block = jnp.concatenate([w_ref[a * 3 + b] for b in range(3)], 0)
        wt[:, a * depth : (a + 1) * depth] = block.T

    copies = []
    for h in range(rows):
        stack = jnp.reshape(taps[h : h + 3], (depth, taps.shape[2]))
        for start in range(0, lanes, 256):
            rhs = jnp.concatenate(
                [stack[:, (2 - a) * 128 + start : (2 - a) * 128 + start + 256] for a in range(3)], 0
            )
            total = jnp.dot(wt[...], rhs, preferred_element_type=F32).astype(BF16)
            for t in range(8):
                parts[t, h, :, start : start + 256] = total[t * width : (t + 1) * width]
        if h % half == half - 1:
            part, first = h // half, h + 1 - half
            for r in range(8):
                source = parts.at[place_ref[r], first : first + half]
                target = outs[r].at[first : first + half] if r < 7 else outs[7 + part]
                copies.append(pltpu.make_async_copy(source, target, sems.at[part, r]))
                copies[-1].start()
    for copy in copies:
        copy.wait()


def pick_kernel(row_ref, from_ref, own_ref, other_ref, out_ref):
    for d in range(out_ref.shape[0]):
        own, other = own_ref[row_ref[d]], other_ref[row_ref[d]]
        chosen = jnp.where(from_ref[d] == 1, own, other)
        out_ref[d] = jnp.where(from_ref[d] == 0, jnp.zeros_like(chosen), chosen)


CHUNK = 2


def start_loads(place_ref, blocks, x, sems):
    rows, width = blocks[0].shape[0], blocks[0].shape[1]
    half = rows // 2
    x[0] = jnp.zeros(x.shape[1:], BF16)
    x[rows + 1] = jnp.zeros(x.shape[1:], BF16)
    lists = []
    for part in range(rows // CHUNK):
        first = part * CHUNK
        copies = []
        for r in range(8):
            channel = pl.ds(pl.multiple_of(place_ref[r] * width, 16), width)
            block, skip = (blocks[r], 0) if r < 7 else (blocks[7 + first // half], first // half * half)
            copies.append(
                pltpu.make_async_copy(
                    block.at[first - skip : first - skip + CHUNK],
                    x.at[first + 1 : first + 1 + CHUNK, channel],
                    sems.at[part, r],
                )
            )
            copies[-1].start()
        lists.append(copies)
    return lists


def wait_for(copies):
    for copy in copies:
        copy.wait()


def forward_kernel(place_ref, after_ref, *rest):
    del after_ref
    blocks, (w_ref, out_ref, carry_ref, x, sems) = rest[:9], rest[9:]
    rows, width, lanes = out_ref.shape
    loads = start_loads(place_ref, blocks, x, sems)
    lhs = jnp.concatenate(
        [jnp.concatenate([w_ref[a * 3 + 2 - b] for a in range(3)], 0) for b in range(3)], 1
    )
    wait_for(loads[0])
    for h in range(rows):
        if (h + 1) % CHUNK == 0 and h + 1 < rows:
            wait_for(loads[(h + 1) // CHUNK])
        stack = jnp.reshape(x[h : h + 3], (3 * x.shape[1], lanes))
        y = jnp.dot(lhs, stack, preferred_element_type=F32)
        sums = []
        for e in range(3):
            frames = []
            for g in range(lanes // 128 + 2):
                terms = []
                for a in range(3):
                    f = g + a - 2
                    if 0 <= f < lanes // 128:
                        row = (a * 3 + e) * width
                        terms.append(y[row : row + width, f * 128 : f * 128 + 128])
                total = terms[0]
                for term in terms[1:]:
                    total = total + term
                frames.append(total)
            sums.append(jnp.concatenate(frames, 1))
        result = sums[1] + shifted(sums[0], 1) + shifted(sums[2], -1)
        out_ref[h] = result[:, :lanes]
        carry_ref[h, :width] = result[:, lanes : lanes + 128].astype(BF16)
        carry_ref[h, width:] = result[:, lanes + 128 :].astype(BF16)


def kernel_grad_kernel(place_ref, live_ref, rep_ref, after_ref, *rest):
    del after_ref
    blocks, (m_ref, head_ref, mine_ref, theirs_ref, x, taps, total, result, sems, out_sems) = rest[:9], rest[9:]
    rows, width, lanes = m_ref.shape
    loads = start_loads(place_ref, blocks, x, sems)
    fill_taps(live_ref, m_ref, head_ref, taps)
    depth = 9 * width
    result[9 * depth :, :] = jnp.zeros((result.shape[0] - 9 * depth, 128), F32)
    for h in range(rows):
        if h % CHUNK == 0:
            wait_for(loads[h // CHUNK])
        stack = jnp.reshape(taps[h : h + 3], (depth, taps.shape[2]))
        right = x[h + 1]
        for a in range(3):
            left = stack[:, (2 - a) * 128 : (2 - a) * 128 + lanes]
            product = lax.dot_general(
                left, right, (((1,), (1,)), ((), ())), preferred_element_type=F32
            )
            if h == 0:
                total[a] = product
            elif h < rows - 1:
                total[a] += product
            else:
                product = total[a] + product
                for block in range(3):
                    row = (a * 3 + block) * depth
                    result[row : row + depth, :] = product[:, block * 128 : block * 128 + 128]
    half = result.shape[0] // 2
    copies = []
    for slot, (target, rep) in enumerate(((theirs_ref, 1 - rep_ref[0]), (mine_ref, rep_ref[0]))):
        source = result.at[pl.ds(pl.multiple_of(rep * half, 16), half)]
        copies.append(pltpu.make_async_copy(source, target, out_sems.at[slot]))
        copies[-1].start()
    wait_for(copies)


def params():
    return pltpu.CompilerParams(vmem_limit_bytes=VMEM_LIMIT)


def cost(flops, size):
    return pl.CostEstimate(flops=flops, bytes_accessed=size, transcendentals=0)


FLOPS = 2 * 27 * 48 * 384 * 4096


def input_partials(place, live, m, head, weight):
    rows, width, lanes = m.shape
    channels = weight.shape[2]
    whole = jax.ShapeDtypeStruct((rows, width, lanes), BF16)
    half = jax.ShapeDtypeStruct((rows // 2, width, lanes), BF16)
    return pl.pallas_call(
        input_grad_kernel,
        out_shape=[whole] * 7 + [half] * 2,
        in_specs=[SMEM, SMEM, VMEM, VMEM, VMEM],
        out_specs=[ANY] * 9,
        scratch_shapes=[
            pltpu.VMEM((rows + 2, 3 * width, lanes + 256), BF16),
            pltpu.VMEM((channels, 27 * width), BF16),
            pltpu.VMEM((8, rows, width, lanes), BF16),
            pltpu.SemaphoreType.DMA((2, 8)),
        ],
        compiler_params=params(),
        cost_estimate=cost(FLOPS, 5_000_000),
        name="input_partials",
    )(place, live, m, head, weight)


def pick(row, origin, own, other):
    return pl.pallas_call(
        pick_kernel,
        out_shape=jax.ShapeDtypeStruct(own.shape, own.dtype),
        in_specs=[SMEM, SMEM, VMEM, VMEM],
        out_specs=VMEM,
        compiler_params=params(),
        name="pick",
    )(row, origin, own, other)


def forward(place, after, blocks, weight):
    rows, width, lanes = blocks[0].shape
    channels = weight.shape[2]
    return pl.pallas_call(
        forward_kernel,
        out_shape=[
            jax.ShapeDtypeStruct((rows, width, lanes), F32),
            jax.ShapeDtypeStruct((rows, 2 * width, 128), BF16),
        ],
        in_specs=[SMEM] + [ANY] * 10 + [VMEM],
        out_specs=[VMEM, VMEM],
        scratch_shapes=[
            pltpu.VMEM((rows + 2, channels, lanes), BF16),
            pltpu.SemaphoreType.DMA((rows // CHUNK, 8)),
        ],
        compiler_params=params(),
        cost_estimate=cost(FLOPS, 5_000_000),
        name="forward",
    )(place, after, *blocks, weight)


def kernel_grad(place, live, rep, after, blocks, m, head):
    rows, width, lanes = m.shape
    channels = 8 * width
    return pl.pallas_call(
        kernel_grad_kernel,
        out_shape=[jax.ShapeDtypeStruct((2048, 128), F32)] * 2,
        in_specs=[SMEM] * 3 + [ANY] * 10 + [VMEM, VMEM],
        out_specs=[ANY, ANY],
        scratch_shapes=[
            pltpu.VMEM((rows + 2, channels, lanes), BF16),
            pltpu.VMEM((rows + 2, 3 * width, lanes + 256), BF16),
            pltpu.VMEM((3, 9 * width, channels), F32),
            pltpu.VMEM((4096, 128), F32),
            pltpu.SemaphoreType.DMA((rows // CHUNK, 8)),
            pltpu.SemaphoreType.DMA((2,)),
        ],
        compiler_params=params(),
        cost_estimate=cost(FLOPS, 6_000_000),
        name="kernel_grad",
    )(place, live, rep, after, *blocks, m, head)


def to_rows(x):
    f, c, h, w = x.shape
    return x.transpose(2, 1, 0, 3).reshape(h, c, f * w)


def from_rows(x):
    h, c, lanes = x.shape
    return x.reshape(h, c, lanes // 128, 128).transpose(2, 1, 0, 3)


def core_swap(x):
    return lax.ppermute(x, "rep", [(0, 1), (1, 0)])


def exchange(x):
    return lax.all_to_all(x, "dp", 0, 0, tiled=True)


def handed_on(own, source):
    rep = lax.axis_index("rep")
    wanted = lax.dynamic_slice_in_dim(source, rep * 8, 8, 0)
    row = jnp.maximum(wanted, 0) % 8
    origin = jnp.where(wanted < 0, 0, jnp.where(wanted // 8 == rep, 1, 2)).astype(jnp.int32)
    return pick(row, origin, own, core_swap(own))


def first_exchange(mine, theirs, payload):
    pair = (mine + core_swap(theirs)).astype(BF16).reshape(8, 256, 128)
    return jnp.concatenate([pair, payload], 1)


def second_exchange(spread, scale, source):
    rep = lax.axis_index("rep")
    spread = exchange(spread)
    handed = handed_on(spread[:, 256:], source)
    share = (jnp.sum(spread[:, :256].astype(F32), 0) * scale).astype(BF16)
    share = jnp.broadcast_to(share[None], (8, 256, 128))
    spread = exchange(jnp.concatenate([share, handed], 1))
    half = spread[:, :256].reshape(2048, 128)
    there = core_swap(half)
    low = jnp.where(rep == 0, half, there)
    high = jnp.where(rep == 0, there, half)
    return jnp.concatenate([low, high], 0), spread[:, 256:]


def per_device(frames, weight, cotangent, prev_owner, lengths):
    seg_len, width, height, columns = frames.shape
    channels = weight.shape[4]
    rep, me = lax.axis_index("rep"), lax.axis_index("dp")
    member = rep * 8 + me
    tensor = Group("tensor", tensor_index, lambda i: (i // 2, i % 2))
    place = jnp.stack(tensor.absolute()).astype(jnp.int32)
    segments = jnp.arange(prev_owner.shape[0], dtype=jnp.int32)
    follows = prev_owner[None, :] == segments[:, None]
    follower = jnp.max(jnp.where(follows, segments[None, :], -1), 1)

    x = to_rows(frames)
    m = to_rows(cotangent)
    rows = weight.transpose(1, 2, 3, 0, 4)[:, ::-1].reshape(9, 3 * width, channels)

    payload, x = lax.optimization_barrier((exchange(m[:, :, :256]), x))
    blocks = tensor.gather(x)
    head = exchange(handed_on(payload, follower))
    keep = jnp.arange(seg_len) < lengths[member]
    keep_head = jnp.arange(2) < lengths[jnp.maximum(follower[member], 0)]
    live = jnp.concatenate([keep, keep_head]).astype(jnp.int32)

    partials = input_partials(place, live, m, head, rows)
    partials, blocks = lax.optimization_barrier((partials, blocks))
    mine, theirs = kernel_grad(place, live, rep.astype(jnp.int32)[None], partials[0], blocks, m, head)
    conv, carry = forward(place, theirs, blocks, rows)
    spread = first_exchange(mine, theirs, carry)
    input_grad = from_rows(tensor.scatter_sum(partials))

    cells = prev_owner.shape[0] * seg_len * height * columns
    total, received = second_exchange(spread, 1.0 / math.sqrt(cells), prev_owner)
    total = total[: 81 * width].reshape(3, 3, 3, 3, width, 128)
    weight_grad = total[:, :, ::-1].transpose(4, 0, 2, 3, 1, 5).reshape(weight.shape).astype(F32)

    conv = conv.reshape(height, width, seg_len, columns).transpose(2, 1, 0, 3)
    received = received.reshape(height, 2, width, columns).transpose(1, 2, 0, 3).astype(F32)
    conv = conv + jnp.concatenate([received, jnp.zeros_like(received)], 0)
    output = jnp.where(keep[:, None, None, None], conv, 0.0).astype(BF16)
    return (output, input_grad, weight_grad)


def solution(mesh):
    split = P(("rep", "dp"), "tensor", None, None)
    kernel = P("tensor", None, None, None, None)
    return jax.shard_map(
        per_device,
        mesh=mesh,
        in_specs=(split, kernel, split, P(), P()),
        out_specs=(split, split, kernel),
        check_vma=False,
    )
```

```python
import math

import jax
import jax.numpy as jnp
from jax import lax
from jax.experimental import pallas as pl
from jax.experimental.pallas import tpu as pltpu
from jax.sharding import PartitionSpec as P

BF16 = jnp.bfloat16
F32 = jnp.float32
VMEM_LIMIT = 56 * 1024 * 1024
ANY = pl.BlockSpec(memory_space=pl.ANY)
VMEM = pl.BlockSpec(memory_space=pltpu.VMEM)
SMEM = pl.BlockSpec(memory_space=pltpu.SMEM)

PLACES = ((0, 0), (0, 1), (1, 0), (3, 0), (1, 1), (3, 1), (2, 0), (2, 1))


def tensor_index(ring, pair):
    return ring * 2 + pair


class Group:
    def __init__(self, name, index_of, coords):
        self.name = name
        self.index_of = index_of
        me = lax.axis_index(name)
        self.ring, self.pair = coords(me)
        cells = [(r, p) for r in range(4) for p in range(2)]
        self.perm_up = [(index_of(r, p), index_of((r + 1) % 4, p)) for r, p in cells]
        self.perm_down = [(index_of(r, p), index_of((r + 3) % 4, p)) for r, p in cells]
        self.perm_swap = [(index_of(r, p), index_of(r, 1 - p)) for r, p in cells]

    def up(self, x):
        return lax.ppermute(x, self.name, self.perm_up)

    def down(self, x):
        return lax.ppermute(x, self.name, self.perm_down)

    def swap(self, x):
        return lax.ppermute(x, self.name, self.perm_swap)

    def absolute(self):
        return [self.index_of((self.ring + dr) % 4, self.pair ^ dp) for dr, dp in PLACES]

    def gather(self, x):
        half = x.shape[0] // 2
        following, prev, pair = lax.optimization_barrier((self.down(x), self.up(x), self.swap(x)))
        pair_next = self.swap(following)
        pair_prev = self.up(pair)
        second = self.down(following)
        far_a = self.down(pair_next[:half])
        far_b = self.up(pair_prev[half:])
        return [x, pair, following, prev, pair_next, pair_prev, second, far_a, far_b]

    def scatter_sum(self, parts):
        own, pair, following, prev, pair_next, pair_prev, second, far_a, far_b = parts
        from_prev = self.down(prev)
        in_a = self.up(far_a)
        in_b = self.down(far_b)
        pair_next = added(pair_next, jnp.concatenate([in_a, jnp.zeros_like(in_a)], 0))
        pair_prev = added(pair_prev, jnp.concatenate([jnp.zeros_like(in_b), in_b], 0))
        got_up = self.up(second)
        got_swap = self.swap(pair_next)
        got_down = self.down(pair_prev)
        last_up = self.up(added(following, got_swap, got_up))
        last_swap = self.swap(added(pair, got_down))
        return sum(x.astype(F32) for x in (own, from_prev, last_up, last_swap))


def added(*terms):
    return sum(x.astype(F32) for x in terms).astype(BF16)


def shifted(x, by):
    lanes = x.shape[-1]
    column = lax.broadcasted_iota(jnp.int32, x.shape, x.ndim - 1) % 128
    rolled = pltpu.roll(x, by % lanes, x.ndim - 1)
    edge = 0 if by == 1 else 127
    return jnp.where(column == edge, 0.0, rolled)


def fill_taps(live_ref, m_ref, head_ref, taps):
    rows, width, lanes = m_ref.shape
    frames = taps.shape[2] // 128
    taps[0] = jnp.zeros(taps.shape[1:], BF16)
    taps[rows + 1] = jnp.zeros(taps.shape[1:], BF16)
    for h in range(rows):
        whole = jnp.concatenate([m_ref[h], head_ref[h]], 1).astype(F32)
        wide = jnp.concatenate(
            [
                jnp.where(live_ref[f] > 0, whole[:, f * 128 : f * 128 + 128], 0.0)
                for f in range(frames)
            ],
            1,
        )
        taps[h + 1, 0:width] = shifted(wide, -1).astype(BF16)
        taps[h + 1, width : 2 * width] = wide.astype(BF16)
        taps[h + 1, 2 * width : 3 * width] = shifted(wide, 1).astype(BF16)


def input_grad_kernel(place_ref, live_ref, m_ref, head_ref, w_ref, *rest):
    outs, (taps, wt, parts, sems) = rest[:9], rest[9:]
    rows, width, lanes = m_ref.shape
    half = rows // 2
    fill_taps(live_ref, m_ref, head_ref, taps)
    depth = 3 * 3 * width
    for a in range(3):
        block = jnp.concatenate([w_ref[a * 3 + b] for b in range(3)], 0)
        wt[:, a * depth : (a + 1) * depth] = block.T

    copies = []
    for h in range(rows):
        stack = jnp.reshape(taps[h : h + 3], (depth, taps.shape[2]))
        for start in range(0, lanes, 256):
            rhs = jnp.concatenate(
                [stack[:, (2 - a) * 128 + start : (2 - a) * 128 + start + 256] for a in range(3)], 0
            )
            total = jnp.dot(wt[...], rhs, preferred_element_type=F32).astype(BF16)
            for t in range(8):
                parts[t, h, :, start : start + 256] = total[t * width : (t + 1) * width]
        if h % half == half - 1:
            part, first = h // half, h + 1 - half
            for r in range(8):
                source = parts.at[place_ref[r], first : first + half]
                target = outs[r].at[first : first + half] if r < 7 else outs[7 + part]
                copies.append(pltpu.make_async_copy(source, target, sems.at[part, r]))
                copies[-1].start()
    for copy in copies:
        copy.wait()


def pick_kernel(row_ref, from_ref, own_ref, other_ref, out_ref):
    for d in range(out_ref.shape[0]):
        own, other = own_ref[row_ref[d]], other_ref[row_ref[d]]
        chosen = jnp.where(from_ref[d] == 1, own, other)
        out_ref[d] = jnp.where(from_ref[d] == 0, jnp.zeros_like(chosen), chosen)


CHUNK = 2


def start_loads(place_ref, blocks, x, sems):
    rows, width = blocks[0].shape[0], blocks[0].shape[1]
    half = rows // 2
    x[0] = jnp.zeros(x.shape[1:], BF16)
    x[rows + 1] = jnp.zeros(x.shape[1:], BF16)
    lists = []
    for part in range(rows // CHUNK):
        first = part * CHUNK
        copies = []
        for r in range(8):
            channel = pl.ds(pl.multiple_of(place_ref[r] * width, 16), width)
            block, skip = (blocks[r], 0) if r < 7 else (blocks[7 + first // half], first // half * half)
            copies.append(
                pltpu.make_async_copy(
                    block.at[first - skip : first - skip + CHUNK],
                    x.at[first + 1 : first + 1 + CHUNK, channel],
                    sems.at[part, r],
                )
            )
            copies[-1].start()
        lists.append(copies)
    return lists


def wait_for(copies):
    for copy in copies:
        copy.wait()


def forward_kernel(place_ref, after_ref, *rest):
    del after_ref
    blocks, (w_ref, out_ref, carry_ref, x, sems) = rest[:9], rest[9:]
    rows, width, lanes = out_ref.shape
    loads = start_loads(place_ref, blocks, x, sems)
    lhs = jnp.concatenate(
        [jnp.concatenate([w_ref[a * 3 + 2 - b] for a in range(3)], 0) for b in range(3)], 1
    )
    wait_for(loads[0])
    for h in range(rows):
        if (h + 1) % CHUNK == 0 and h + 1 < rows:
            wait_for(loads[(h + 1) // CHUNK])
        stack = jnp.reshape(x[h : h + 3], (3 * x.shape[1], lanes))
        y = jnp.dot(lhs, stack, preferred_element_type=F32)
        sums = []
        for e in range(3):
            frames = []
            for g in range(lanes // 128 + 2):
                terms = []
                for a in range(3):
                    f = g + a - 2
                    if 0 <= f < lanes // 128:
                        row = (a * 3 + e) * width
                        terms.append(y[row : row + width, f * 128 : f * 128 + 128])
                total = terms[0]
                for term in terms[1:]:
                    total = total + term
                frames.append(total)
            sums.append(jnp.concatenate(frames, 1))
        result = sums[1] + shifted(sums[0], 1) + shifted(sums[2], -1)
        out_ref[h] = result[:, :lanes]
        carry_ref[h, :width] = result[:, lanes : lanes + 128].astype(BF16)
        carry_ref[h, width:] = result[:, lanes + 128 :].astype(BF16)


def kernel_grad_kernel(place_ref, live_ref, rep_ref, after_ref, *rest):
    del after_ref
    blocks, (m_ref, head_ref, mine_ref, theirs_ref, x, taps, total, result, sems, out_sems) = rest[:9], rest[9:]
    rows, width, lanes = m_ref.shape
    loads = start_loads(place_ref, blocks, x, sems)
    fill_taps(live_ref, m_ref, head_ref, taps)
    depth = 9 * width
    result[9 * depth :, :] = jnp.zeros((result.shape[0] - 9 * depth, 128), F32)
    for h in range(rows):
        if h % CHUNK == 0:
            wait_for(loads[h // CHUNK])
        stack = jnp.reshape(taps[h : h + 3], (depth, taps.shape[2]))
        right = x[h + 1]
        for a in range(3):
            left = stack[:, (2 - a) * 128 : (2 - a) * 128 + lanes]
            product = lax.dot_general(
                left, right, (((1,), (1,)), ((), ())), preferred_element_type=F32
            )
            if h == 0:
                total[a] = product
            elif h < rows - 1:
                total[a] += product
            else:
                product = total[a] + product
                for block in range(3):
                    row = (a * 3 + block) * depth
                    result[row : row + depth, :] = product[:, block * 128 : block * 128 + 128]
    half = result.shape[0] // 2
    copies = []
    for slot, (target, rep) in enumerate(((theirs_ref, 1 - rep_ref[0]), (mine_ref, rep_ref[0]))):
        source = result.at[pl.ds(pl.multiple_of(rep * half, 16), half)]
        copies.append(pltpu.make_async_copy(source, target, out_sems.at[slot]))
        copies[-1].start()
    wait_for(copies)


def params():
    return pltpu.CompilerParams(vmem_limit_bytes=VMEM_LIMIT)


def cost(flops, size):
    return pl.CostEstimate(flops=flops, bytes_accessed=size, transcendentals=0)


FLOPS = 2 * 27 * 48 * 384 * 4096


def input_partials(place, live, m, head, weight):
    rows, width, lanes = m.shape
    channels = weight.shape[2]
    whole = jax.ShapeDtypeStruct((rows, width, lanes), BF16)
    half = jax.ShapeDtypeStruct((rows // 2, width, lanes), BF16)
    return pl.pallas_call(
        input_grad_kernel,
        out_shape=[whole] * 7 + [half] * 2,
        in_specs=[SMEM, SMEM, VMEM, VMEM, VMEM],
        out_specs=[ANY] * 9,
        scratch_shapes=[
            pltpu.VMEM((rows + 2, 3 * width, lanes + 256), BF16),
            pltpu.VMEM((channels, 27 * width), BF16),
            pltpu.VMEM((8, rows, width, lanes), BF16),
            pltpu.SemaphoreType.DMA((2, 8)),
        ],
        compiler_params=params(),
        cost_estimate=cost(FLOPS, 5_000_000),
        name="input_partials",
    )(place, live, m, head, weight)


def pick(row, origin, own, other):
    return pl.pallas_call(
        pick_kernel,
        out_shape=jax.ShapeDtypeStruct(own.shape, own.dtype),
        in_specs=[SMEM, SMEM, VMEM, VMEM],
        out_specs=VMEM,
        compiler_params=params(),
        name="pick",
    )(row, origin, own, other)


def forward(place, after, blocks, weight):
    rows, width, lanes = blocks[0].shape
    channels = weight.shape[2]
    return pl.pallas_call(
        forward_kernel,
        out_shape=[
            jax.ShapeDtypeStruct((rows, width, lanes), F32),
            jax.ShapeDtypeStruct((rows, 2 * width, 128), BF16),
        ],
        in_specs=[SMEM] + [ANY] * 10 + [VMEM],
        out_specs=[VMEM, VMEM],
        scratch_shapes=[
            pltpu.VMEM((rows + 2, channels, lanes), BF16),
            pltpu.SemaphoreType.DMA((rows // CHUNK, 8)),
        ],
        compiler_params=params(),
        cost_estimate=cost(FLOPS, 5_000_000),
        name="forward",
    )(place, after, *blocks, weight)


def kernel_grad(place, live, rep, after, blocks, m, head):
    rows, width, lanes = m.shape
    channels = 8 * width
    return pl.pallas_call(
        kernel_grad_kernel,
        out_shape=[jax.ShapeDtypeStruct((2048, 128), F32)] * 2,
        in_specs=[SMEM] * 3 + [ANY] * 10 + [VMEM, VMEM],
        out_specs=[ANY, ANY],
        scratch_shapes=[
            pltpu.VMEM((rows + 2, channels, lanes), BF16),
            pltpu.VMEM((rows + 2, 3 * width, lanes + 256), BF16),
            pltpu.VMEM((3, 9 * width, channels), F32),
            pltpu.VMEM((4096, 128), F32),
            pltpu.SemaphoreType.DMA((rows // CHUNK, 8)),
            pltpu.SemaphoreType.DMA((2,)),
        ],
        compiler_params=params(),
        cost_estimate=cost(FLOPS, 6_000_000),
        name="kernel_grad",
    )(place, live, rep, after, *blocks, m, head)


def to_rows(x):
    f, c, h, w = x.shape
    return x.transpose(2, 1, 0, 3).reshape(h, c, f * w)


def from_rows(x):
    h, c, lanes = x.shape
    return x.reshape(h, c, lanes // 128, 128).transpose(2, 1, 0, 3)


def core_swap(x):
    return lax.ppermute(x, "rep", [(0, 1), (1, 0)])


def exchange(x):
    return lax.all_to_all(x, "dp", 0, 0, tiled=True)


def handed_on(own, source):
    rep = lax.axis_index("rep")
    wanted = lax.dynamic_slice_in_dim(source, rep * 8, 8, 0)
    row = jnp.maximum(wanted, 0) % 8
    origin = jnp.where(wanted < 0, 0, jnp.where(wanted // 8 == rep, 1, 2)).astype(jnp.int32)
    return pick(row, origin, own, core_swap(own))


def first_exchange(mine, theirs, payload):
    pair = (mine + core_swap(theirs)).astype(BF16).reshape(8, 256, 128)
    return jnp.concatenate([pair, payload], 1)


def second_exchange(spread, scale, source):
    rep = lax.axis_index("rep")
    handed = handed_on(spread[:, 256:], source)
    share = (jnp.sum(spread[:, :256].astype(F32), 0) * scale).astype(BF16)
    share = jnp.broadcast_to(share[None], (8, 256, 128))
    spread = exchange(jnp.concatenate([share, handed], 1))
    half = spread[:, :256].reshape(2048, 128)
    there = core_swap(half)
    low = jnp.where(rep == 0, half, there)
    high = jnp.where(rep == 0, there, half)
    return jnp.concatenate([low, high], 0), spread[:, 256:]


def per_device(frames, weight, cotangent, prev_owner, lengths):
    seg_len, width, height, columns = frames.shape
    channels = weight.shape[4]
    rep, me = lax.axis_index("rep"), lax.axis_index("dp")
    member = rep * 8 + me
    tensor = Group("tensor", tensor_index, lambda i: (i // 2, i % 2))
    place = jnp.stack(tensor.absolute()).astype(jnp.int32)
    segments = jnp.arange(prev_owner.shape[0], dtype=jnp.int32)
    follows = prev_owner[None, :] == segments[:, None]
    follower = jnp.max(jnp.where(follows, segments[None, :], -1), 1)

    x = to_rows(frames)
    m = to_rows(cotangent)
    rows = weight.transpose(1, 2, 3, 0, 4)[:, ::-1].reshape(9, 3 * width, channels)

    payload, x = lax.optimization_barrier((m[:, :, :256], x))
    payload = exchange(payload)
    blocks = tensor.gather(x)
    head = exchange(handed_on(payload, follower))
    keep = jnp.arange(seg_len) < lengths[member]
    keep_head = jnp.arange(2) < lengths[jnp.maximum(follower[member], 0)]
    live = jnp.concatenate([keep, keep_head]).astype(jnp.int32)

    partials = input_partials(place, live, m, head, rows)
    partials, blocks = lax.optimization_barrier((partials, blocks))
    mine, theirs = kernel_grad(place, live, rep.astype(jnp.int32)[None], partials[0], blocks, m, head)
    conv, carry = forward(place, theirs, blocks, rows)
    spread = first_exchange(mine, theirs, carry)
    input_grad = from_rows(tensor.scatter_sum(partials))

    cells = prev_owner.shape[0] * seg_len * height * columns
    conv = conv.reshape(height, width, seg_len, columns).transpose(2, 1, 0, 3)
    spread, conv = lax.optimization_barrier((exchange(spread), conv))
    total, received = second_exchange(spread, 1.0 / math.sqrt(cells), prev_owner)
    total = total[: 81 * width].reshape(3, 3, 3, 3, width, 128)
    weight_grad = total[:, :, ::-1].transpose(4, 0, 2, 3, 1, 5).reshape(weight.shape).astype(F32)

    received = received.reshape(height, 2, width, columns).transpose(1, 2, 0, 3).astype(F32)
    conv = conv + jnp.concatenate([received, jnp.zeros_like(received)], 0)
    output = jnp.where(keep[:, None, None, None], conv, 0.0).astype(BF16)
    return (output, input_grad, weight_grad)


def solution(mesh):
    split = P(("rep", "dp"), "tensor", None, None)
    kernel = P("tensor", None, None, None, None)
    return jax.shard_map(
        per_device,
        mesh=mesh,
        in_specs=(split, kernel, split, P(), P()),
        out_specs=(split, split, kernel),
        check_vma=False,
    )
```

```python
import math

import jax
import jax.numpy as jnp
from jax import lax
from jax.experimental import pallas as pl
from jax.experimental.pallas import tpu as pltpu
from jax.sharding import PartitionSpec as P

BF16 = jnp.bfloat16
F32 = jnp.float32
VMEM_LIMIT = 56 * 1024 * 1024
ANY = pl.BlockSpec(memory_space=pl.ANY)
VMEM = pl.BlockSpec(memory_space=pltpu.VMEM)
SMEM = pl.BlockSpec(memory_space=pltpu.SMEM)

PLACES = ((0, 0), (0, 1), (1, 0), (3, 0), (1, 1), (3, 1), (2, 0), (2, 1))


def tensor_index(ring, pair):
    return ring * 2 + pair


class Group:
    def __init__(self, name, index_of, coords):
        self.name = name
        self.index_of = index_of
        me = lax.axis_index(name)
        self.ring, self.pair = coords(me)
        cells = [(r, p) for r in range(4) for p in range(2)]
        self.perm_up = [(index_of(r, p), index_of((r + 1) % 4, p)) for r, p in cells]
        self.perm_down = [(index_of(r, p), index_of((r + 3) % 4, p)) for r, p in cells]
        self.perm_swap = [(index_of(r, p), index_of(r, 1 - p)) for r, p in cells]

    def up(self, x):
        return lax.ppermute(x, self.name, self.perm_up)

    def down(self, x):
        return lax.ppermute(x, self.name, self.perm_down)

    def swap(self, x):
        return lax.ppermute(x, self.name, self.perm_swap)

    def absolute(self):
        return [self.index_of((self.ring + dr) % 4, self.pair ^ dp) for dr, dp in PLACES]

    def gather(self, x):
        half = x.shape[0] // 2
        following, prev, pair = lax.optimization_barrier((self.down(x), self.up(x), self.swap(x)))
        pair_next = self.swap(following)
        pair_prev = self.up(pair)
        second = self.down(following)
        far_a = self.down(pair_next[:half])
        far_b = self.up(pair_prev[half:])
        return [x, pair, following, prev, pair_next, pair_prev, second, far_a, far_b]

    def scatter_sum(self, parts, tie):
        own, pair, following, prev, pair_next, pair_prev, second, far_a, far_b = parts
        from_prev = self.down(prev)
        in_a = self.up(far_a)
        in_b = self.down(far_b)
        in_a, in_b, tie = lax.optimization_barrier((in_a, in_b, tie))
        pair_next = added(pair_next, jnp.concatenate([in_a, jnp.zeros_like(in_a)], 0))
        pair_prev = added(pair_prev, jnp.concatenate([jnp.zeros_like(in_b), in_b], 0))
        got_up = self.up(second)
        got_swap = self.swap(pair_next)
        got_down = self.down(pair_prev)
        last_up = self.up(added(following, got_swap, got_up))
        last_swap = self.swap(added(pair, got_down))
        return sum(x.astype(F32) for x in (own, from_prev, last_up, last_swap)), tie


def added(*terms):
    return sum(x.astype(F32) for x in terms).astype(BF16)


def shifted(x, by):
    lanes = x.shape[-1]
    column = lax.broadcasted_iota(jnp.int32, x.shape, x.ndim - 1) % 128
    rolled = pltpu.roll(x, by % lanes, x.ndim - 1)
    edge = 0 if by == 1 else 127
    return jnp.where(column == edge, 0.0, rolled)


def fill_taps(live_ref, m_ref, head_ref, taps):
    rows, width, lanes = m_ref.shape
    frames = taps.shape[2] // 128
    taps[0] = jnp.zeros(taps.shape[1:], BF16)
    taps[rows + 1] = jnp.zeros(taps.shape[1:], BF16)
    for h in range(rows):
        whole = jnp.concatenate([m_ref[h], head_ref[h]], 1).astype(F32)
        wide = jnp.concatenate(
            [
                jnp.where(live_ref[f] > 0, whole[:, f * 128 : f * 128 + 128], 0.0)
                for f in range(frames)
            ],
            1,
        )
        taps[h + 1, 0:width] = shifted(wide, -1).astype(BF16)
        taps[h + 1, width : 2 * width] = wide.astype(BF16)
        taps[h + 1, 2 * width : 3 * width] = shifted(wide, 1).astype(BF16)


def input_grad_kernel(place_ref, live_ref, after_ref, m_ref, head_ref, w_ref, *rest):
    del after_ref
    outs, (taps, wt, parts, sems) = rest[:9], rest[9:]
    rows, width, lanes = m_ref.shape
    half = rows // 2
    fill_taps(live_ref, m_ref, head_ref, taps)
    depth = 3 * 3 * width
    for a in range(3):
        block = jnp.concatenate([w_ref[a * 3 + b] for b in range(3)], 0)
        wt[:, a * depth : (a + 1) * depth] = block.T

    copies = []
    for h in range(rows):
        stack = jnp.reshape(taps[h : h + 3], (depth, taps.shape[2]))
        for start in range(0, lanes, 256):
            rhs = jnp.concatenate(
                [stack[:, (2 - a) * 128 + start : (2 - a) * 128 + start + 256] for a in range(3)], 0
            )
            total = jnp.dot(wt[...], rhs, preferred_element_type=F32).astype(BF16)
            for t in range(8):
                parts[t, h, :, start : start + 256] = total[t * width : (t + 1) * width]
        if h % half == half - 1:
            part, first = h // half, h + 1 - half
            for r in range(8):
                source = parts.at[place_ref[r], first : first + half]
                target = outs[r].at[first : first + half] if r < 7 else outs[7 + part]
                copies.append(pltpu.make_async_copy(source, target, sems.at[part, r]))
                copies[-1].start()
    for copy in copies:
        copy.wait()


def pick_kernel(row_ref, from_ref, own_ref, other_ref, out_ref):
    for d in range(out_ref.shape[0]):
        own, other = own_ref[row_ref[d]], other_ref[row_ref[d]]
        chosen = jnp.where(from_ref[d] == 1, own, other)
        out_ref[d] = jnp.where(from_ref[d] == 0, jnp.zeros_like(chosen), chosen)


CHUNK = 2


def start_loads(place_ref, blocks, x, sems):
    rows, width = blocks[0].shape[0], blocks[0].shape[1]
    half = rows // 2
    x[0] = jnp.zeros(x.shape[1:], BF16)
    x[rows + 1] = jnp.zeros(x.shape[1:], BF16)
    lists = []
    for part in range(rows // CHUNK):
        first = part * CHUNK
        copies = []
        for r in range(8):
            channel = pl.ds(pl.multiple_of(place_ref[r] * width, 16), width)
            block, skip = (blocks[r], 0) if r < 7 else (blocks[7 + first // half], first // half * half)
            copies.append(
                pltpu.make_async_copy(
                    block.at[first - skip : first - skip + CHUNK],
                    x.at[first + 1 : first + 1 + CHUNK, channel],
                    sems.at[part, r],
                )
            )
            copies[-1].start()
        lists.append(copies)
    return lists


def wait_for(copies):
    for copy in copies:
        copy.wait()


def forward_kernel(place_ref, *rest):
    blocks, (w_ref, out_ref, carry_ref, x, sems) = rest[:9], rest[9:]
    rows, width, lanes = out_ref.shape
    loads = start_loads(place_ref, blocks, x, sems)
    lhs = jnp.concatenate(
        [jnp.concatenate([w_ref[a * 3 + 2 - b] for a in range(3)], 0) for b in range(3)], 1
    )
    wait_for(loads[0])
    for h in range(rows):
        if (h + 1) % CHUNK == 0 and h + 1 < rows:
            wait_for(loads[(h + 1) // CHUNK])
        stack = jnp.reshape(x[h : h + 3], (3 * x.shape[1], lanes))
        y = jnp.dot(lhs, stack, preferred_element_type=F32)
        sums = []
        for e in range(3):
            frames = []
            for g in range(lanes // 128 + 2):
                terms = []
                for a in range(3):
                    f = g + a - 2
                    if 0 <= f < lanes // 128:
                        row = (a * 3 + e) * width
                        terms.append(y[row : row + width, f * 128 : f * 128 + 128])
                total = terms[0]
                for term in terms[1:]:
                    total = total + term
                frames.append(total)
            sums.append(jnp.concatenate(frames, 1))
        result = sums[1] + shifted(sums[0], 1) + shifted(sums[2], -1)
        out_ref[h] = result[:, :lanes]
        carry_ref[h, :width] = result[:, lanes : lanes + 128].astype(BF16)
        carry_ref[h, width:] = result[:, lanes + 128 :].astype(BF16)


def kernel_grad_kernel(place_ref, live_ref, rep_ref, after_ref, *rest):
    del after_ref
    blocks, (m_ref, head_ref, mine_ref, theirs_ref, x, taps, total, result, sems, out_sems) = rest[:9], rest[9:]
    rows, width, lanes = m_ref.shape
    loads = start_loads(place_ref, blocks, x, sems)
    fill_taps(live_ref, m_ref, head_ref, taps)
    depth = 9 * width
    result[9 * depth :, :] = jnp.zeros((result.shape[0] - 9 * depth, 128), F32)
    for h in range(rows):
        if h % CHUNK == 0:
            wait_for(loads[h // CHUNK])
        stack = jnp.reshape(taps[h : h + 3], (depth, taps.shape[2]))
        right = x[h + 1]
        for a in range(3):
            left = stack[:, (2 - a) * 128 : (2 - a) * 128 + lanes]
            product = lax.dot_general(
                left, right, (((1,), (1,)), ((), ())), preferred_element_type=F32
            )
            if h == 0:
                total[a] = product
            elif h < rows - 1:
                total[a] += product
            else:
                product = total[a] + product
                for block in range(3):
                    row = (a * 3 + block) * depth
                    result[row : row + depth, :] = product[:, block * 128 : block * 128 + 128]
    half = result.shape[0] // 2
    copies = []
    for slot, (target, rep) in enumerate(((theirs_ref, 1 - rep_ref[0]), (mine_ref, rep_ref[0]))):
        source = result.at[pl.ds(pl.multiple_of(rep * half, 16), half)]
        copies.append(pltpu.make_async_copy(source, target, out_sems.at[slot]))
        copies[-1].start()
    wait_for(copies)


def params():
    return pltpu.CompilerParams(vmem_limit_bytes=VMEM_LIMIT)


def cost(flops, size):
    return pl.CostEstimate(flops=flops, bytes_accessed=size, transcendentals=0)


FLOPS = 2 * 27 * 48 * 384 * 4096


def input_partials(place, live, after, m, head, weight):
    rows, width, lanes = m.shape
    channels = weight.shape[2]
    whole = jax.ShapeDtypeStruct((rows, width, lanes), BF16)
    half = jax.ShapeDtypeStruct((rows // 2, width, lanes), BF16)
    return pl.pallas_call(
        input_grad_kernel,
        out_shape=[whole] * 7 + [half] * 2,
        in_specs=[SMEM, SMEM, ANY, VMEM, VMEM, VMEM],
        out_specs=[ANY] * 9,
        scratch_shapes=[
            pltpu.VMEM((rows + 2, 3 * width, lanes + 256), BF16),
            pltpu.VMEM((channels, 27 * width), BF16),
            pltpu.VMEM((8, rows, width, lanes), BF16),
            pltpu.SemaphoreType.DMA((2, 8)),
        ],
        compiler_params=params(),
        cost_estimate=cost(FLOPS, 5_000_000),
        name="input_partials",
    )(place, live, after, m, head, weight)


def pick(row, origin, own, other):
    return pl.pallas_call(
        pick_kernel,
        out_shape=jax.ShapeDtypeStruct(own.shape, own.dtype),
        in_specs=[SMEM, SMEM, VMEM, VMEM],
        out_specs=VMEM,
        compiler_params=params(),
        name="pick",
    )(row, origin, own, other)


def forward(place, blocks, weight):
    rows, width, lanes = blocks[0].shape
    channels = weight.shape[2]
    return pl.pallas_call(
        forward_kernel,
        out_shape=[
            jax.ShapeDtypeStruct((rows, width, lanes), F32),
            jax.ShapeDtypeStruct((rows, 2 * width, 128), BF16),
        ],
        in_specs=[SMEM] + [ANY] * 9 + [VMEM],
        out_specs=[VMEM, VMEM],
        scratch_shapes=[
            pltpu.VMEM((rows + 2, channels, lanes), BF16),
            pltpu.SemaphoreType.DMA((rows // CHUNK, 8)),
        ],
        compiler_params=params(),
        cost_estimate=cost(FLOPS, 5_000_000),
        name="forward",
    )(place, *blocks, weight)


def kernel_grad(place, live, rep, after, blocks, m, head):
    rows, width, lanes = m.shape
    channels = 8 * width
    return pl.pallas_call(
        kernel_grad_kernel,
        out_shape=[jax.ShapeDtypeStruct((2048, 128), F32)] * 2,
        in_specs=[SMEM] * 3 + [ANY] * 10 + [VMEM, VMEM],
        out_specs=[ANY, ANY],
        scratch_shapes=[
            pltpu.VMEM((rows + 2, channels, lanes), BF16),
            pltpu.VMEM((rows + 2, 3 * width, lanes + 256), BF16),
            pltpu.VMEM((3, 9 * width, channels), F32),
            pltpu.VMEM((4096, 128), F32),
            pltpu.SemaphoreType.DMA((rows // CHUNK, 8)),
            pltpu.SemaphoreType.DMA((2,)),
        ],
        compiler_params=params(),
        cost_estimate=cost(FLOPS, 6_000_000),
        name="kernel_grad",
    )(place, live, rep, after, *blocks, m, head)


def to_rows(x):
    f, c, h, w = x.shape
    return x.transpose(2, 1, 0, 3).reshape(h, c, f * w)


def from_rows(x):
    h, c, lanes = x.shape
    return x.reshape(h, c, lanes // 128, 128).transpose(2, 1, 0, 3)


def core_swap(x):
    return lax.ppermute(x, "rep", [(0, 1), (1, 0)])


def exchange(x):
    return lax.all_to_all(x, "dp", 0, 0, tiled=True)


def handed_on(own, source):
    rep = lax.axis_index("rep")
    wanted = lax.dynamic_slice_in_dim(source, rep * 8, 8, 0)
    row = jnp.maximum(wanted, 0) % 8
    origin = jnp.where(wanted < 0, 0, jnp.where(wanted // 8 == rep, 1, 2)).astype(jnp.int32)
    return pick(row, origin, own, core_swap(own))


def first_exchange(mine, theirs, payload):
    pair = (mine + core_swap(theirs)).astype(BF16).reshape(8, 256, 128)
    return jnp.concatenate([pair, payload], 1)


def second_exchange(spread, scale, source):
    rep = lax.axis_index("rep")
    handed = handed_on(spread[:, 256:], source)
    share = (jnp.sum(spread[:, :256].astype(F32), 0) * scale).astype(BF16)
    share = jnp.broadcast_to(share[None], (8, 256, 128))
    spread = exchange(jnp.concatenate([share, handed], 1))
    half = spread[:, :256].reshape(2048, 128)
    there = core_swap(half)
    low = jnp.where(rep == 0, half, there)
    high = jnp.where(rep == 0, there, half)
    return jnp.concatenate([low, high], 0), spread[:, 256:]


def per_device(frames, weight, cotangent, prev_owner, lengths):
    seg_len, width, height, columns = frames.shape
    channels = weight.shape[4]
    rep, me = lax.axis_index("rep"), lax.axis_index("dp")
    member = rep * 8 + me
    tensor = Group("tensor", tensor_index, lambda i: (i // 2, i % 2))
    place = jnp.stack(tensor.absolute()).astype(jnp.int32)
    segments = jnp.arange(prev_owner.shape[0], dtype=jnp.int32)
    follows = prev_owner[None, :] == segments[:, None]
    follower = jnp.max(jnp.where(follows, segments[None, :], -1), 1)

    x = to_rows(frames)
    m = to_rows(cotangent)
    rows = weight.transpose(1, 2, 3, 0, 4)[:, ::-1].reshape(9, 3 * width, channels)

    payload, x = lax.optimization_barrier((m[:, :, :256], x))
    payload = exchange(payload)
    blocks = tensor.gather(x)
    payload, _ = lax.optimization_barrier((payload, blocks[4]))
    head = exchange(handed_on(payload, follower))
    keep = jnp.arange(seg_len) < lengths[member]
    keep_head = jnp.arange(2) < lengths[jnp.maximum(follower[member], 0)]
    live = jnp.concatenate([keep, keep_head]).astype(jnp.int32)

    conv, carry = forward(place, blocks, rows)
    mine, theirs = kernel_grad(place, live, rep.astype(jnp.int32)[None], carry, blocks, m, head)
    spread = first_exchange(mine, theirs, carry)
    partials = input_partials(place, live, spread, m, head, rows)
    input_grad, spread = tensor.scatter_sum(partials, exchange(spread))
    input_grad = from_rows(input_grad)

    cells = prev_owner.shape[0] * seg_len * height * columns
    conv = conv.reshape(height, width, seg_len, columns).transpose(2, 1, 0, 3)
    spread, conv = lax.optimization_barrier((spread, conv))
    total, received = second_exchange(spread, 1.0 / math.sqrt(cells), prev_owner)
    total = total[: 81 * width].reshape(3, 3, 3, 3, width, 128)
    weight_grad = total[:, :, ::-1].transpose(4, 0, 2, 3, 1, 5).reshape(weight.shape).astype(F32)

    received = received.reshape(height, 2, width, columns).transpose(1, 2, 0, 3).astype(F32)
    conv = conv + jnp.concatenate([received, jnp.zeros_like(received)], 0)
    output = jnp.where(keep[:, None, None, None], conv, 0.0).astype(BF16)
    return (output, input_grad, weight_grad)


def solution(mesh):
    split = P(("rep", "dp"), "tensor", None, None)
    kernel = P("tensor", None, None, None, None)
    return jax.shard_map(
        per_device,
        mesh=mesh,
        in_specs=(split, kernel, split, P(), P()),
        out_specs=(split, split, kernel),
        check_vma=False,
    )
```

```python
import math

import jax
import jax.numpy as jnp
from jax import lax
from jax.experimental import pallas as pl
from jax.experimental.pallas import tpu as pltpu
from jax.sharding import PartitionSpec as P

BF16 = jnp.bfloat16
F32 = jnp.float32
VMEM_LIMIT = 56 * 1024 * 1024
ANY = pl.BlockSpec(memory_space=pl.ANY)
VMEM = pl.BlockSpec(memory_space=pltpu.VMEM)
SMEM = pl.BlockSpec(memory_space=pltpu.SMEM)

PLACES = ((0, 0), (0, 1), (1, 0), (3, 0), (1, 1), (3, 1), (2, 0), (2, 1))


def tensor_index(ring, pair):
    return ring * 2 + pair


class Group:
    def __init__(self, name, index_of, coords):
        self.name = name
        self.index_of = index_of
        me = lax.axis_index(name)
        self.ring, self.pair = coords(me)
        cells = [(r, p) for r in range(4) for p in range(2)]
        self.perm_up = [(index_of(r, p), index_of((r + 1) % 4, p)) for r, p in cells]
        self.perm_down = [(index_of(r, p), index_of((r + 3) % 4, p)) for r, p in cells]
        self.perm_swap = [(index_of(r, p), index_of(r, 1 - p)) for r, p in cells]

    def up(self, x):
        return lax.ppermute(x, self.name, self.perm_up)

    def down(self, x):
        return lax.ppermute(x, self.name, self.perm_down)

    def swap(self, x):
        return lax.ppermute(x, self.name, self.perm_swap)

    def absolute(self):
        return [self.index_of((self.ring + dr) % 4, self.pair ^ dp) for dr, dp in PLACES]

    def gather(self, x):
        half = x.shape[0] // 2
        following, prev, pair = lax.optimization_barrier((self.down(x), self.up(x), self.swap(x)))
        pair_next = self.swap(following)
        pair_prev = self.up(pair)
        second = self.down(following)
        far_a = self.down(pair_next[:half])
        far_b = self.up(pair_prev[half:])
        return [x, pair, following, prev, pair_next, pair_prev, second, far_a, far_b]

    def scatter_sum(self, parts, tie):
        own, pair, following, prev, pair_next, pair_prev, second, far_a, far_b = parts
        from_prev = self.down(prev)
        in_a = self.up(far_a)
        in_b = self.down(far_b)
        in_a, in_b, tie = lax.optimization_barrier((in_a, in_b, tie))
        pair_next = added(pair_next, jnp.concatenate([in_a, jnp.zeros_like(in_a)], 0))
        pair_prev = added(pair_prev, jnp.concatenate([jnp.zeros_like(in_b), in_b], 0))
        got_up = self.up(second)
        got_swap = self.swap(pair_next)
        got_down = self.down(pair_prev)
        last_up = self.up(added(following, got_swap, got_up))
        last_swap = self.swap(added(pair, got_down))
        return sum(x.astype(F32) for x in (own, from_prev, last_up, last_swap)), tie


def added(*terms):
    return sum(x.astype(F32) for x in terms).astype(BF16)


def shifted(x, by):
    lanes = x.shape[-1]
    column = lax.broadcasted_iota(jnp.int32, x.shape, x.ndim - 1) % 128
    rolled = pltpu.roll(x, by % lanes, x.ndim - 1)
    edge = 0 if by == 1 else 127
    return jnp.where(column == edge, 0.0, rolled)


def fill_taps(live_ref, m_ref, head_ref, taps):
    rows, width, lanes = m_ref.shape
    frames = taps.shape[2] // 128
    taps[0] = jnp.zeros(taps.shape[1:], BF16)
    taps[rows + 1] = jnp.zeros(taps.shape[1:], BF16)
    for h in range(rows):
        whole = jnp.concatenate([m_ref[h], head_ref[h]], 1).astype(F32)
        wide = jnp.concatenate(
            [
                jnp.where(live_ref[f] > 0, whole[:, f * 128 : f * 128 + 128], 0.0)
                for f in range(frames)
            ],
            1,
        )
        taps[h + 1, 0:width] = shifted(wide, -1).astype(BF16)
        taps[h + 1, width : 2 * width] = wide.astype(BF16)
        taps[h + 1, 2 * width : 3 * width] = shifted(wide, 1).astype(BF16)


def input_grad_kernel(place_ref, live_ref, after_ref, m_ref, head_ref, w_ref, *rest):
    del after_ref
    outs, (taps, wt, parts, sems) = rest[:9], rest[9:]
    rows, width, lanes = m_ref.shape
    half = rows // 2
    fill_taps(live_ref, m_ref, head_ref, taps)
    depth = 3 * 3 * width
    for a in range(3):
        block = jnp.concatenate([w_ref[a * 3 + b] for b in range(3)], 0)
        wt[:, a * depth : (a + 1) * depth] = block.T

    copies = []
    for h in range(rows):
        stack = jnp.reshape(taps[h : h + 3], (depth, taps.shape[2]))
        for start in range(0, lanes, 256):
            rhs = jnp.concatenate(
                [stack[:, (2 - a) * 128 + start : (2 - a) * 128 + start + 256] for a in range(3)], 0
            )
            total = jnp.dot(wt[...], rhs, preferred_element_type=F32).astype(BF16)
            for t in range(8):
                parts[t, h, :, start : start + 256] = total[t * width : (t + 1) * width]
        if h % half == half - 1:
            part, first = h // half, h + 1 - half
            for r in range(8):
                source = parts.at[place_ref[r], first : first + half]
                target = outs[r].at[first : first + half] if r < 7 else outs[7 + part]
                copies.append(pltpu.make_async_copy(source, target, sems.at[part, r]))
                copies[-1].start()
    for copy in copies:
        copy.wait()


CHUNK = 2


def start_loads(place_ref, blocks, x, sems):
    rows, width = blocks[0].shape[0], blocks[0].shape[1]
    half = rows // 2
    x[0] = jnp.zeros(x.shape[1:], BF16)
    x[rows + 1] = jnp.zeros(x.shape[1:], BF16)
    lists = []
    for part in range(rows // CHUNK):
        first = part * CHUNK
        copies = []
        for r in range(8):
            channel = pl.ds(pl.multiple_of(place_ref[r] * width, 16), width)
            block, skip = (blocks[r], 0) if r < 7 else (blocks[7 + first // half], first // half * half)
            copies.append(
                pltpu.make_async_copy(
                    block.at[first - skip : first - skip + CHUNK],
                    x.at[first + 1 : first + 1 + CHUNK, channel],
                    sems.at[part, r],
                )
            )
            copies[-1].start()
        lists.append(copies)
    return lists


def wait_for(copies):
    for copy in copies:
        copy.wait()


def forward_kernel(place_ref, *rest):
    blocks, (w_ref, out_ref, carry_ref, x, sems) = rest[:9], rest[9:]
    rows, width, lanes = out_ref.shape
    loads = start_loads(place_ref, blocks, x, sems)
    lhs = jnp.concatenate(
        [jnp.concatenate([w_ref[a * 3 + 2 - b] for a in range(3)], 0) for b in range(3)], 1
    )
    wait_for(loads[0])
    for h in range(rows):
        if (h + 1) % CHUNK == 0 and h + 1 < rows:
            wait_for(loads[(h + 1) // CHUNK])
        stack = jnp.reshape(x[h : h + 3], (3 * x.shape[1], lanes))
        y = jnp.dot(lhs, stack, preferred_element_type=F32)
        sums = []
        for e in range(3):
            frames = []
            for g in range(lanes // 128 + 2):
                terms = []
                for a in range(3):
                    f = g + a - 2
                    if 0 <= f < lanes // 128:
                        row = (a * 3 + e) * width
                        terms.append(y[row : row + width, f * 128 : f * 128 + 128])
                total = terms[0]
                for term in terms[1:]:
                    total = total + term
                frames.append(total)
            sums.append(jnp.concatenate(frames, 1))
        result = sums[1] + shifted(sums[0], 1) + shifted(sums[2], -1)
        out_ref[h] = result[:, :lanes]
        carry_ref[h, :width] = result[:, lanes : lanes + 128].astype(BF16)
        carry_ref[h, width:] = result[:, lanes + 128 :].astype(BF16)


def kernel_grad_kernel(place_ref, live_ref, rep_ref, after_ref, *rest):
    del after_ref
    blocks, (m_ref, head_ref, mine_ref, theirs_ref, x, taps, total, result, sems, out_sems) = rest[:9], rest[9:]
    rows, width, lanes = m_ref.shape
    loads = start_loads(place_ref, blocks, x, sems)
    fill_taps(live_ref, m_ref, head_ref, taps)
    depth = 9 * width
    result[9 * depth :, :] = jnp.zeros((result.shape[0] - 9 * depth, 128), F32)
    for h in range(rows):
        if h % CHUNK == 0:
            wait_for(loads[h // CHUNK])
        stack = jnp.reshape(taps[h : h + 3], (depth, taps.shape[2]))
        right = x[h + 1]
        for a in range(3):
            left = stack[:, (2 - a) * 128 : (2 - a) * 128 + lanes]
            product = lax.dot_general(
                left, right, (((1,), (1,)), ((), ())), preferred_element_type=F32
            )
            if h == 0:
                total[a] = product
            elif h < rows - 1:
                total[a] += product
            else:
                product = total[a] + product
                for block in range(3):
                    row = (a * 3 + block) * depth
                    result[row : row + depth, :] = product[:, block * 128 : block * 128 + 128]
    half = result.shape[0] // 2
    copies = []
    for slot, (target, rep) in enumerate(((theirs_ref, 1 - rep_ref[0]), (mine_ref, rep_ref[0]))):
        source = result.at[pl.ds(pl.multiple_of(rep * half, 16), half)]
        copies.append(pltpu.make_async_copy(source, target, out_sems.at[slot]))
        copies[-1].start()
    wait_for(copies)


def params():
    return pltpu.CompilerParams(vmem_limit_bytes=VMEM_LIMIT)


def cost(flops, size):
    return pl.CostEstimate(flops=flops, bytes_accessed=size, transcendentals=0)


FLOPS = 2 * 27 * 48 * 384 * 4096


def input_partials(place, live, after, m, head, weight):
    rows, width, lanes = m.shape
    channels = weight.shape[2]
    whole = jax.ShapeDtypeStruct((rows, width, lanes), BF16)
    half = jax.ShapeDtypeStruct((rows // 2, width, lanes), BF16)
    return pl.pallas_call(
        input_grad_kernel,
        out_shape=[whole] * 7 + [half] * 2,
        in_specs=[SMEM, SMEM, ANY, VMEM, VMEM, VMEM],
        out_specs=[ANY] * 9,
        scratch_shapes=[
            pltpu.VMEM((rows + 2, 3 * width, lanes + 256), BF16),
            pltpu.VMEM((channels, 27 * width), BF16),
            pltpu.VMEM((8, rows, width, lanes), BF16),
            pltpu.SemaphoreType.DMA((2, 8)),
        ],
        compiler_params=params(),
        cost_estimate=cost(FLOPS, 5_000_000),
        name="input_partials",
    )(place, live, after, m, head, weight)


def forward(place, blocks, weight):
    rows, width, lanes = blocks[0].shape
    channels = weight.shape[2]
    return pl.pallas_call(
        forward_kernel,
        out_shape=[
            jax.ShapeDtypeStruct((rows, width, lanes), F32),
            jax.ShapeDtypeStruct((rows, 2 * width, 128), BF16),
        ],
        in_specs=[SMEM] + [ANY] * 9 + [VMEM],
        out_specs=[VMEM, VMEM],
        scratch_shapes=[
            pltpu.VMEM((rows + 2, channels, lanes), BF16),
            pltpu.SemaphoreType.DMA((rows // CHUNK, 8)),
        ],
        compiler_params=params(),
        cost_estimate=cost(FLOPS, 5_000_000),
        name="forward",
    )(place, *blocks, weight)


def kernel_grad(place, live, rep, after, blocks, m, head):
    rows, width, lanes = m.shape
    channels = 8 * width
    return pl.pallas_call(
        kernel_grad_kernel,
        out_shape=[jax.ShapeDtypeStruct((2048, 128), F32)] * 2,
        in_specs=[SMEM] * 3 + [ANY] * 10 + [VMEM, VMEM],
        out_specs=[ANY, ANY],
        scratch_shapes=[
            pltpu.VMEM((rows + 2, channels, lanes), BF16),
            pltpu.VMEM((rows + 2, 3 * width, lanes + 256), BF16),
            pltpu.VMEM((3, 9 * width, channels), F32),
            pltpu.VMEM((4096, 128), F32),
            pltpu.SemaphoreType.DMA((rows // CHUNK, 8)),
            pltpu.SemaphoreType.DMA((2,)),
        ],
        compiler_params=params(),
        cost_estimate=cost(FLOPS, 6_000_000),
        name="kernel_grad",
    )(place, live, rep, after, *blocks, m, head)


def to_rows(x):
    f, c, h, w = x.shape
    return x.transpose(2, 1, 0, 3).reshape(h, c, f * w)


def from_rows(x):
    h, c, lanes = x.shape
    return x.reshape(h, c, lanes // 128, 128).transpose(2, 1, 0, 3)


def core_swap(x):
    return lax.ppermute(x, "rep", [(0, 1), (1, 0)])


def exchange(x):
    return lax.all_to_all(x, "dp", 0, 0, tiled=True)


def route(payload, source):
    rep, me = lax.axis_index("rep"), lax.axis_index("dp")
    blocks = lax.all_gather(payload, "dp", axis=0)
    mine, other = source[rep * 8 + me], source[(1 - rep) * 8 + me]
    crossed = core_swap(lax.dynamic_index_in_dim(blocks, jnp.maximum(other, 0) % 8, 0, False))
    direct = lax.dynamic_index_in_dim(blocks, jnp.maximum(mine, 0) % 8, 0, False)
    result = jnp.where(jnp.maximum(mine, 0) // 8 == rep, direct, crossed)
    return jnp.where(mine >= 0, result, jnp.zeros_like(result))


def chip_sum(mine, theirs):
    return (mine + core_swap(theirs)).astype(BF16).reshape(8, 256, 128)


def all_rows(spread, scale):
    rep = lax.axis_index("rep")
    share = (jnp.sum(spread.astype(F32), 0) * scale).astype(BF16)
    half = exchange(jnp.broadcast_to(share[None], (8, 256, 128))).reshape(2048, 128)
    there = core_swap(half)
    low = jnp.where(rep == 0, half, there)
    high = jnp.where(rep == 0, there, half)
    return jnp.concatenate([low, high], 0)


def per_device(frames, weight, cotangent, prev_owner, lengths):
    seg_len, width, height, columns = frames.shape
    channels = weight.shape[4]
    rep, me = lax.axis_index("rep"), lax.axis_index("dp")
    member = rep * 8 + me
    tensor = Group("tensor", tensor_index, lambda i: (i // 2, i % 2))
    place = jnp.stack(tensor.absolute()).astype(jnp.int32)
    segments = jnp.arange(prev_owner.shape[0], dtype=jnp.int32)
    follows = prev_owner[None, :] == segments[:, None]
    follower = jnp.max(jnp.where(follows, segments[None, :], -1), 1)

    x = to_rows(frames)
    m = to_rows(cotangent)
    rows = weight.transpose(1, 2, 3, 0, 4)[:, ::-1].reshape(9, 3 * width, channels)

    payload, x = lax.optimization_barrier((m[:, :, :256], x))
    blocks = tensor.gather(x)
    head = route(payload, follower)
    keep = jnp.arange(seg_len) < lengths[member]
    keep_head = jnp.arange(2) < lengths[jnp.maximum(follower[member], 0)]
    live = jnp.concatenate([keep, keep_head]).astype(jnp.int32)

    conv, carry = forward(place, blocks, rows)
    received = route(carry, prev_owner)
    conv = conv.reshape(height, width, seg_len, columns).transpose(2, 1, 0, 3)
    mine, theirs = kernel_grad(place, live, rep.astype(jnp.int32)[None], carry, blocks, m, head)
    spread = chip_sum(mine, theirs)
    partials = input_partials(place, live, spread, m, head, rows)
    input_grad, spread = tensor.scatter_sum(partials, exchange(spread))
    input_grad = from_rows(input_grad)

    cells = prev_owner.shape[0] * seg_len * height * columns
    total = all_rows(spread, 1.0 / math.sqrt(cells))
    total = total[: 81 * width].reshape(3, 3, 3, 3, width, 128)
    weight_grad = total[:, :, ::-1].transpose(4, 0, 2, 3, 1, 5).reshape(weight.shape).astype(F32)

    received = received.reshape(height, 2, width, columns).transpose(1, 2, 0, 3).astype(F32)
    conv = conv + jnp.concatenate([received, jnp.zeros_like(received)], 0)
    output = jnp.where(keep[:, None, None, None], conv, 0.0).astype(BF16)
    return (output, input_grad, weight_grad)


def solution(mesh):
    split = P(("rep", "dp"), "tensor", None, None)
    kernel = P("tensor", None, None, None, None)
    return jax.shard_map(
        per_device,
        mesh=mesh,
        in_specs=(split, kernel, split, P(), P()),
        out_specs=(split, split, kernel),
        check_vma=False,
    )
```

```python
import math

import jax
import jax.numpy as jnp
from jax import lax
from jax.experimental import pallas as pl
from jax.experimental.pallas import tpu as pltpu
from jax.sharding import PartitionSpec as P

BF16 = jnp.bfloat16
F32 = jnp.float32
VMEM_LIMIT = 56 * 1024 * 1024
ANY = pl.BlockSpec(memory_space=pl.ANY)
VMEM = pl.BlockSpec(memory_space=pltpu.VMEM)
SMEM = pl.BlockSpec(memory_space=pltpu.SMEM)

PLACES = ((0, 0), (0, 1), (1, 0), (3, 0), (1, 1), (3, 1), (2, 0), (2, 1))


def tensor_index(ring, pair):
    return ring * 2 + pair


class Group:
    def __init__(self, name, index_of, coords):
        self.name = name
        self.index_of = index_of
        me = lax.axis_index(name)
        self.ring, self.pair = coords(me)
        cells = [(r, p) for r in range(4) for p in range(2)]
        self.perm_up = [(index_of(r, p), index_of((r + 1) % 4, p)) for r, p in cells]
        self.perm_down = [(index_of(r, p), index_of((r + 3) % 4, p)) for r, p in cells]
        self.perm_swap = [(index_of(r, p), index_of(r, 1 - p)) for r, p in cells]

    def up(self, x):
        return lax.ppermute(x, self.name, self.perm_up)

    def down(self, x):
        return lax.ppermute(x, self.name, self.perm_down)

    def swap(self, x):
        return lax.ppermute(x, self.name, self.perm_swap)

    def absolute(self):
        return [self.index_of((self.ring + dr) % 4, self.pair ^ dp) for dr, dp in PLACES]

    def gather(self, x):
        half = x.shape[0] // 2
        following, prev, pair = lax.optimization_barrier((self.down(x), self.up(x), self.swap(x)))
        pair_next = self.swap(following)
        pair_prev = self.up(pair)
        second = self.down(following)
        far_a = self.down(pair_next[:half])
        far_b = self.up(pair_prev[half:])
        return [x, pair, following, prev, pair_next, pair_prev, second, far_a, far_b]

    def scatter_sum(self, parts):
        own, pair, following, prev, pair_next, pair_prev, second, far_a, far_b = parts
        from_prev = self.down(prev)
        in_a = self.up(far_a)
        in_b = self.down(far_b)
        pair_next = added(pair_next, jnp.concatenate([in_a, jnp.zeros_like(in_a)], 0))
        pair_prev = added(pair_prev, jnp.concatenate([jnp.zeros_like(in_b), in_b], 0))
        got_up = self.up(second)
        got_swap = self.swap(pair_next)
        got_down = self.down(pair_prev)
        last_up = self.up(added(following, got_swap, got_up))
        last_swap = self.swap(added(pair, got_down))
        return sum(x.astype(F32) for x in (own, from_prev, last_up, last_swap))


def added(*terms):
    return sum(x.astype(F32) for x in terms).astype(BF16)


def shifted(x, by):
    lanes = x.shape[-1]
    column = lax.broadcasted_iota(jnp.int32, x.shape, x.ndim - 1) % 128
    rolled = pltpu.roll(x, by % lanes, x.ndim - 1)
    edge = 0 if by == 1 else 127
    return jnp.where(column == edge, 0.0, rolled)


def fill_taps(live_ref, m_ref, head_ref, taps):
    rows, width, lanes = m_ref.shape
    frames = taps.shape[2] // 128
    taps[0] = jnp.zeros(taps.shape[1:], BF16)
    taps[rows + 1] = jnp.zeros(taps.shape[1:], BF16)
    for h in range(rows):
        whole = jnp.concatenate([m_ref[h], head_ref[h]], 1).astype(F32)
        wide = jnp.concatenate(
            [
                jnp.where(live_ref[f] > 0, whole[:, f * 128 : f * 128 + 128], 0.0)
                for f in range(frames)
            ],
            1,
        )
        taps[h + 1, 0:width] = shifted(wide, -1).astype(BF16)
        taps[h + 1, width : 2 * width] = wide.astype(BF16)
        taps[h + 1, 2 * width : 3 * width] = shifted(wide, 1).astype(BF16)


def input_grad_kernel(place_ref, live_ref, m_ref, head_ref, w_ref, *rest):
    outs, (taps, wt, parts, sems) = rest[:9], rest[9:]
    rows, width, lanes = m_ref.shape
    half = rows // 2
    fill_taps(live_ref, m_ref, head_ref, taps)
    depth = 3 * 3 * width
    for a in range(3):
        block = jnp.concatenate([w_ref[a * 3 + b] for b in range(3)], 0)
        wt[:, a * depth : (a + 1) * depth] = block.T

    copies = []
    for h in range(rows):
        stack = jnp.reshape(taps[h : h + 3], (depth, taps.shape[2]))
        for start in range(0, lanes, 256):
            rhs = jnp.concatenate(
                [stack[:, (2 - a) * 128 + start : (2 - a) * 128 + start + 256] for a in range(3)], 0
            )
            total = jnp.dot(wt[...], rhs, preferred_element_type=F32).astype(BF16)
            for t in range(8):
                parts[t, h, :, start : start + 256] = total[t * width : (t + 1) * width]
        if h % half == half - 1:
            part, first = h // half, h + 1 - half
            for r in range(8):
                source = parts.at[place_ref[r], first : first + half]
                target = outs[r].at[first : first + half] if r < 7 else outs[7 + part]
                copies.append(pltpu.make_async_copy(source, target, sems.at[part, r]))
                copies[-1].start()
    for copy in copies:
        copy.wait()


def pick_kernel(row_ref, from_ref, own_ref, other_ref, out_ref):
    for d in range(out_ref.shape[0]):
        own, other = own_ref[row_ref[d]], other_ref[row_ref[d]]
        chosen = jnp.where(from_ref[d] == 1, own, other)
        out_ref[d] = jnp.where(from_ref[d] == 0, jnp.zeros_like(chosen), chosen)


CHUNK = 2


def start_loads(place_ref, blocks, x, sems):
    rows, width = blocks[0].shape[0], blocks[0].shape[1]
    half = rows // 2
    x[0] = jnp.zeros(x.shape[1:], BF16)
    x[rows + 1] = jnp.zeros(x.shape[1:], BF16)
    lists = []
    for part in range(rows // CHUNK):
        first = part * CHUNK
        copies = []
        for r in range(8):
            channel = pl.ds(pl.multiple_of(place_ref[r] * width, 16), width)
            block, skip = (blocks[r], 0) if r < 7 else (blocks[7 + first // half], first // half * half)
            copies.append(
                pltpu.make_async_copy(
                    block.at[first - skip : first - skip + CHUNK],
                    x.at[first + 1 : first + 1 + CHUNK, channel],
                    sems.at[part, r],
                )
            )
            copies[-1].start()
        lists.append(copies)
    return lists


def wait_for(copies):
    for copy in copies:
        copy.wait()


def forward_kernel(place_ref, after_ref, *rest):
    del after_ref
    blocks, (w_ref, out_ref, carry_ref, x, sems) = rest[:9], rest[9:]
    rows, width, lanes = out_ref.shape
    loads = start_loads(place_ref, blocks, x, sems)
    lhs = jnp.concatenate(
        [jnp.concatenate([w_ref[a * 3 + 2 - b] for a in range(3)], 0) for b in range(3)], 1
    )
    wait_for(loads[0])
    for h in range(rows):
        if (h + 1) % CHUNK == 0 and h + 1 < rows:
            wait_for(loads[(h + 1) // CHUNK])
        stack = jnp.reshape(x[h : h + 3], (3 * x.shape[1], lanes))
        y = jnp.dot(lhs, stack, preferred_element_type=F32)
        sums = []
        for e in range(3):
            frames = []
            for g in range(lanes // 128 + 2):
                terms = []
                for a in range(3):
                    f = g + a - 2
                    if 0 <= f < lanes // 128:
                        row = (a * 3 + e) * width
                        terms.append(y[row : row + width, f * 128 : f * 128 + 128])
                total = terms[0]
                for term in terms[1:]:
                    total = total + term
                frames.append(total)
            sums.append(jnp.concatenate(frames, 1))
        result = sums[1] + shifted(sums[0], 1) + shifted(sums[2], -1)
        out_ref[h] = result[:, :lanes]
        carry_ref[h, :width] = result[:, lanes : lanes + 128].astype(BF16)
        carry_ref[h, width:] = result[:, lanes + 128 :].astype(BF16)


def kernel_grad_kernel(place_ref, live_ref, rep_ref, after_ref, *rest):
    del after_ref
    blocks, (m_ref, head_ref, mine_ref, theirs_ref, x, taps, total, result, sems, out_sems) = rest[:9], rest[9:]
    rows, width, lanes = m_ref.shape
    loads = start_loads(place_ref, blocks, x, sems)
    fill_taps(live_ref, m_ref, head_ref, taps)
    depth = 9 * width
    result[9 * depth :, :] = jnp.zeros((result.shape[0] - 9 * depth, 128), F32)
    for h in range(rows):
        if h % CHUNK == 0:
            wait_for(loads[h // CHUNK])
        stack = jnp.reshape(taps[h : h + 3], (depth, taps.shape[2]))
        right = x[h + 1]
        for a in range(3):
            left = stack[:, (2 - a) * 128 : (2 - a) * 128 + lanes]
            product = lax.dot_general(
                left, right, (((1,), (1,)), ((), ())), preferred_element_type=F32
            )
            if h == 0:
                total[a] = product
            elif h < rows - 1:
                total[a] += product
            else:
                product = total[a] + product
                for block in range(3):
                    row = (a * 3 + block) * depth
                    result[row : row + depth, :] = product[:, block * 128 : block * 128 + 128]
    half = result.shape[0] // 2
    copies = []
    for slot, (target, rep) in enumerate(((theirs_ref, 1 - rep_ref[0]), (mine_ref, rep_ref[0]))):
        source = result.at[pl.ds(pl.multiple_of(rep * half, 16), half)]
        copies.append(pltpu.make_async_copy(source, target, out_sems.at[slot]))
        copies[-1].start()
    wait_for(copies)


def params():
    return pltpu.CompilerParams(vmem_limit_bytes=VMEM_LIMIT)


def cost(flops, size):
    return pl.CostEstimate(flops=flops, bytes_accessed=size, transcendentals=0)


FLOPS = 2 * 27 * 48 * 384 * 4096


def input_partials(place, live, m, head, weight):
    rows, width, lanes = m.shape
    channels = weight.shape[2]
    whole = jax.ShapeDtypeStruct((rows, width, lanes), BF16)
    half = jax.ShapeDtypeStruct((rows // 2, width, lanes), BF16)
    return pl.pallas_call(
        input_grad_kernel,
        out_shape=[whole] * 7 + [half] * 2,
        in_specs=[SMEM, SMEM, VMEM, VMEM, VMEM],
        out_specs=[ANY] * 9,
        scratch_shapes=[
            pltpu.VMEM((rows + 2, 3 * width, lanes + 256), BF16),
            pltpu.VMEM((channels, 27 * width), BF16),
            pltpu.VMEM((8, rows, width, lanes), BF16),
            pltpu.SemaphoreType.DMA((2, 8)),
        ],
        compiler_params=params(),
        cost_estimate=cost(FLOPS, 5_000_000),
        name="input_partials",
    )(place, live, m, head, weight)


def pick(row, origin, own, other):
    return pl.pallas_call(
        pick_kernel,
        out_shape=jax.ShapeDtypeStruct(own.shape, own.dtype),
        in_specs=[SMEM, SMEM, VMEM, VMEM],
        out_specs=VMEM,
        compiler_params=params(),
        name="pick",
    )(row, origin, own, other)


def forward(place, after, blocks, weight):
    rows, width, lanes = blocks[0].shape
    channels = weight.shape[2]
    return pl.pallas_call(
        forward_kernel,
        out_shape=[
            jax.ShapeDtypeStruct((rows, width, lanes), F32),
            jax.ShapeDtypeStruct((rows, 2 * width, 128), BF16),
        ],
        in_specs=[SMEM] + [ANY] * 10 + [VMEM],
        out_specs=[VMEM, VMEM],
        scratch_shapes=[
            pltpu.VMEM((rows + 2, channels, lanes), BF16),
            pltpu.SemaphoreType.DMA((rows // CHUNK, 8)),
        ],
        compiler_params=params(),
        cost_estimate=cost(FLOPS, 5_000_000),
        name="forward",
    )(place, after, *blocks, weight)


def kernel_grad(place, live, rep, after, blocks, m, head):
    rows, width, lanes = m.shape
    channels = 8 * width
    return pl.pallas_call(
        kernel_grad_kernel,
        out_shape=[jax.ShapeDtypeStruct((2048, 128), F32)] * 2,
        in_specs=[SMEM] * 3 + [ANY] * 10 + [VMEM, VMEM],
        out_specs=[ANY, ANY],
        scratch_shapes=[
            pltpu.VMEM((rows + 2, channels, lanes), BF16),
            pltpu.VMEM((rows + 2, 3 * width, lanes + 256), BF16),
            pltpu.VMEM((3, 9 * width, channels), F32),
            pltpu.VMEM((4096, 128), F32),
            pltpu.SemaphoreType.DMA((rows // CHUNK, 8)),
            pltpu.SemaphoreType.DMA((2,)),
        ],
        compiler_params=params(),
        cost_estimate=cost(FLOPS, 6_000_000),
        name="kernel_grad",
    )(place, live, rep, after, *blocks, m, head)


def to_rows(x):
    f, c, h, w = x.shape
    return x.transpose(2, 1, 0, 3).reshape(h, c, f * w)


def from_rows(x):
    h, c, lanes = x.shape
    return x.reshape(h, c, lanes // 128, 128).transpose(2, 1, 0, 3)


def core_swap(x):
    return lax.ppermute(x, "rep", [(0, 1), (1, 0)])


def exchange(x):
    return lax.all_to_all(x, "dp", 0, 0, tiled=True)


def handed_on(own, source):
    rep = lax.axis_index("rep")
    wanted = lax.dynamic_slice_in_dim(source, rep * 8, 8, 0)
    row = jnp.maximum(wanted, 0) % 8
    origin = jnp.where(wanted < 0, 0, jnp.where(wanted // 8 == rep, 1, 2)).astype(jnp.int32)
    return pick(row, origin, own, core_swap(own))


def chip_sum(mine, theirs):
    return (mine + core_swap(theirs)).astype(BF16).reshape(8, 256, 128)


def both_cores(half):
    rep = lax.axis_index("rep")
    there = core_swap(half)
    low = jnp.where(rep == 0, half, there)
    high = jnp.where(rep == 0, there, half)
    return jnp.concatenate([low, high], 0)


def per_device(frames, weight, cotangent, prev_owner, lengths):
    seg_len, width, height, columns = frames.shape
    channels = weight.shape[4]
    rep, me = lax.axis_index("rep"), lax.axis_index("dp")
    member = rep * 8 + me
    tensor = Group("tensor", tensor_index, lambda i: (i // 2, i % 2))
    place = jnp.stack(tensor.absolute()).astype(jnp.int32)
    segments = jnp.arange(prev_owner.shape[0], dtype=jnp.int32)
    follows = prev_owner[None, :] == segments[:, None]
    follower = jnp.max(jnp.where(follows, segments[None, :], -1), 1)

    x = to_rows(frames)
    m = to_rows(cotangent)
    rows = weight.transpose(1, 2, 3, 0, 4)[:, ::-1].reshape(9, 3 * width, channels)

    payload, x = lax.optimization_barrier((m[:, :, :256], x))
    payload = exchange(payload)
    blocks = tensor.gather(x)
    payload, _ = lax.optimization_barrier((payload, (blocks[1], blocks[2])))
    head = exchange(handed_on(payload, follower))
    keep = jnp.arange(seg_len) < lengths[member]
    keep_head = jnp.arange(2) < lengths[jnp.maximum(follower[member], 0)]
    live = jnp.concatenate([keep, keep_head]).astype(jnp.int32)

    partials = input_partials(place, live, m, head, rows)
    mine, theirs = kernel_grad(place, live, rep.astype(jnp.int32)[None], partials[0], blocks, m, head)
    spread = chip_sum(mine, theirs)
    partials, spread = lax.optimization_barrier((partials, spread))
    conv, carry = forward(place, spread, blocks, rows)
    conv = conv.reshape(height, width, seg_len, columns).transpose(2, 1, 0, 3)
    input_grad = from_rows(tensor.scatter_sum(partials))

    cells = prev_owner.shape[0] * seg_len * height * columns
    share = (jnp.sum(exchange(spread).astype(F32), 0) * (1.0 / math.sqrt(cells))).astype(BF16)
    share = jnp.broadcast_to(share[None], spread.shape)
    spread, conv = lax.optimization_barrier((exchange(jnp.concatenate([share, carry], 1)), conv))
    received = exchange(handed_on(spread[:, 256:], prev_owner))
    total = both_cores(spread[:, :256].reshape(2048, 128))
    total = total[: 81 * width].reshape(3, 3, 3, 3, width, 128)
    weight_grad = total[:, :, ::-1].transpose(4, 0, 2, 3, 1, 5).reshape(weight.shape).astype(F32)

    received = received.reshape(height, 2, width, columns).transpose(1, 2, 0, 3).astype(F32)
    conv = conv + jnp.concatenate([received, jnp.zeros_like(received)], 0)
    output = jnp.where(keep[:, None, None, None], conv, 0.0).astype(BF16)
    return (output, input_grad, weight_grad)


def solution(mesh):
    split = P(("rep", "dp"), "tensor", None, None)
    kernel = P("tensor", None, None, None, None)
    return jax.shard_map(
        per_device,
        mesh=mesh,
        in_specs=(split, kernel, split, P(), P()),
        out_specs=(split, split, kernel),
        check_vma=False,
    )
```

```python
import functools
import math

import jax
import jax.numpy as jnp
from jax import lax
from jax.experimental import pallas as pl
from jax.experimental.pallas import tpu as pltpu
from jax.sharding import PartitionSpec as P

BF16 = jnp.bfloat16
F32 = jnp.float32
VMEM_LIMIT = 56 * 1024 * 1024
ANY = pl.BlockSpec(memory_space=pl.ANY)
VMEM = pl.BlockSpec(memory_space=pltpu.VMEM)
SMEM = pl.BlockSpec(memory_space=pltpu.SMEM)

PLACES = ((0, 0), (0, 1), (1, 0), (3, 0), (1, 1), (3, 1), (2, 0), (2, 1))


def tensor_index(ring, pair):
    return ring * 2 + pair


class Group:
    def __init__(self, name, index_of, coords):
        self.name = name
        self.index_of = index_of
        me = lax.axis_index(name)
        self.ring, self.pair = coords(me)
        cells = [(r, p) for r in range(4) for p in range(2)]
        self.perm_up = [(index_of(r, p), index_of((r + 1) % 4, p)) for r, p in cells]
        self.perm_down = [(index_of(r, p), index_of((r + 3) % 4, p)) for r, p in cells]
        self.perm_swap = [(index_of(r, p), index_of(r, 1 - p)) for r, p in cells]

    def up(self, x):
        return lax.ppermute(x, self.name, self.perm_up)

    def down(self, x):
        return lax.ppermute(x, self.name, self.perm_down)

    def swap(self, x):
        return lax.ppermute(x, self.name, self.perm_swap)

    def absolute(self):
        return [self.index_of((self.ring + dr) % 4, self.pair ^ dp) for dr, dp in PLACES]

    def gather(self, x):
        half = x.shape[0] // 2
        following, prev, pair = lax.optimization_barrier((self.down(x), self.up(x), self.swap(x)))
        pair_next = self.swap(following)
        pair_prev = self.up(pair)
        second = self.down(following)
        far_a = self.down(pair_next[:half])
        far_b = self.up(pair_prev[half:])
        return [x, pair, following, prev, pair_next, pair_prev, second, far_a, far_b]

    def begin_sum(self, parts, tie):
        own, pair, following, prev, pair_next, pair_prev, second, far_a, far_b = parts
        in_a, in_b, tie = lax.optimization_barrier((self.up(far_a), self.down(far_b), tie))
        got_up, from_prev = self.up(second), self.down(prev)
        pair_next = added(pair_next, jnp.concatenate([in_a, jnp.zeros_like(in_a)], 0))
        pair_prev = added(pair_prev, jnp.concatenate([jnp.zeros_like(in_b), in_b], 0))
        return (own, pair, following, pair_next, pair_prev), (got_up, from_prev), tie

    def end_sum(self, parts, early, tie):
        parts, tie = lax.optimization_barrier((parts, tie))
        own, pair, following, pair_next, pair_prev = parts
        got_up, from_prev = early
        got_swap = self.swap(pair_next)
        got_down = self.down(pair_prev)
        last_up = self.up(added(following, got_swap, got_up))
        last_swap = self.swap(added(pair, got_down))
        return sum(x.astype(F32) for x in (own, from_prev, last_up, last_swap)), tie


def added(*terms):
    return sum(x.astype(F32) for x in terms).astype(BF16)


def shifted(x, by):
    lanes = x.shape[-1]
    column = lax.broadcasted_iota(jnp.int32, x.shape, x.ndim - 1) % 128
    rolled = pltpu.roll(x, by % lanes, x.ndim - 1)
    edge = 0 if by == 1 else 127
    return jnp.where(column == edge, 0.0, rolled)


def fill_taps(live_ref, m_ref, head_ref, taps):
    rows, width, lanes = m_ref.shape
    frames = taps.shape[2] // 128
    taps[0] = jnp.zeros(taps.shape[1:], BF16)
    taps[rows + 1] = jnp.zeros(taps.shape[1:], BF16)
    for h in range(rows):
        whole = jnp.concatenate([m_ref[h], head_ref[h]], 1).astype(F32)
        wide = jnp.concatenate(
            [
                jnp.where(live_ref[f] > 0, whole[:, f * 128 : f * 128 + 128], 0.0)
                for f in range(frames)
            ],
            1,
        )
        taps[h + 1, 0:width] = shifted(wide, -1).astype(BF16)
        taps[h + 1, width : 2 * width] = wide.astype(BF16)
        taps[h + 1, 2 * width : 3 * width] = shifted(wide, 1).astype(BF16)


def input_grad_kernel(place_ref, live_ref, after_ref, m_ref, head_ref, w_ref, *rest):
    del after_ref
    outs, (taps, wt, parts, sems) = rest[:9], rest[9:]
    rows, width, lanes = m_ref.shape
    half = rows // 2
    fill_taps(live_ref, m_ref, head_ref, taps)
    depth = 3 * 3 * width
    for a in range(3):
        block = jnp.concatenate([w_ref[a * 3 + b] for b in range(3)], 0)
        wt[:, a * depth : (a + 1) * depth] = block.T

    copies = []
    for h in range(rows):
        stack = jnp.reshape(taps[h : h + 3], (depth, taps.shape[2]))
        for start in range(0, lanes, 256):
            rhs = jnp.concatenate(
                [stack[:, (2 - a) * 128 + start : (2 - a) * 128 + start + 256] for a in range(3)], 0
            )
            total = jnp.dot(wt[...], rhs, preferred_element_type=F32).astype(BF16)
            for t in range(8):
                parts[t, h, :, start : start + 256] = total[t * width : (t + 1) * width]
        if h % half == half - 1:
            part, first = h // half, h + 1 - half
            for r in range(8):
                source = parts.at[place_ref[r], first : first + half]
                target = outs[r].at[first : first + half] if r < 7 else outs[7 + part]
                copies.append(pltpu.make_async_copy(source, target, sems.at[part, r]))
                copies[-1].start()
    for copy in copies:
        copy.wait()


def pick_kernel(row_ref, from_ref, own_ref, other_ref, out_ref):
    for d in range(out_ref.shape[0]):
        own, other = own_ref[row_ref[d]], other_ref[row_ref[d]]
        chosen = jnp.where(from_ref[d] == 1, own, other)
        out_ref[d] = jnp.where(from_ref[d] == 0, jnp.zeros_like(chosen), chosen)


def assemble_kernel(scale, row_ref, from_ref, own_ref, other_ref, out_ref):
    count, summed = own_ref.shape[0], own_ref.shape[1] - other_ref.shape[1]
    total = own_ref[0, :summed].astype(F32)
    for d in range(1, count):
        total = total + own_ref[d, :summed].astype(F32)
    share = (total * scale).astype(BF16)
    for d in range(count):
        out_ref[d, :summed] = share
        own, other = own_ref[row_ref[d], summed:], other_ref[row_ref[d]]
        chosen = jnp.where(from_ref[d] == 1, own, other)
        out_ref[d, summed:] = jnp.where(from_ref[d] == 0, jnp.zeros_like(chosen), chosen)


CHUNK = 2


def start_loads(place_ref, blocks, x, sems):
    rows, width = blocks[0].shape[0], blocks[0].shape[1]
    half = rows // 2
    x[0] = jnp.zeros(x.shape[1:], BF16)
    x[rows + 1] = jnp.zeros(x.shape[1:], BF16)
    lists = []
    for part in range(rows // CHUNK):
        first = part * CHUNK
        copies = []
        for r in range(8):
            channel = pl.ds(pl.multiple_of(place_ref[r] * width, 16), width)
            block, skip = (blocks[r], 0) if r < 7 else (blocks[7 + first // half], first // half * half)
            copies.append(
                pltpu.make_async_copy(
                    block.at[first - skip : first - skip + CHUNK],
                    x.at[first + 1 : first + 1 + CHUNK, channel],
                    sems.at[part, r],
                )
            )
            copies[-1].start()
        lists.append(copies)
    return lists


def wait_for(copies):
    for copy in copies:
        copy.wait()


def forward_kernel(place_ref, after_ref, *rest):
    del after_ref
    blocks, (w_ref, out_ref, carry_ref, x, sems) = rest[:9], rest[9:]
    rows, width, lanes = out_ref.shape
    loads = start_loads(place_ref, blocks, x, sems)
    lhs = jnp.concatenate(
        [jnp.concatenate([w_ref[a * 3 + 2 - b] for a in range(3)], 0) for b in range(3)], 1
    )
    wait_for(loads[0])
    for h in range(rows):
        if (h + 1) % CHUNK == 0 and h + 1 < rows:
            wait_for(loads[(h + 1) // CHUNK])
        stack = jnp.reshape(x[h : h + 3], (3 * x.shape[1], lanes))
        y = jnp.dot(lhs, stack, preferred_element_type=F32)
        sums = []
        for e in range(3):
            frames = []
            for g in range(lanes // 128 + 2):
                terms = []
                for a in range(3):
                    f = g + a - 2
                    if 0 <= f < lanes // 128:
                        row = (a * 3 + e) * width
                        terms.append(y[row : row + width, f * 128 : f * 128 + 128])
                total = terms[0]
                for term in terms[1:]:
                    total = total + term
                frames.append(total)
            sums.append(jnp.concatenate(frames, 1))
        result = sums[1] + shifted(sums[0], 1) + shifted(sums[2], -1)
        out_ref[h] = result[:, :lanes]
        carry_ref[h, :width] = result[:, lanes : lanes + 128].astype(BF16)
        carry_ref[h, width:] = result[:, lanes + 128 :].astype(BF16)


def kernel_grad_kernel(place_ref, live_ref, rep_ref, *rest):
    blocks, (m_ref, head_ref, mine_ref, theirs_ref, x, taps, total, result, sems, out_sems) = rest[:9], rest[9:]
    rows, width, lanes = m_ref.shape
    loads = start_loads(place_ref, blocks, x, sems)
    fill_taps(live_ref, m_ref, head_ref, taps)
    depth = 9 * width
    result[9 * depth :, :] = jnp.zeros((result.shape[0] - 9 * depth, 128), F32)
    for h in range(rows):
        if h % CHUNK == 0:
            wait_for(loads[h // CHUNK])
        stack = jnp.reshape(taps[h : h + 3], (depth, taps.shape[2]))
        right = x[h + 1]
        for a in range(3):
            left = stack[:, (2 - a) * 128 : (2 - a) * 128 + lanes]
            product = lax.dot_general(
                left, right, (((1,), (1,)), ((), ())), preferred_element_type=F32
            )
            if h == 0:
                total[a] = product
            elif h < rows - 1:
                total[a] += product
            else:
                product = total[a] + product
                for block in range(3):
                    row = (a * 3 + block) * depth
                    result[row : row + depth, :] = product[:, block * 128 : block * 128 + 128]
    half = result.shape[0] // 2
    copies = []
    for slot, (target, rep) in enumerate(((theirs_ref, 1 - rep_ref[0]), (mine_ref, rep_ref[0]))):
        source = result.at[pl.ds(pl.multiple_of(rep * half, 16), half)]
        copies.append(pltpu.make_async_copy(source, target, out_sems.at[slot]))
        copies[-1].start()
    wait_for(copies)


def params():
    return pltpu.CompilerParams(vmem_limit_bytes=VMEM_LIMIT)


def cost(flops, size):
    return pl.CostEstimate(flops=flops, bytes_accessed=size, transcendentals=0)


FLOPS = 2 * 27 * 48 * 384 * 4096


def input_partials(place, live, after, m, head, weight):
    rows, width, lanes = m.shape
    channels = weight.shape[2]
    whole = jax.ShapeDtypeStruct((rows, width, lanes), BF16)
    half = jax.ShapeDtypeStruct((rows // 2, width, lanes), BF16)
    return pl.pallas_call(
        input_grad_kernel,
        out_shape=[whole] * 7 + [half] * 2,
        in_specs=[SMEM, SMEM, ANY, VMEM, VMEM, VMEM],
        out_specs=[ANY] * 9,
        scratch_shapes=[
            pltpu.VMEM((rows + 2, 3 * width, lanes + 256), BF16),
            pltpu.VMEM((channels, 27 * width), BF16),
            pltpu.VMEM((8, rows, width, lanes), BF16),
            pltpu.SemaphoreType.DMA((2, 8)),
        ],
        compiler_params=params(),
        cost_estimate=cost(FLOPS, 5_000_000),
        name="input_partials",
    )(place, live, after, m, head, weight)


def pick(row, origin, own, other):
    return pl.pallas_call(
        pick_kernel,
        out_shape=jax.ShapeDtypeStruct(own.shape, own.dtype),
        in_specs=[SMEM, SMEM, VMEM, VMEM],
        out_specs=VMEM,
        compiler_params=params(),
        name="pick",
    )(row, origin, own, other)


def assemble(scale, row, origin, own, other):
    return pl.pallas_call(
        functools.partial(assemble_kernel, scale),
        out_shape=jax.ShapeDtypeStruct(own.shape, own.dtype),
        in_specs=[SMEM, SMEM, VMEM, VMEM],
        out_specs=VMEM,
        compiler_params=params(),
        name="assemble",
    )(row, origin, own, other)


def forward(place, after, blocks, weight):
    rows, width, lanes = blocks[0].shape
    channels = weight.shape[2]
    return pl.pallas_call(
        forward_kernel,
        out_shape=[
            jax.ShapeDtypeStruct((rows, width, lanes), F32),
            jax.ShapeDtypeStruct((rows, 2 * width, 128), BF16),
        ],
        in_specs=[SMEM] + [ANY] * 10 + [VMEM],
        out_specs=[VMEM, VMEM],
        scratch_shapes=[
            pltpu.VMEM((rows + 2, channels, lanes), BF16),
            pltpu.SemaphoreType.DMA((rows // CHUNK, 8)),
        ],
        compiler_params=params(),
        cost_estimate=cost(FLOPS, 5_000_000),
        name="forward",
    )(place, after, *blocks, weight)


def kernel_grad(place, live, rep, blocks, m, head):
    rows, width, lanes = m.shape
    channels = 8 * width
    return pl.pallas_call(
        kernel_grad_kernel,
        out_shape=[jax.ShapeDtypeStruct((2048, 128), F32)] * 2,
        in_specs=[SMEM] * 3 + [ANY] * 9 + [VMEM, VMEM],
        out_specs=[ANY, ANY],
        scratch_shapes=[
            pltpu.VMEM((rows + 2, channels, lanes), BF16),
            pltpu.VMEM((rows + 2, 3 * width, lanes + 256), BF16),
            pltpu.VMEM((3, 9 * width, channels), F32),
            pltpu.VMEM((4096, 128), F32),
            pltpu.SemaphoreType.DMA((rows // CHUNK, 8)),
            pltpu.SemaphoreType.DMA((2,)),
        ],
        compiler_params=params(),
        cost_estimate=cost(FLOPS, 6_000_000),
        name="kernel_grad",
    )(place, live, rep, *blocks, m, head)


def to_rows(x):
    f, c, h, w = x.shape
    return x.transpose(2, 1, 0, 3).reshape(h, c, f * w)


def from_rows(x):
    h, c, lanes = x.shape
    return x.reshape(h, c, lanes // 128, 128).transpose(2, 1, 0, 3)


def core_swap(x):
    return lax.ppermute(x, "rep", [(0, 1), (1, 0)])


def exchange(x):
    return lax.all_to_all(x, "dp", 0, 0, tiled=True)


def asked_for(source):
    rep = lax.axis_index("rep")
    wanted = lax.dynamic_slice_in_dim(source, rep * 8, 8, 0)
    row = jnp.maximum(wanted, 0) % 8
    origin = jnp.where(wanted < 0, 0, jnp.where(wanted // 8 == rep, 1, 2)).astype(jnp.int32)
    return row, origin


def handed_on(own, source):
    row, origin = asked_for(source)
    return pick(row, origin, own, core_swap(own))


def first_exchange(mine, theirs, payload):
    pair = (mine + core_swap(theirs)).astype(BF16).reshape(8, 256, 128)
    return jnp.concatenate([pair, payload], 1)


def both_cores(half):
    rep = lax.axis_index("rep")
    there = core_swap(half)
    low = jnp.where(rep == 0, half, there)
    high = jnp.where(rep == 0, there, half)
    return jnp.concatenate([low, high], 0)


def per_device(frames, weight, cotangent, prev_owner, lengths):
    seg_len, width, height, columns = frames.shape
    channels = weight.shape[4]
    rep, me = lax.axis_index("rep"), lax.axis_index("dp")
    member = rep * 8 + me
    tensor = Group("tensor", tensor_index, lambda i: (i // 2, i % 2))
    place = jnp.stack(tensor.absolute()).astype(jnp.int32)
    segments = jnp.arange(prev_owner.shape[0], dtype=jnp.int32)
    follows = prev_owner[None, :] == segments[:, None]
    follower = jnp.max(jnp.where(follows, segments[None, :], -1), 1)

    x = to_rows(frames)
    m = to_rows(cotangent)
    rows = weight.transpose(1, 2, 3, 0, 4)[:, ::-1].reshape(9, 3 * width, channels)

    payload, x = lax.optimization_barrier((m[:, :, :256], x))
    payload = exchange(payload)
    blocks = tensor.gather(x)
    payload, _ = lax.optimization_barrier((payload, (blocks[1], blocks[2])))
    head = exchange(handed_on(payload, follower))
    keep = jnp.arange(seg_len) < lengths[member]
    keep_head = jnp.arange(2) < lengths[jnp.maximum(follower[member], 0)]
    live = jnp.concatenate([keep, keep_head]).astype(jnp.int32)

    mine, theirs = kernel_grad(place, live, rep.astype(jnp.int32)[None], blocks, m, head)
    conv, carry = forward(place, theirs, blocks, rows)
    spread = first_exchange(mine, theirs, carry)
    partials = input_partials(place, live, spread, m, head, rows)
    conv = conv.reshape(height, width, seg_len, columns).transpose(2, 1, 0, 3)
    partials, early, spread = tensor.begin_sum(partials, exchange(spread))
    spread, conv = lax.optimization_barrier((spread, conv))

    cells = prev_owner.shape[0] * seg_len * height * columns
    row, origin = asked_for(prev_owner)
    spread = assemble(1.0 / math.sqrt(cells), row, origin, spread, core_swap(spread[:, 256:]))
    input_grad, spread = tensor.end_sum(partials, early, spread)
    input_grad = from_rows(input_grad)
    spread = exchange(spread)
    received = spread[:, 256:]
    total = both_cores(spread[:, :256].reshape(2048, 128))
    total = total[: 81 * width].reshape(3, 3, 3, 3, width, 128)
    weight_grad = total[:, :, ::-1].transpose(4, 0, 2, 3, 1, 5).reshape(weight.shape).astype(F32)

    received = received.reshape(height, 2, width, columns).transpose(1, 2, 0, 3).astype(F32)
    conv = conv + jnp.concatenate([received, jnp.zeros_like(received)], 0)
    output = jnp.where(keep[:, None, None, None], conv, 0.0).astype(BF16)
    return (output, input_grad, weight_grad)


def solution(mesh):
    split = P(("rep", "dp"), "tensor", None, None)
    kernel = P("tensor", None, None, None, None)
    return jax.shard_map(
        per_device,
        mesh=mesh,
        in_specs=(split, kernel, split, P(), P()),
        out_specs=(split, split, kernel),
        check_vma=False,
    )
```

```python
import functools
import math

import jax
import jax.numpy as jnp
from jax import lax
from jax.experimental import pallas as pl
from jax.experimental.pallas import tpu as pltpu
from jax.sharding import PartitionSpec as P

BF16 = jnp.bfloat16
F32 = jnp.float32
VMEM_LIMIT = 56 * 1024 * 1024
ANY = pl.BlockSpec(memory_space=pl.ANY)
VMEM = pl.BlockSpec(memory_space=pltpu.VMEM)
SMEM = pl.BlockSpec(memory_space=pltpu.SMEM)

PLACES = ((0, 0), (0, 1), (1, 0), (3, 0), (1, 1), (3, 1), (2, 0), (2, 1))


def tensor_index(ring, pair):
    return ring * 2 + pair


class Group:
    def __init__(self, name, index_of, coords):
        self.name = name
        self.index_of = index_of
        me = lax.axis_index(name)
        self.ring, self.pair = coords(me)
        cells = [(r, p) for r in range(4) for p in range(2)]
        self.perm_up = [(index_of(r, p), index_of((r + 1) % 4, p)) for r, p in cells]
        self.perm_down = [(index_of(r, p), index_of((r + 3) % 4, p)) for r, p in cells]
        self.perm_swap = [(index_of(r, p), index_of(r, 1 - p)) for r, p in cells]

    def up(self, x):
        return lax.ppermute(x, self.name, self.perm_up)

    def down(self, x):
        return lax.ppermute(x, self.name, self.perm_down)

    def swap(self, x):
        return lax.ppermute(x, self.name, self.perm_swap)

    def absolute(self):
        return [self.index_of((self.ring + dr) % 4, self.pair ^ dp) for dr, dp in PLACES]

    def gather(self, x):
        half = x.shape[0] // 2
        following, prev, pair = lax.optimization_barrier((self.down(x), self.up(x), self.swap(x)))
        pair_next = self.swap(following)
        pair_prev = self.up(pair)
        second = self.down(following)
        far_a = self.down(pair_next[:half])
        far_b = self.up(pair_prev[half:])
        return [x, pair, following, prev, pair_next, pair_prev, second, far_a, far_b]

    def begin_sum(self, parts):
        far_a, far_b = parts[7:]
        return self.up(far_a), self.down(far_b)

    def end_sum(self, parts, arrived):
        own, pair, following, prev, pair_next, pair_prev, second = parts[:7]
        in_a, in_b = arrived
        got_swap = self.swap(added(pair_next, jnp.concatenate([in_a, jnp.zeros_like(in_a)], 0)))
        got_down = self.down(added(pair_prev, jnp.concatenate([jnp.zeros_like(in_b), in_b], 0)))
        got_up, from_prev = self.up(second), self.down(prev)
        last_up = self.up(added(following, got_swap, got_up))
        last_swap = self.swap(added(pair, got_down))
        return sum(x.astype(F32) for x in (own, from_prev, last_up, last_swap))


def added(*terms):
    return sum(x.astype(F32) for x in terms).astype(BF16)


def shifted(x, by):
    lanes = x.shape[-1]
    column = lax.broadcasted_iota(jnp.int32, x.shape, x.ndim - 1) % 128
    rolled = pltpu.roll(x, by % lanes, x.ndim - 1)
    edge = 0 if by == 1 else 127
    return jnp.where(column == edge, 0.0, rolled)


def fill_taps(live_ref, m_ref, head_ref, taps):
    rows, width, lanes = m_ref.shape
    frames = taps.shape[2] // 128
    taps[0] = jnp.zeros(taps.shape[1:], BF16)
    taps[rows + 1] = jnp.zeros(taps.shape[1:], BF16)
    for h in range(rows):
        whole = jnp.concatenate([m_ref[h], head_ref[h]], 1).astype(F32)
        wide = jnp.concatenate(
            [
                jnp.where(live_ref[f] > 0, whole[:, f * 128 : f * 128 + 128], 0.0)
                for f in range(frames)
            ],
            1,
        )
        taps[h + 1, 0:width] = shifted(wide, -1).astype(BF16)
        taps[h + 1, width : 2 * width] = wide.astype(BF16)
        taps[h + 1, 2 * width : 3 * width] = shifted(wide, 1).astype(BF16)


def input_grad_kernel(place_ref, live_ref, m_ref, head_ref, w_ref, *rest):
    outs, (taps, wt, parts, sems) = rest[:9], rest[9:]
    rows, width, lanes = m_ref.shape
    half = rows // 2
    fill_taps(live_ref, m_ref, head_ref, taps)
    depth = 3 * 3 * width
    for a in range(3):
        block = jnp.concatenate([w_ref[a * 3 + b] for b in range(3)], 0)
        wt[:, a * depth : (a + 1) * depth] = block.T

    copies = []
    for h in range(rows):
        stack = jnp.reshape(taps[h : h + 3], (depth, taps.shape[2]))
        for start in range(0, lanes, 256):
            rhs = jnp.concatenate(
                [stack[:, (2 - a) * 128 + start : (2 - a) * 128 + start + 256] for a in range(3)], 0
            )
            total = jnp.dot(wt[...], rhs, preferred_element_type=F32).astype(BF16)
            for t in range(8):
                parts[t, h, :, start : start + 256] = total[t * width : (t + 1) * width]
        if h % half == half - 1:
            part, first = h // half, h + 1 - half
            for r in range(8):
                source = parts.at[place_ref[r], first : first + half]
                target = outs[r].at[first : first + half] if r < 7 else outs[7 + part]
                copies.append(pltpu.make_async_copy(source, target, sems.at[part, r]))
                copies[-1].start()
    for copy in copies:
        copy.wait()


def pick_kernel(row_ref, from_ref, own_ref, other_ref, out_ref):
    for d in range(out_ref.shape[0]):
        own, other = own_ref[row_ref[d]], other_ref[row_ref[d]]
        chosen = jnp.where(from_ref[d] == 1, own, other)
        out_ref[d] = jnp.where(from_ref[d] == 0, jnp.zeros_like(chosen), chosen)


def assemble_kernel(scale, row_ref, from_ref, own_ref, other_ref, out_ref):
    count, summed = own_ref.shape[0], own_ref.shape[1] - other_ref.shape[1]
    total = own_ref[0, :summed].astype(F32)
    for d in range(1, count):
        total = total + own_ref[d, :summed].astype(F32)
    share = (total * scale).astype(BF16)
    for d in range(count):
        out_ref[d, :summed] = share
        own, other = own_ref[row_ref[d], summed:], other_ref[row_ref[d]]
        chosen = jnp.where(from_ref[d] == 1, own, other)
        out_ref[d, summed:] = jnp.where(from_ref[d] == 0, jnp.zeros_like(chosen), chosen)


CHUNK = 2


def start_loads(place_ref, blocks, x, sems):
    rows, width = blocks[0].shape[0], blocks[0].shape[1]
    half = rows // 2
    x[0] = jnp.zeros(x.shape[1:], BF16)
    x[rows + 1] = jnp.zeros(x.shape[1:], BF16)
    lists = []
    for part in range(rows // CHUNK):
        first = part * CHUNK
        copies = []
        for r in range(8):
            channel = pl.ds(pl.multiple_of(place_ref[r] * width, 16), width)
            block, skip = (blocks[r], 0) if r < 7 else (blocks[7 + first // half], first // half * half)
            copies.append(
                pltpu.make_async_copy(
                    block.at[first - skip : first - skip + CHUNK],
                    x.at[first + 1 : first + 1 + CHUNK, channel],
                    sems.at[part, r],
                )
            )
            copies[-1].start()
        lists.append(copies)
    return lists


def wait_for(copies):
    for copy in copies:
        copy.wait()


def forward_kernel(place_ref, after_ref, *rest):
    del after_ref
    blocks, (w_ref, out_ref, carry_ref, x, sems) = rest[:9], rest[9:]
    rows, width, lanes = out_ref.shape
    loads = start_loads(place_ref, blocks, x, sems)
    lhs = jnp.concatenate(
        [jnp.concatenate([w_ref[a * 3 + 2 - b] for a in range(3)], 0) for b in range(3)], 1
    )
    wait_for(loads[0])
    for h in range(rows):
        if (h + 1) % CHUNK == 0 and h + 1 < rows:
            wait_for(loads[(h + 1) // CHUNK])
        stack = jnp.reshape(x[h : h + 3], (3 * x.shape[1], lanes))
        y = jnp.dot(lhs, stack, preferred_element_type=F32)
        sums = []
        for e in range(3):
            frames = []
            for g in range(lanes // 128 + 2):
                terms = []
                for a in range(3):
                    f = g + a - 2
                    if 0 <= f < lanes // 128:
                        row = (a * 3 + e) * width
                        terms.append(y[row : row + width, f * 128 : f * 128 + 128])
                total = terms[0]
                for term in terms[1:]:
                    total = total + term
                frames.append(total)
            sums.append(jnp.concatenate(frames, 1))
        result = sums[1] + shifted(sums[0], 1) + shifted(sums[2], -1)
        out_ref[h] = result[:, :lanes]
        carry_ref[h, :width] = result[:, lanes : lanes + 128].astype(BF16)
        carry_ref[h, width:] = result[:, lanes + 128 :].astype(BF16)


def kernel_grad_kernel(place_ref, live_ref, rep_ref, after_ref, *rest):
    del after_ref
    blocks, (m_ref, head_ref, mine_ref, theirs_ref, x, taps, total, result, sems, out_sems) = rest[:9], rest[9:]
    rows, width, lanes = m_ref.shape
    loads = start_loads(place_ref, blocks, x, sems)
    fill_taps(live_ref, m_ref, head_ref, taps)
    depth = 9 * width
    result[9 * depth :, :] = jnp.zeros((result.shape[0] - 9 * depth, 128), F32)
    for h in range(rows):
        if h % CHUNK == 0:
            wait_for(loads[h // CHUNK])
        stack = jnp.reshape(taps[h : h + 3], (depth, taps.shape[2]))
        right = x[h + 1]
        for a in range(3):
            left = stack[:, (2 - a) * 128 : (2 - a) * 128 + lanes]
            product = lax.dot_general(
                left, right, (((1,), (1,)), ((), ())), preferred_element_type=F32
            )
            if h == 0:
                total[a] = product
            elif h < rows - 1:
                total[a] += product
            else:
                product = total[a] + product
                for block in range(3):
                    row = (a * 3 + block) * depth
                    result[row : row + depth, :] = product[:, block * 128 : block * 128 + 128]
    half = result.shape[0] // 2
    copies = []
    for slot, (target, rep) in enumerate(((theirs_ref, 1 - rep_ref[0]), (mine_ref, rep_ref[0]))):
        source = result.at[pl.ds(pl.multiple_of(rep * half, 16), half)]
        copies.append(pltpu.make_async_copy(source, target, out_sems.at[slot]))
        copies[-1].start()
    wait_for(copies)


def params():
    return pltpu.CompilerParams(vmem_limit_bytes=VMEM_LIMIT)


def cost(flops, size):
    return pl.CostEstimate(flops=flops, bytes_accessed=size, transcendentals=0)


FLOPS = 2 * 27 * 48 * 384 * 4096


def input_partials(place, live, m, head, weight):
    rows, width, lanes = m.shape
    channels = weight.shape[2]
    whole = jax.ShapeDtypeStruct((rows, width, lanes), BF16)
    half = jax.ShapeDtypeStruct((rows // 2, width, lanes), BF16)
    return pl.pallas_call(
        input_grad_kernel,
        out_shape=[whole] * 7 + [half] * 2,
        in_specs=[SMEM, SMEM, VMEM, VMEM, VMEM],
        out_specs=[ANY] * 9,
        scratch_shapes=[
            pltpu.VMEM((rows + 2, 3 * width, lanes + 256), BF16),
            pltpu.VMEM((channels, 27 * width), BF16),
            pltpu.VMEM((8, rows, width, lanes), BF16),
            pltpu.SemaphoreType.DMA((2, 8)),
        ],
        compiler_params=params(),
        cost_estimate=cost(FLOPS, 5_000_000),
        name="input_partials",
    )(place, live, m, head, weight)


def pick(row, origin, own, other):
    return pl.pallas_call(
        pick_kernel,
        out_shape=jax.ShapeDtypeStruct(own.shape, own.dtype),
        in_specs=[SMEM, SMEM, VMEM, VMEM],
        out_specs=VMEM,
        compiler_params=params(),
        name="pick",
    )(row, origin, own, other)


def assemble(scale, row, origin, own, other):
    return pl.pallas_call(
        functools.partial(assemble_kernel, scale),
        out_shape=jax.ShapeDtypeStruct(own.shape, own.dtype),
        in_specs=[SMEM, SMEM, VMEM, VMEM],
        out_specs=VMEM,
        compiler_params=params(),
        name="assemble",
    )(row, origin, own, other)


def forward(place, after, blocks, weight):
    rows, width, lanes = blocks[0].shape
    channels = weight.shape[2]
    return pl.pallas_call(
        forward_kernel,
        out_shape=[
            jax.ShapeDtypeStruct((rows, width, lanes), F32),
            jax.ShapeDtypeStruct((rows, 2 * width, 128), BF16),
        ],
        in_specs=[SMEM] + [ANY] * 10 + [VMEM],
        out_specs=[VMEM, VMEM],
        scratch_shapes=[
            pltpu.VMEM((rows + 2, channels, lanes), BF16),
            pltpu.SemaphoreType.DMA((rows // CHUNK, 8)),
        ],
        compiler_params=params(),
        cost_estimate=cost(FLOPS, 5_000_000),
        name="forward",
    )(place, after, *blocks, weight)


def kernel_grad(place, live, rep, after, blocks, m, head):
    rows, width, lanes = m.shape
    channels = 8 * width
    return pl.pallas_call(
        kernel_grad_kernel,
        out_shape=[jax.ShapeDtypeStruct((2048, 128), F32)] * 2,
        in_specs=[SMEM] * 3 + [ANY] * 10 + [VMEM, VMEM],
        out_specs=[ANY, ANY],
        scratch_shapes=[
            pltpu.VMEM((rows + 2, channels, lanes), BF16),
            pltpu.VMEM((rows + 2, 3 * width, lanes + 256), BF16),
            pltpu.VMEM((3, 9 * width, channels), F32),
            pltpu.VMEM((4096, 128), F32),
            pltpu.SemaphoreType.DMA((rows // CHUNK, 8)),
            pltpu.SemaphoreType.DMA((2,)),
        ],
        compiler_params=params(),
        cost_estimate=cost(FLOPS, 6_000_000),
        name="kernel_grad",
    )(place, live, rep, after, *blocks, m, head)


def to_rows(x):
    f, c, h, w = x.shape
    return x.transpose(2, 1, 0, 3).reshape(h, c, f * w)


def from_rows(x):
    h, c, lanes = x.shape
    return x.reshape(h, c, lanes // 128, 128).transpose(2, 1, 0, 3)


def core_swap(x):
    return lax.ppermute(x, "rep", [(0, 1), (1, 0)])


def exchange(x):
    return lax.all_to_all(x, "dp", 0, 0, tiled=True)


def asked_for(source):
    rep = lax.axis_index("rep")
    wanted = lax.dynamic_slice_in_dim(source, rep * 8, 8, 0)
    row = jnp.maximum(wanted, 0) % 8
    origin = jnp.where(wanted < 0, 0, jnp.where(wanted // 8 == rep, 1, 2)).astype(jnp.int32)
    return row, origin


def handed_on(own, source):
    row, origin = asked_for(source)
    return pick(row, origin, own, core_swap(own))


def first_exchange(mine, theirs, payload):
    pair = (mine + core_swap(theirs)).astype(BF16).reshape(8, 256, 128)
    return jnp.concatenate([pair, payload], 1)


def both_cores(half):
    rep = lax.axis_index("rep")
    there = core_swap(half)
    low = jnp.where(rep == 0, half, there)
    high = jnp.where(rep == 0, there, half)
    return jnp.concatenate([low, high], 0)


def per_device(frames, weight, cotangent, prev_owner, lengths):
    seg_len, width, height, columns = frames.shape
    channels = weight.shape[4]
    rep, me = lax.axis_index("rep"), lax.axis_index("dp")
    member = rep * 8 + me
    tensor = Group("tensor", tensor_index, lambda i: (i // 2, i % 2))
    place = jnp.stack(tensor.absolute()).astype(jnp.int32)
    segments = jnp.arange(prev_owner.shape[0], dtype=jnp.int32)
    follows = prev_owner[None, :] == segments[:, None]
    follower = jnp.max(jnp.where(follows, segments[None, :], -1), 1)

    x = to_rows(frames)
    m = to_rows(cotangent)
    rows = weight.transpose(1, 2, 3, 0, 4)[:, ::-1].reshape(9, 3 * width, channels)

    payload, x = lax.optimization_barrier((m[:, :, :256], x))
    payload = exchange(payload)
    blocks = tensor.gather(x)
    payload, _ = lax.optimization_barrier((payload, (blocks[1], blocks[2])))
    head = exchange(handed_on(payload, follower))
    keep = jnp.arange(seg_len) < lengths[member]
    keep_head = jnp.arange(2) < lengths[jnp.maximum(follower[member], 0)]
    live = jnp.concatenate([keep, keep_head]).astype(jnp.int32)

    partials = input_partials(place, live, m, head, rows)
    partials, blocks = lax.optimization_barrier((partials, blocks))
    arrived = tensor.begin_sum(partials)
    mine, theirs = kernel_grad(place, live, rep.astype(jnp.int32)[None], partials[0], blocks, m, head)
    conv, carry = forward(place, theirs, blocks, rows)
    spread = first_exchange(mine, theirs, carry)
    arrived, spread = lax.optimization_barrier((arrived, spread))
    input_grad = from_rows(tensor.end_sum(partials, arrived))
    conv = conv.reshape(height, width, seg_len, columns).transpose(2, 1, 0, 3)
    spread, conv = lax.optimization_barrier((exchange(spread), conv))

    cells = prev_owner.shape[0] * seg_len * height * columns
    row, origin = asked_for(prev_owner)
    spread = exchange(
        assemble(1.0 / math.sqrt(cells), row, origin, spread, core_swap(spread[:, 256:]))
    )
    received = spread[:, 256:]
    total = both_cores(spread[:, :256].reshape(2048, 128))
    total = total[: 81 * width].reshape(3, 3, 3, 3, width, 128)
    weight_grad = total[:, :, ::-1].transpose(4, 0, 2, 3, 1, 5).reshape(weight.shape).astype(F32)

    received = received.reshape(height, 2, width, columns).transpose(1, 2, 0, 3).astype(F32)
    conv = conv + jnp.concatenate([received, jnp.zeros_like(received)], 0)
    output = jnp.where(keep[:, None, None, None], conv, 0.0).astype(BF16)
    return (output, input_grad, weight_grad)


def solution(mesh):
    split = P(("rep", "dp"), "tensor", None, None)
    kernel = P("tensor", None, None, None, None)
    return jax.shard_map(
        per_device,
        mesh=mesh,
        in_specs=(split, kernel, split, P(), P()),
        out_specs=(split, split, kernel),
        check_vma=False,
    )
```

```python
import functools
import math

import jax
import jax.numpy as jnp
from jax import lax
from jax.experimental import pallas as pl
from jax.experimental.pallas import tpu as pltpu
from jax.sharding import PartitionSpec as P

BF16 = jnp.bfloat16
F32 = jnp.float32
MIB = 1024 * 1024
ANY = pl.BlockSpec(memory_space=pl.ANY)
VMEM = pl.BlockSpec(memory_space=pltpu.VMEM)
SMEM = pl.BlockSpec(memory_space=pltpu.SMEM)

PLACES = ((0, 0), (0, 1), (1, 0), (3, 0), (1, 1), (3, 1), (2, 0), (2, 1))


def tensor_index(ring, pair):
    return ring * 2 + pair


class Group:
    def __init__(self, name, index_of, coords):
        self.name = name
        self.index_of = index_of
        me = lax.axis_index(name)
        self.ring, self.pair = coords(me)
        cells = [(r, p) for r in range(4) for p in range(2)]
        self.perm_up = [(index_of(r, p), index_of((r + 1) % 4, p)) for r, p in cells]
        self.perm_down = [(index_of(r, p), index_of((r + 3) % 4, p)) for r, p in cells]
        self.perm_swap = [(index_of(r, p), index_of(r, 1 - p)) for r, p in cells]

    def up(self, x):
        return lax.ppermute(x, self.name, self.perm_up)

    def down(self, x):
        return lax.ppermute(x, self.name, self.perm_down)

    def swap(self, x):
        return lax.ppermute(x, self.name, self.perm_swap)

    def absolute(self):
        return [self.index_of((self.ring + dr) % 4, self.pair ^ dp) for dr, dp in PLACES]

    def gather(self, x):
        half = x.shape[0] // 2
        following, prev, pair = lax.optimization_barrier((self.down(x), self.up(x), self.swap(x)))
        pair_next = self.swap(following)
        pair_prev = self.up(pair)
        second = self.down(following)
        far_a = self.down(pair_next[:half])
        far_b = self.up(pair_prev[half:])
        return [x, pair, following, prev, pair_next, pair_prev, second, far_a, far_b]

    def begin_sum(self, parts):
        far_a, far_b = parts[7:]
        return self.up(far_a), self.down(far_b)

    def end_sum(self, parts, arrived):
        own, pair, following, prev, pair_next, pair_prev, second = parts[:7]
        in_a, in_b = arrived
        got_swap = self.swap(added(pair_next, jnp.concatenate([in_a, jnp.zeros_like(in_a)], 0)))
        got_down = self.down(added(pair_prev, jnp.concatenate([jnp.zeros_like(in_b), in_b], 0)))
        got_up, from_prev = self.up(second), self.down(prev)
        last_up = self.up(added(following, got_swap, got_up))
        last_swap = self.swap(added(pair, got_down))
        return sum(x.astype(F32) for x in (own, from_prev, last_up, last_swap))


def added(*terms):
    return sum(x.astype(F32) for x in terms).astype(BF16)


def shifted(x, by):
    lanes = x.shape[-1]
    column = lax.broadcasted_iota(jnp.int32, x.shape, x.ndim - 1) % 128
    rolled = pltpu.roll(x, by % lanes, x.ndim - 1)
    edge = 0 if by == 1 else 127
    return jnp.where(column == edge, 0.0, rolled)


def fill_taps(live_ref, m_ref, head_ref, taps):
    rows, width, lanes = m_ref.shape
    frames = taps.shape[2] // 128
    taps[0] = jnp.zeros(taps.shape[1:], BF16)
    taps[rows + 1] = jnp.zeros(taps.shape[1:], BF16)
    for h in range(rows):
        whole = jnp.concatenate([m_ref[h], head_ref[h]], 1).astype(F32)
        wide = jnp.concatenate(
            [
                jnp.where(live_ref[f] > 0, whole[:, f * 128 : f * 128 + 128], 0.0)
                for f in range(frames)
            ],
            1,
        )
        taps[h + 1, 0:width] = shifted(wide, -1).astype(BF16)
        taps[h + 1, width : 2 * width] = wide.astype(BF16)
        taps[h + 1, 2 * width : 3 * width] = shifted(wide, 1).astype(BF16)


def input_grad_kernel(place_ref, live_ref, m_ref, head_ref, w_ref, *rest):
    outs, (taps, wt, parts, sems) = rest[:9], rest[9:]
    rows, width, lanes = m_ref.shape
    half = rows // 2
    fill_taps(live_ref, m_ref, head_ref, taps)
    depth = 3 * 3 * width
    for a in range(3):
        block = jnp.concatenate([w_ref[a * 3 + b] for b in range(3)], 0)
        wt[:, a * depth : (a + 1) * depth] = block.T

    copies = []
    for h in range(rows):
        stack = jnp.reshape(taps[h : h + 3], (depth, taps.shape[2]))
        for start in range(0, lanes, 256):
            rhs = jnp.concatenate(
                [stack[:, (2 - a) * 128 + start : (2 - a) * 128 + start + 256] for a in range(3)], 0
            )
            total = jnp.dot(wt[...], rhs, preferred_element_type=F32).astype(BF16)
            for t in range(8):
                parts[t, h, :, start : start + 256] = total[t * width : (t + 1) * width]
        if h % half == half - 1:
            part, first = h // half, h + 1 - half
            for r in range(8):
                source = parts.at[place_ref[r], first : first + half]
                target = outs[r].at[first : first + half] if r < 7 else outs[7 + part]
                copies.append(pltpu.make_async_copy(source, target, sems.at[part, r]))
                copies[-1].start()
    for copy in copies:
        copy.wait()


def pick_kernel(row_ref, from_ref, own_ref, other_ref, out_ref):
    for d in range(out_ref.shape[0]):
        own, other = own_ref[row_ref[d]], other_ref[row_ref[d]]
        chosen = jnp.where(from_ref[d] == 1, own, other)
        out_ref[d] = jnp.where(from_ref[d] == 0, jnp.zeros_like(chosen), chosen)


def assemble_kernel(scale, row_ref, from_ref, own_ref, other_ref, out_ref):
    count, summed = own_ref.shape[0], own_ref.shape[1] - other_ref.shape[1]
    total = own_ref[0, :summed].astype(F32)
    for d in range(1, count):
        total = total + own_ref[d, :summed].astype(F32)
    share = (total * scale).astype(BF16)
    for d in range(count):
        out_ref[d, :summed] = share
        own, other = own_ref[row_ref[d], summed:], other_ref[row_ref[d]]
        chosen = jnp.where(from_ref[d] == 1, own, other)
        out_ref[d, summed:] = jnp.where(from_ref[d] == 0, jnp.zeros_like(chosen), chosen)


CHUNK = 2


def start_loads(place_ref, blocks, x, sems):
    rows, width = blocks[0].shape[0], blocks[0].shape[1]
    half = rows // 2
    x[0] = jnp.zeros(x.shape[1:], BF16)
    x[rows + 1] = jnp.zeros(x.shape[1:], BF16)
    lists = []
    for part in range(rows // CHUNK):
        first = part * CHUNK
        copies = []
        for r in range(8):
            channel = pl.ds(pl.multiple_of(place_ref[r] * width, 16), width)
            block, skip = (blocks[r], 0) if r < 7 else (blocks[7 + first // half], first // half * half)
            copies.append(
                pltpu.make_async_copy(
                    block.at[first - skip : first - skip + CHUNK],
                    x.at[first + 1 : first + 1 + CHUNK, channel],
                    sems.at[part, r],
                )
            )
            copies[-1].start()
        lists.append(copies)
    return lists


def wait_for(copies):
    for copy in copies:
        copy.wait()


def forward_kernel(place_ref, after_ref, *rest):
    del after_ref
    blocks, (w_ref, out_ref, carry_ref, x, sems) = rest[:9], rest[9:]
    rows, width, lanes = out_ref.shape
    loads = start_loads(place_ref, blocks, x, sems)
    lhs = jnp.concatenate(
        [jnp.concatenate([w_ref[a * 3 + 2 - b] for a in range(3)], 0) for b in range(3)], 1
    )
    wait_for(loads[0])
    for h in range(rows):
        if (h + 1) % CHUNK == 0 and h + 1 < rows:
            wait_for(loads[(h + 1) // CHUNK])
        stack = jnp.reshape(x[h : h + 3], (3 * x.shape[1], lanes))
        y = jnp.dot(lhs, stack, preferred_element_type=F32)
        sums = []
        for e in range(3):
            frames = []
            for g in range(lanes // 128 + 2):
                terms = []
                for a in range(3):
                    f = g + a - 2
                    if 0 <= f < lanes // 128:
                        row = (a * 3 + e) * width
                        terms.append(y[row : row + width, f * 128 : f * 128 + 128])
                total = terms[0]
                for term in terms[1:]:
                    total = total + term
                frames.append(total)
            sums.append(jnp.concatenate(frames, 1))
        result = sums[1] + shifted(sums[0], 1) + shifted(sums[2], -1)
        out_ref[h] = result[:, :lanes]
        carry_ref[h, :width] = result[:, lanes : lanes + 128].astype(BF16)
        carry_ref[h, width:] = result[:, lanes + 128 :].astype(BF16)


def kernel_grad_kernel(place_ref, live_ref, rep_ref, after_ref, *rest):
    del after_ref
    blocks, (m_ref, head_ref, mine_ref, theirs_ref, x, taps, total, result, sems, out_sems) = rest[:9], rest[9:]
    rows, width, lanes = m_ref.shape
    loads = start_loads(place_ref, blocks, x, sems)
    fill_taps(live_ref, m_ref, head_ref, taps)
    depth = 9 * width
    result[9 * depth :, :] = jnp.zeros((result.shape[0] - 9 * depth, 128), F32)
    for h in range(rows):
        if h % CHUNK == 0:
            wait_for(loads[h // CHUNK])
        stack = jnp.reshape(taps[h : h + 3], (depth, taps.shape[2]))
        right = x[h + 1]
        for a in range(3):
            left = stack[:, (2 - a) * 128 : (2 - a) * 128 + lanes]
            product = lax.dot_general(
                left, right, (((1,), (1,)), ((), ())), preferred_element_type=F32
            )
            if h == 0:
                total[a] = product
            elif h < rows - 1:
                total[a] += product
            else:
                product = total[a] + product
                for block in range(3):
                    row = (a * 3 + block) * depth
                    result[row : row + depth, :] = product[:, block * 128 : block * 128 + 128]
    half = result.shape[0] // 2
    copies = []
    for slot, (target, rep) in enumerate(((theirs_ref, 1 - rep_ref[0]), (mine_ref, rep_ref[0]))):
        source = result.at[pl.ds(pl.multiple_of(rep * half, 16), half)]
        copies.append(pltpu.make_async_copy(source, target, out_sems.at[slot]))
        copies[-1].start()
    wait_for(copies)


def params(mib):
    return pltpu.CompilerParams(vmem_limit_bytes=mib * MIB)


def cost(flops, size):
    return pl.CostEstimate(flops=flops, bytes_accessed=size, transcendentals=0)


FLOPS = 2 * 27 * 48 * 384 * 4096


def input_partials(place, live, m, head, weight):
    rows, width, lanes = m.shape
    channels = weight.shape[2]
    whole = jax.ShapeDtypeStruct((rows, width, lanes), BF16)
    half = jax.ShapeDtypeStruct((rows // 2, width, lanes), BF16)
    return pl.pallas_call(
        input_grad_kernel,
        out_shape=[whole] * 7 + [half] * 2,
        in_specs=[SMEM, SMEM, VMEM, VMEM, VMEM],
        out_specs=[ANY] * 9,
        scratch_shapes=[
            pltpu.VMEM((rows + 2, 3 * width, lanes + 256), BF16),
            pltpu.VMEM((channels, 27 * width), BF16),
            pltpu.VMEM((8, rows, width, lanes), BF16),
            pltpu.SemaphoreType.DMA((2, 8)),
        ],
        compiler_params=params(20),
        cost_estimate=cost(FLOPS, 5_000_000),
        name="input_partials",
    )(place, live, m, head, weight)


def pick(row, origin, own, other):
    return pl.pallas_call(
        pick_kernel,
        out_shape=jax.ShapeDtypeStruct(own.shape, own.dtype),
        in_specs=[SMEM, SMEM, VMEM, VMEM],
        out_specs=VMEM,
        compiler_params=params(4),
        name="pick",
    )(row, origin, own, other)


def assemble(scale, row, origin, own, other):
    return pl.pallas_call(
        functools.partial(assemble_kernel, scale),
        out_shape=jax.ShapeDtypeStruct(own.shape, own.dtype),
        in_specs=[SMEM, SMEM, VMEM, VMEM],
        out_specs=VMEM,
        compiler_params=params(6),
        name="assemble",
    )(row, origin, own, other)


def forward(place, after, blocks, weight):
    rows, width, lanes = blocks[0].shape
    channels = weight.shape[2]
    return pl.pallas_call(
        forward_kernel,
        out_shape=[
            jax.ShapeDtypeStruct((rows, width, lanes), F32),
            jax.ShapeDtypeStruct((rows, 2 * width, 128), BF16),
        ],
        in_specs=[SMEM] + [ANY] * 10 + [VMEM],
        out_specs=[VMEM, VMEM],
        scratch_shapes=[
            pltpu.VMEM((rows + 2, channels, lanes), BF16),
            pltpu.SemaphoreType.DMA((rows // CHUNK, 8)),
        ],
        compiler_params=params(20),
        cost_estimate=cost(FLOPS, 5_000_000),
        name="forward",
    )(place, after, *blocks, weight)


def kernel_grad(place, live, rep, after, blocks, m, head):
    rows, width, lanes = m.shape
    channels = 8 * width
    return pl.pallas_call(
        kernel_grad_kernel,
        out_shape=[jax.ShapeDtypeStruct((2048, 128), F32)] * 2,
        in_specs=[SMEM] * 3 + [ANY] * 10 + [VMEM, VMEM],
        out_specs=[ANY, ANY],
        scratch_shapes=[
            pltpu.VMEM((rows + 2, channels, lanes), BF16),
            pltpu.VMEM((rows + 2, 3 * width, lanes + 256), BF16),
            pltpu.VMEM((3, 9 * width, channels), F32),
            pltpu.VMEM((4096, 128), F32),
            pltpu.SemaphoreType.DMA((rows // CHUNK, 8)),
            pltpu.SemaphoreType.DMA((2,)),
        ],
        compiler_params=params(20),
        cost_estimate=cost(FLOPS, 6_000_000),
        name="kernel_grad",
    )(place, live, rep, after, *blocks, m, head)


def to_rows(x):
    f, c, h, w = x.shape
    return x.transpose(2, 1, 0, 3).reshape(h, c, f * w)


def from_rows(x):
    h, c, lanes = x.shape
    return x.reshape(h, c, lanes // 128, 128).transpose(2, 1, 0, 3)


def core_swap(x):
    return lax.ppermute(x, "rep", [(0, 1), (1, 0)])


def exchange(x):
    return lax.all_to_all(x, "dp", 0, 0, tiled=True)


def asked_for(source):
    rep = lax.axis_index("rep")
    wanted = lax.dynamic_slice_in_dim(source, rep * 8, 8, 0)
    row = jnp.maximum(wanted, 0) % 8
    origin = jnp.where(wanted < 0, 0, jnp.where(wanted // 8 == rep, 1, 2)).astype(jnp.int32)
    return row, origin


def handed_on(own, source):
    row, origin = asked_for(source)
    return pick(row, origin, own, core_swap(own))


def first_exchange(mine, theirs, payload):
    pair = (mine + core_swap(theirs)).astype(BF16).reshape(8, 256, 128)
    return jnp.concatenate([pair, payload], 1)


def both_cores(spread):
    rep = lax.axis_index("rep")
    there = core_swap(spread)
    half, there = (x[:, :256].reshape(2048, 128) for x in (spread, there))
    low = jnp.where(rep == 0, half, there)
    high = jnp.where(rep == 0, there, half)
    return jnp.concatenate([low, high], 0)


def per_device(frames, weight, cotangent, prev_owner, lengths):
    seg_len, width, height, columns = frames.shape
    channels = weight.shape[4]
    rep, me = lax.axis_index("rep"), lax.axis_index("dp")
    member = rep * 8 + me
    tensor = Group("tensor", tensor_index, lambda i: (i // 2, i % 2))
    place = jnp.stack(tensor.absolute()).astype(jnp.int32)
    segments = jnp.arange(prev_owner.shape[0], dtype=jnp.int32)
    follows = prev_owner[None, :] == segments[:, None]
    follower = jnp.max(jnp.where(follows, segments[None, :], -1), 1)

    x = to_rows(frames)
    m = to_rows(cotangent)
    rows = weight.transpose(1, 2, 3, 0, 4)[:, ::-1].reshape(9, 3 * width, channels)

    payload, x = lax.optimization_barrier((m[:, :, :256], x))
    payload = exchange(payload)
    blocks = tensor.gather(x)
    payload, _ = lax.optimization_barrier((payload, (blocks[1], blocks[2])))
    head = exchange(handed_on(payload, follower))
    keep = jnp.arange(seg_len) < lengths[member]
    keep_head = jnp.arange(2) < lengths[jnp.maximum(follower[member], 0)]
    live = jnp.concatenate([keep, keep_head]).astype(jnp.int32)

    partials = input_partials(place, live, m, head, rows)
    partials, blocks = lax.optimization_barrier((partials, blocks))
    arrived = tensor.begin_sum(partials)
    mine, theirs = kernel_grad(place, live, rep.astype(jnp.int32)[None], partials[0], blocks, m, head)
    conv, carry = forward(place, theirs, blocks, rows)
    spread = first_exchange(mine, theirs, carry)
    arrived, spread = lax.optimization_barrier((arrived, spread))
    input_grad = from_rows(tensor.end_sum(partials, arrived))
    conv = conv.reshape(height, width, seg_len, columns).transpose(2, 1, 0, 3)
    spread, conv = lax.optimization_barrier((exchange(spread), conv))

    cells = prev_owner.shape[0] * seg_len * height * columns
    row, origin = asked_for(prev_owner)
    spread = exchange(
        assemble(1.0 / math.sqrt(cells), row, origin, spread, core_swap(spread[:, 256:]))
    )
    received = spread[:, 256:]
    total = both_cores(spread)
    total = total[: 81 * width].reshape(3, 3, 3, 3, width, 128)
    weight_grad = total[:, :, ::-1].transpose(4, 0, 2, 3, 1, 5).reshape(weight.shape).astype(F32)

    received = received.reshape(height, 2, width, columns).transpose(1, 2, 0, 3).astype(F32)
    conv = conv + jnp.concatenate([received, jnp.zeros_like(received)], 0)
    output = jnp.where(keep[:, None, None, None], conv, 0.0).astype(BF16)
    return (output, input_grad, weight_grad)


def solution(mesh):
    split = P(("rep", "dp"), "tensor", None, None)
    kernel = P("tensor", None, None, None, None)
    return jax.shard_map(
        per_device,
        mesh=mesh,
        in_specs=(split, kernel, split, P(), P()),
        out_specs=(split, split, kernel),
        check_vma=False,
    )
```

```python
import functools
import math

import jax
import jax.numpy as jnp
from jax import lax
from jax.experimental import pallas as pl
from jax.experimental.pallas import tpu as pltpu
from jax.sharding import PartitionSpec as P

BF16 = jnp.bfloat16
F32 = jnp.float32
MIB = 1024 * 1024
ANY = pl.BlockSpec(memory_space=pl.ANY)
VMEM = pl.BlockSpec(memory_space=pltpu.VMEM)
SMEM = pl.BlockSpec(memory_space=pltpu.SMEM)

PLACES = ((0, 0), (0, 1), (1, 0), (3, 0), (1, 1), (3, 1), (2, 0), (2, 1))


def tensor_index(ring, pair):
    return ring * 2 + pair


class Group:
    def __init__(self, name, index_of, coords):
        self.name = name
        self.index_of = index_of
        me = lax.axis_index(name)
        self.ring, self.pair = coords(me)
        cells = [(r, p) for r in range(4) for p in range(2)]
        self.perm_up = [(index_of(r, p), index_of((r + 1) % 4, p)) for r, p in cells]
        self.perm_down = [(index_of(r, p), index_of((r + 3) % 4, p)) for r, p in cells]
        self.perm_swap = [(index_of(r, p), index_of(r, 1 - p)) for r, p in cells]

    def up(self, x):
        return lax.ppermute(x, self.name, self.perm_up)

    def down(self, x):
        return lax.ppermute(x, self.name, self.perm_down)

    def swap(self, x):
        return lax.ppermute(x, self.name, self.perm_swap)

    def absolute(self):
        return [self.index_of((self.ring + dr) % 4, self.pair ^ dp) for dr, dp in PLACES]

    def gather(self, x):
        half = x.shape[0] // 2
        following, prev, pair = lax.optimization_barrier((self.down(x), self.up(x), self.swap(x)))
        pair_next = self.swap(following)
        pair_prev = self.up(pair)
        second = self.down(following)
        far_a = self.down(pair_next[:half])
        far_b = self.up(pair_prev[half:])
        return [x, pair, following, prev, pair_next, pair_prev, second, far_a, far_b]

    def begin_sum(self, parts):
        far_a, far_b = parts[7:]
        return self.up(far_a), self.down(far_b)

    def end_sum(self, parts, arrived):
        own, pair, following, prev, pair_next, pair_prev, second = parts[:7]
        in_a, in_b = arrived
        got_swap = self.swap(added(pair_next, jnp.concatenate([in_a, jnp.zeros_like(in_a)], 0)))
        got_down = self.down(added(pair_prev, jnp.concatenate([jnp.zeros_like(in_b), in_b], 0)))
        got_up, from_prev = self.up(second), self.down(prev)
        last_up = self.up(added(following, got_swap, got_up))
        last_swap = self.swap(added(pair, got_down))
        return sum(x.astype(F32) for x in (own, from_prev, last_up, last_swap))


def added(*terms):
    return sum(x.astype(F32) for x in terms).astype(BF16)


def shifted(x, by):
    lanes = x.shape[-1]
    column = lax.broadcasted_iota(jnp.int32, x.shape, x.ndim - 1) % 128
    rolled = pltpu.roll(x, by % lanes, x.ndim - 1)
    edge = 0 if by == 1 else 127
    return jnp.where(column == edge, 0.0, rolled)


def fill_taps(live_ref, m_ref, head_ref, taps):
    rows, width, lanes = m_ref.shape
    frames = taps.shape[2] // 128
    taps[0] = jnp.zeros(taps.shape[1:], BF16)
    taps[rows + 1] = jnp.zeros(taps.shape[1:], BF16)
    for h in range(rows):
        whole = jnp.concatenate([m_ref[h], head_ref[h]], 1).astype(F32)
        wide = jnp.concatenate(
            [
                jnp.where(live_ref[f] > 0, whole[:, f * 128 : f * 128 + 128], 0.0)
                for f in range(frames)
            ],
            1,
        )
        taps[h + 1, 0:width] = shifted(wide, -1).astype(BF16)
        taps[h + 1, width : 2 * width] = wide.astype(BF16)
        taps[h + 1, 2 * width : 3 * width] = shifted(wide, 1).astype(BF16)


def input_grad_kernel(place_ref, live_ref, m_ref, head_ref, w_ref, *rest):
    outs, (taps, wt, parts) = rest[:9], rest[9:]
    rows, width, lanes = m_ref.shape
    half = rows // 2
    fill_taps(live_ref, m_ref, head_ref, taps)
    depth = 3 * 3 * width
    for a in range(3):
        block = jnp.concatenate([w_ref[a * 3 + b] for b in range(3)], 0)
        wt[:, a * depth : (a + 1) * depth] = block.T

    for h in range(rows):
        stack = jnp.reshape(taps[h : h + 3], (depth, taps.shape[2]))
        for start in range(0, lanes, 256):
            rhs = jnp.concatenate(
                [stack[:, (2 - a) * 128 + start : (2 - a) * 128 + start + 256] for a in range(3)], 0
            )
            total = jnp.dot(wt[...], rhs, preferred_element_type=F32).astype(BF16)
            for t in range(8):
                parts[t, :, start : start + 256] = total[t * width : (t + 1) * width]
        for r in range(8):
            target = outs[r].at[h] if r < 7 else outs[7 + h // half].at[h % half]
            target[...] = parts[place_ref[r]]


def pick_kernel(row_ref, from_ref, own_ref, other_ref, out_ref):
    for d in range(out_ref.shape[0]):
        own, other = own_ref[row_ref[d]], other_ref[row_ref[d]]
        chosen = jnp.where(from_ref[d] == 1, own, other)
        out_ref[d] = jnp.where(from_ref[d] == 0, jnp.zeros_like(chosen), chosen)


def assemble_kernel(scale, row_ref, from_ref, own_ref, other_ref, out_ref):
    count, summed = own_ref.shape[0], own_ref.shape[1] - other_ref.shape[1]
    total = own_ref[0, :summed].astype(F32)
    for d in range(1, count):
        total = total + own_ref[d, :summed].astype(F32)
    share = (total * scale).astype(BF16)
    for d in range(count):
        out_ref[d, :summed] = share
        own, other = own_ref[row_ref[d], summed:], other_ref[row_ref[d]]
        chosen = jnp.where(from_ref[d] == 1, own, other)
        out_ref[d, summed:] = jnp.where(from_ref[d] == 0, jnp.zeros_like(chosen), chosen)


CHUNK = 2


def start_loads(place_ref, blocks, x, sems):
    rows, width = blocks[0].shape[0], blocks[0].shape[1]
    half = rows // 2
    x[0] = jnp.zeros(x.shape[1:], BF16)
    x[rows + 1] = jnp.zeros(x.shape[1:], BF16)
    lists = []
    for part in range(rows // CHUNK):
        first = part * CHUNK
        copies = []
        for r in range(8):
            channel = pl.ds(pl.multiple_of(place_ref[r] * width, 16), width)
            block, skip = (blocks[r], 0) if r < 7 else (blocks[7 + first // half], first // half * half)
            copies.append(
                pltpu.make_async_copy(
                    block.at[first - skip : first - skip + CHUNK],
                    x.at[first + 1 : first + 1 + CHUNK, channel],
                    sems.at[part, r],
                )
            )
            copies[-1].start()
        lists.append(copies)
    return lists


def wait_for(copies):
    for copy in copies:
        copy.wait()


def forward_kernel(place_ref, after_ref, *rest):
    del after_ref
    blocks, (w_ref, out_ref, carry_ref, x, sems) = rest[:9], rest[9:]
    rows, width, lanes = out_ref.shape
    loads = start_loads(place_ref, blocks, x, sems)
    lhs = jnp.concatenate(
        [jnp.concatenate([w_ref[a * 3 + 2 - b] for a in range(3)], 0) for b in range(3)], 1
    )
    wait_for(loads[0])
    for h in range(rows):
        if (h + 1) % CHUNK == 0 and h + 1 < rows:
            wait_for(loads[(h + 1) // CHUNK])
        stack = jnp.reshape(x[h : h + 3], (3 * x.shape[1], lanes))
        y = jnp.dot(lhs, stack, preferred_element_type=F32)
        sums = []
        for e in range(3):
            frames = []
            for g in range(lanes // 128 + 2):
                terms = []
                for a in range(3):
                    f = g + a - 2
                    if 0 <= f < lanes // 128:
                        row = (a * 3 + e) * width
                        terms.append(y[row : row + width, f * 128 : f * 128 + 128])
                total = terms[0]
                for term in terms[1:]:
                    total = total + term
                frames.append(total)
            sums.append(jnp.concatenate(frames, 1))
        result = sums[1] + shifted(sums[0], 1) + shifted(sums[2], -1)
        out_ref[h] = result[:, :lanes]
        carry_ref[h, :width] = result[:, lanes : lanes + 128].astype(BF16)
        carry_ref[h, width:] = result[:, lanes + 128 :].astype(BF16)


def kernel_grad_kernel(place_ref, live_ref, rep_ref, after_ref, *rest):
    del after_ref
    blocks, (m_ref, head_ref, mine_ref, theirs_ref, x, taps, total, result, sems, out_sems) = rest[:9], rest[9:]
    rows, width, lanes = m_ref.shape
    loads = start_loads(place_ref, blocks, x, sems)
    fill_taps(live_ref, m_ref, head_ref, taps)
    depth = 9 * width
    result[9 * depth :, :] = jnp.zeros((result.shape[0] - 9 * depth, 128), F32)
    for h in range(rows):
        if h % CHUNK == 0:
            wait_for(loads[h // CHUNK])
        stack = jnp.reshape(taps[h : h + 3], (depth, taps.shape[2]))
        right = x[h + 1]
        for a in range(3):
            left = stack[:, (2 - a) * 128 : (2 - a) * 128 + lanes]
            product = lax.dot_general(
                left, right, (((1,), (1,)), ((), ())), preferred_element_type=F32
            )
            if h == 0:
                total[a] = product
            elif h < rows - 1:
                total[a] += product
            else:
                product = total[a] + product
                for block in range(3):
                    row = (a * 3 + block) * depth
                    result[row : row + depth, :] = product[:, block * 128 : block * 128 + 128]
    half = result.shape[0] // 2
    copies = []
    for slot, (target, rep) in enumerate(((theirs_ref, 1 - rep_ref[0]), (mine_ref, rep_ref[0]))):
        source = result.at[pl.ds(pl.multiple_of(rep * half, 16), half)]
        copies.append(pltpu.make_async_copy(source, target, out_sems.at[slot]))
        copies[-1].start()
    wait_for(copies)


def params(mib):
    return pltpu.CompilerParams(vmem_limit_bytes=mib * MIB)


def cost(flops, size):
    return pl.CostEstimate(flops=flops, bytes_accessed=size, transcendentals=0)


FLOPS = 2 * 27 * 48 * 384 * 4096


def input_partials(place, live, m, head, weight):
    rows, width, lanes = m.shape
    channels = weight.shape[2]
    whole = jax.ShapeDtypeStruct((rows, width, lanes), BF16)
    half = jax.ShapeDtypeStruct((rows // 2, width, lanes), BF16)
    return pl.pallas_call(
        input_grad_kernel,
        out_shape=[whole] * 7 + [half] * 2,
        in_specs=[SMEM, SMEM, VMEM, VMEM, VMEM],
        out_specs=[VMEM] * 9,
        scratch_shapes=[
            pltpu.VMEM((rows + 2, 3 * width, lanes + 256), BF16),
            pltpu.VMEM((channels, 27 * width), BF16),
            pltpu.VMEM((8, width, lanes), BF16),
        ],
        compiler_params=params(20),
        cost_estimate=cost(FLOPS, 5_000_000),
        name="input_partials",
    )(place, live, m, head, weight)


def pick(row, origin, own, other):
    return pl.pallas_call(
        pick_kernel,
        out_shape=jax.ShapeDtypeStruct(own.shape, own.dtype),
        in_specs=[SMEM, SMEM, VMEM, VMEM],
        out_specs=VMEM,
        compiler_params=params(4),
        name="pick",
    )(row, origin, own, other)


def assemble(scale, row, origin, own, other):
    return pl.pallas_call(
        functools.partial(assemble_kernel, scale),
        out_shape=jax.ShapeDtypeStruct(own.shape, own.dtype),
        in_specs=[SMEM, SMEM, VMEM, VMEM],
        out_specs=VMEM,
        compiler_params=params(6),
        name="assemble",
    )(row, origin, own, other)


def forward(place, after, blocks, weight):
    rows, width, lanes = blocks[0].shape
    channels = weight.shape[2]
    return pl.pallas_call(
        forward_kernel,
        out_shape=[
            jax.ShapeDtypeStruct((rows, width, lanes), F32),
            jax.ShapeDtypeStruct((rows, 2 * width, 128), BF16),
        ],
        in_specs=[SMEM] + [ANY] * 10 + [VMEM],
        out_specs=[VMEM, VMEM],
        scratch_shapes=[
            pltpu.VMEM((rows + 2, channels, lanes), BF16),
            pltpu.SemaphoreType.DMA((rows // CHUNK, 8)),
        ],
        compiler_params=params(20),
        cost_estimate=cost(FLOPS, 5_000_000),
        name="forward",
    )(place, after, *blocks, weight)


def kernel_grad(place, live, rep, after, blocks, m, head):
    rows, width, lanes = m.shape
    channels = 8 * width
    return pl.pallas_call(
        kernel_grad_kernel,
        out_shape=[jax.ShapeDtypeStruct((2048, 128), F32)] * 2,
        in_specs=[SMEM] * 3 + [ANY] * 10 + [VMEM, VMEM],
        out_specs=[ANY, ANY],
        scratch_shapes=[
            pltpu.VMEM((rows + 2, channels, lanes), BF16),
            pltpu.VMEM((rows + 2, 3 * width, lanes + 256), BF16),
            pltpu.VMEM((3, 9 * width, channels), F32),
            pltpu.VMEM((4096, 128), F32),
            pltpu.SemaphoreType.DMA((rows // CHUNK, 8)),
            pltpu.SemaphoreType.DMA((2,)),
        ],
        compiler_params=params(20),
        cost_estimate=cost(FLOPS, 6_000_000),
        name="kernel_grad",
    )(place, live, rep, after, *blocks, m, head)


def to_rows(x):
    f, c, h, w = x.shape
    return x.transpose(2, 1, 0, 3).reshape(h, c, f * w)


def from_rows(x):
    h, c, lanes = x.shape
    return x.reshape(h, c, lanes // 128, 128).transpose(2, 1, 0, 3)


def core_swap(x):
    return lax.ppermute(x, "rep", [(0, 1), (1, 0)])


def exchange(x):
    return lax.all_to_all(x, "dp", 0, 0, tiled=True)


def asked_for(source):
    rep = lax.axis_index("rep")
    wanted = lax.dynamic_slice_in_dim(source, rep * 8, 8, 0)
    row = jnp.maximum(wanted, 0) % 8
    origin = jnp.where(wanted < 0, 0, jnp.where(wanted // 8 == rep, 1, 2)).astype(jnp.int32)
    return row, origin


def handed_on(own, source):
    row, origin = asked_for(source)
    return pick(row, origin, own, core_swap(own))


def first_exchange(mine, theirs, payload):
    pair = (mine + core_swap(theirs)).astype(BF16).reshape(8, 256, 128)
    return jnp.concatenate([pair, payload], 1)


def both_cores(spread):
    rep = lax.axis_index("rep")
    there = core_swap(spread)
    half, there = (x[:, :256].reshape(2048, 128) for x in (spread, there))
    low = jnp.where(rep == 0, half, there)
    high = jnp.where(rep == 0, there, half)
    return jnp.concatenate([low, high], 0)


def per_device(frames, weight, cotangent, prev_owner, lengths):
    seg_len, width, height, columns = frames.shape
    channels = weight.shape[4]
    rep, me = lax.axis_index("rep"), lax.axis_index("dp")
    member = rep * 8 + me
    tensor = Group("tensor", tensor_index, lambda i: (i // 2, i % 2))
    place = jnp.stack(tensor.absolute()).astype(jnp.int32)
    segments = jnp.arange(prev_owner.shape[0], dtype=jnp.int32)
    follows = prev_owner[None, :] == segments[:, None]
    follower = jnp.max(jnp.where(follows, segments[None, :], -1), 1)

    x = to_rows(frames)
    m = to_rows(cotangent)
    rows = weight.transpose(1, 2, 3, 0, 4)[:, ::-1].reshape(9, 3 * width, channels)

    payload, x = lax.optimization_barrier((m[:, :, :256], x))
    payload = exchange(payload)
    blocks = tensor.gather(x)
    payload, _ = lax.optimization_barrier((payload, (blocks[1], blocks[2])))
    head = exchange(handed_on(payload, follower))
    keep = jnp.arange(seg_len) < lengths[member]
    keep_head = jnp.arange(2) < lengths[jnp.maximum(follower[member], 0)]
    live = jnp.concatenate([keep, keep_head]).astype(jnp.int32)

    partials = input_partials(place, live, m, head, rows)
    partials, blocks = lax.optimization_barrier((partials, blocks))
    arrived = tensor.begin_sum(partials)
    mine, theirs = kernel_grad(place, live, rep.astype(jnp.int32)[None], partials[0], blocks, m, head)
    conv, carry = forward(place, theirs, blocks, rows)
    spread = first_exchange(mine, theirs, carry)
    arrived, spread = lax.optimization_barrier((arrived, spread))
    input_grad = from_rows(tensor.end_sum(partials, arrived))
    conv = conv.reshape(height, width, seg_len, columns).transpose(2, 1, 0, 3)
    spread = exchange(spread)

    cells = prev_owner.shape[0] * seg_len * height * columns
    row, origin = asked_for(prev_owner)
    spread = exchange(
        assemble(1.0 / math.sqrt(cells), row, origin, spread, core_swap(spread[:, 256:]))
    )
    received = spread[:, 256:]
    total = both_cores(spread)
    total = total[: 81 * width].reshape(3, 3, 3, 3, width, 128)
    weight_grad = total[:, :, ::-1].transpose(4, 0, 2, 3, 1, 5).reshape(weight.shape).astype(F32)

    received = received.reshape(height, 2, width, columns).transpose(1, 2, 0, 3).astype(F32)
    conv = conv + jnp.concatenate([received, jnp.zeros_like(received)], 0)
    output = jnp.where(keep[:, None, None, None], conv, 0.0).astype(BF16)
    return (output, input_grad, weight_grad)


def solution(mesh):
    split = P(("rep", "dp"), "tensor", None, None)
    kernel = P("tensor", None, None, None, None)
    return jax.shard_map(
        per_device,
        mesh=mesh,
        in_specs=(split, kernel, split, P(), P()),
        out_specs=(split, split, kernel),
        check_vma=False,
    )
```

```python
import functools
import math

import jax
import jax.numpy as jnp
from jax import lax
from jax.experimental import pallas as pl
from jax.experimental.pallas import tpu as pltpu
from jax.sharding import PartitionSpec as P

BF16 = jnp.bfloat16
F32 = jnp.float32
MIB = 1024 * 1024
ANY = pl.BlockSpec(memory_space=pl.ANY)
VMEM = pl.BlockSpec(memory_space=pltpu.VMEM)
SMEM = pl.BlockSpec(memory_space=pltpu.SMEM)

PLACES = ((0, 0), (0, 1), (1, 0), (3, 0), (1, 1), (3, 1), (2, 0), (2, 1))


def tensor_index(ring, pair):
    return ring * 2 + pair


class Group:
    def __init__(self, name, index_of, coords):
        self.name = name
        self.index_of = index_of
        me = lax.axis_index(name)
        self.ring, self.pair = coords(me)
        cells = [(r, p) for r in range(4) for p in range(2)]
        self.perm_up = [(index_of(r, p), index_of((r + 1) % 4, p)) for r, p in cells]
        self.perm_down = [(index_of(r, p), index_of((r + 3) % 4, p)) for r, p in cells]
        self.perm_swap = [(index_of(r, p), index_of(r, 1 - p)) for r, p in cells]

    def up(self, x):
        return lax.ppermute(x, self.name, self.perm_up)

    def down(self, x):
        return lax.ppermute(x, self.name, self.perm_down)

    def swap(self, x):
        return lax.ppermute(x, self.name, self.perm_swap)

    def absolute(self):
        return [self.index_of((self.ring + dr) % 4, self.pair ^ dp) for dr, dp in PLACES]

    def gather(self, x):
        half = x.shape[0] // 2
        following, prev, pair = lax.optimization_barrier((self.down(x), self.up(x), self.swap(x)))
        pair_next = self.swap(following)
        pair_prev = self.up(pair)
        second = self.down(following)
        far_a = self.down(pair_next[:half])
        far_b = self.up(pair_prev[half:])
        return [x, pair, following, prev, pair_next, pair_prev, second, far_a, far_b]

    def begin_sum(self, parts):
        far_a, far_b = parts[7:]
        return self.up(far_a), self.down(far_b)

    def end_sum(self, parts, arrived, tie):
        own, pair, following, prev, pair_next, pair_prev, second = parts[:7]
        in_a, in_b = arrived
        got_swap = self.swap(added(pair_next, jnp.concatenate([in_a, jnp.zeros_like(in_a)], 0)))
        got_down = self.down(added(pair_prev, jnp.concatenate([jnp.zeros_like(in_b), in_b], 0)))
        got_up, from_prev = self.up(second), self.down(prev)
        got_swap, got_up, tie = lax.optimization_barrier((got_swap, got_up, tie))
        last_up = self.up(added(following, got_swap, got_up))
        last_swap = self.swap(added(pair, got_down))
        return sum(x.astype(F32) for x in (own, from_prev, last_up, last_swap)), tie


def added(*terms):
    return sum(x.astype(F32) for x in terms).astype(BF16)


def shifted(x, by):
    lanes = x.shape[-1]
    column = lax.broadcasted_iota(jnp.int32, x.shape, x.ndim - 1) % 128
    rolled = pltpu.roll(x, by % lanes, x.ndim - 1)
    edge = 0 if by == 1 else 127
    return jnp.where(column == edge, 0.0, rolled)


def fill_taps(live_ref, m_ref, head_ref, taps):
    rows, width, lanes = m_ref.shape
    frames = taps.shape[2] // 128
    taps[0] = jnp.zeros(taps.shape[1:], BF16)
    taps[rows + 1] = jnp.zeros(taps.shape[1:], BF16)
    for h in range(rows):
        whole = jnp.concatenate([m_ref[h], head_ref[h]], 1).astype(F32)
        wide = jnp.concatenate(
            [
                jnp.where(live_ref[f] > 0, whole[:, f * 128 : f * 128 + 128], 0.0)
                for f in range(frames)
            ],
            1,
        )
        taps[h + 1, 0:width] = shifted(wide, -1).astype(BF16)
        taps[h + 1, width : 2 * width] = wide.astype(BF16)
        taps[h + 1, 2 * width : 3 * width] = shifted(wide, 1).astype(BF16)


def input_grad_kernel(place_ref, live_ref, m_ref, head_ref, w_ref, *rest):
    outs, (taps, wt, parts) = rest[:9], rest[9:]
    rows, width, lanes = m_ref.shape
    half = rows // 2
    fill_taps(live_ref, m_ref, head_ref, taps)
    depth = 3 * 3 * width
    for a in range(3):
        block = jnp.concatenate([w_ref[a * 3 + b] for b in range(3)], 0)
        wt[:, a * depth : (a + 1) * depth] = block.T

    for h in range(rows):
        stack = jnp.reshape(taps[h : h + 3], (depth, taps.shape[2]))
        for start in range(0, lanes, 256):
            rhs = jnp.concatenate(
                [stack[:, (2 - a) * 128 + start : (2 - a) * 128 + start + 256] for a in range(3)], 0
            )
            total = jnp.dot(wt[...], rhs, preferred_element_type=F32).astype(BF16)
            for t in range(8):
                parts[t, :, start : start + 256] = total[t * width : (t + 1) * width]
        for r in range(8):
            target = outs[r].at[h] if r < 7 else outs[7 + h // half].at[h % half]
            target[...] = parts[place_ref[r]]


def pick_kernel(row_ref, from_ref, own_ref, other_ref, out_ref):
    for d in range(out_ref.shape[0]):
        own, other = own_ref[row_ref[d]], other_ref[row_ref[d]]
        chosen = jnp.where(from_ref[d] == 1, own, other)
        out_ref[d] = jnp.where(from_ref[d] == 0, jnp.zeros_like(chosen), chosen)


def assemble_kernel(scale, row_ref, from_ref, own_ref, other_ref, out_ref):
    count, summed = own_ref.shape[0], own_ref.shape[1] - other_ref.shape[1]
    total = own_ref[0, :summed].astype(F32)
    for d in range(1, count):
        total = total + own_ref[d, :summed].astype(F32)
    share = (total * scale).astype(BF16)
    for d in range(count):
        out_ref[d, :summed] = share
        own, other = own_ref[row_ref[d], summed:], other_ref[row_ref[d]]
        chosen = jnp.where(from_ref[d] == 1, own, other)
        out_ref[d, summed:] = jnp.where(from_ref[d] == 0, jnp.zeros_like(chosen), chosen)


CHUNK = 2


def start_loads(place_ref, blocks, x, sems):
    rows, width = blocks[0].shape[0], blocks[0].shape[1]
    half = rows // 2
    x[0] = jnp.zeros(x.shape[1:], BF16)
    x[rows + 1] = jnp.zeros(x.shape[1:], BF16)
    lists = []
    for part in range(rows // CHUNK):
        first = part * CHUNK
        copies = []
        for r in range(8):
            channel = pl.ds(pl.multiple_of(place_ref[r] * width, 16), width)
            block, skip = (blocks[r], 0) if r < 7 else (blocks[7 + first // half], first // half * half)
            copies.append(
                pltpu.make_async_copy(
                    block.at[first - skip : first - skip + CHUNK],
                    x.at[first + 1 : first + 1 + CHUNK, channel],
                    sems.at[part, r],
                )
            )
            copies[-1].start()
        lists.append(copies)
    return lists


def wait_for(copies):
    for copy in copies:
        copy.wait()


def forward_kernel(place_ref, after_ref, *rest):
    del after_ref
    blocks, (w_ref, out_ref, carry_ref, x, sems) = rest[:9], rest[9:]
    rows, width, lanes = out_ref.shape
    loads = start_loads(place_ref, blocks, x, sems)
    lhs = jnp.concatenate(
        [jnp.concatenate([w_ref[a * 3 + 2 - b] for a in range(3)], 0) for b in range(3)], 1
    )
    wait_for(loads[0])
    for h in range(rows):
        if (h + 1) % CHUNK == 0 and h + 1 < rows:
            wait_for(loads[(h + 1) // CHUNK])
        stack = jnp.reshape(x[h : h + 3], (3 * x.shape[1], lanes))
        y = jnp.dot(lhs, stack, preferred_element_type=F32)
        sums = []
        for e in range(3):
            frames = []
            for g in range(lanes // 128 + 2):
                terms = []
                for a in range(3):
                    f = g + a - 2
                    if 0 <= f < lanes // 128:
                        row = (a * 3 + e) * width
                        terms.append(y[row : row + width, f * 128 : f * 128 + 128])
                total = terms[0]
                for term in terms[1:]:
                    total = total + term
                frames.append(total)
            sums.append(jnp.concatenate(frames, 1))
        result = sums[1] + shifted(sums[0], 1) + shifted(sums[2], -1)
        out_ref[h] = result[:, :lanes]
        carry_ref[h, :width] = result[:, lanes : lanes + 128].astype(BF16)
        carry_ref[h, width:] = result[:, lanes + 128 :].astype(BF16)


def kernel_grad_kernel(place_ref, live_ref, rep_ref, after_ref, *rest):
    del after_ref
    blocks, (m_ref, head_ref, mine_ref, theirs_ref, x, taps, total, result, sems, out_sems) = rest[:9], rest[9:]
    rows, width, lanes = m_ref.shape
    loads = start_loads(place_ref, blocks, x, sems)
    fill_taps(live_ref, m_ref, head_ref, taps)
    depth = 9 * width
    result[9 * depth :, :] = jnp.zeros((result.shape[0] - 9 * depth, 128), F32)
    for h in range(rows):
        if h % CHUNK == 0:
            wait_for(loads[h // CHUNK])
        stack = jnp.reshape(taps[h : h + 3], (depth, taps.shape[2]))
        right = x[h + 1]
        for a in range(3):
            left = stack[:, (2 - a) * 128 : (2 - a) * 128 + lanes]
            product = lax.dot_general(
                left, right, (((1,), (1,)), ((), ())), preferred_element_type=F32
            )
            if h == 0:
                total[a] = product
            elif h < rows - 1:
                total[a] += product
            else:
                product = total[a] + product
                for block in range(3):
                    row = (a * 3 + block) * depth
                    result[row : row + depth, :] = product[:, block * 128 : block * 128 + 128]
    half = result.shape[0] // 2
    copies = []
    for slot, (target, rep) in enumerate(((theirs_ref, 1 - rep_ref[0]), (mine_ref, rep_ref[0]))):
        source = result.at[pl.ds(pl.multiple_of(rep * half, 16), half)]
        copies.append(pltpu.make_async_copy(source, target, out_sems.at[slot]))
        copies[-1].start()
    wait_for(copies)


def params(mib):
    return pltpu.CompilerParams(vmem_limit_bytes=mib * MIB)


def cost(flops, size):
    return pl.CostEstimate(flops=flops, bytes_accessed=size, transcendentals=0)


FLOPS = 2 * 27 * 48 * 384 * 4096


def input_partials(place, live, m, head, weight):
    rows, width, lanes = m.shape
    channels = weight.shape[2]
    whole = jax.ShapeDtypeStruct((rows, width, lanes), BF16)
    half = jax.ShapeDtypeStruct((rows // 2, width, lanes), BF16)
    return pl.pallas_call(
        input_grad_kernel,
        out_shape=[whole] * 7 + [half] * 2,
        in_specs=[SMEM, SMEM, VMEM, VMEM, VMEM],
        out_specs=[VMEM] * 9,
        scratch_shapes=[
            pltpu.VMEM((rows + 2, 3 * width, lanes + 256), BF16),
            pltpu.VMEM((channels, 27 * width), BF16),
            pltpu.VMEM((8, width, lanes), BF16),
        ],
        compiler_params=params(20),
        cost_estimate=cost(FLOPS, 5_000_000),
        name="input_partials",
    )(place, live, m, head, weight)


def pick(row, origin, own, other):
    return pl.pallas_call(
        pick_kernel,
        out_shape=jax.ShapeDtypeStruct(own.shape, own.dtype),
        in_specs=[SMEM, SMEM, VMEM, VMEM],
        out_specs=VMEM,
        compiler_params=params(4),
        name="pick",
    )(row, origin, own, other)


def assemble(scale, row, origin, own, other):
    return pl.pallas_call(
        functools.partial(assemble_kernel, scale),
        out_shape=jax.ShapeDtypeStruct(own.shape, own.dtype),
        in_specs=[SMEM, SMEM, VMEM, VMEM],
        out_specs=VMEM,
        compiler_params=params(6),
        name="assemble",
    )(row, origin, own, other)


def forward(place, after, blocks, weight):
    rows, width, lanes = blocks[0].shape
    channels = weight.shape[2]
    return pl.pallas_call(
        forward_kernel,
        out_shape=[
            jax.ShapeDtypeStruct((rows, width, lanes), F32),
            jax.ShapeDtypeStruct((rows, 2 * width, 128), BF16),
        ],
        in_specs=[SMEM] + [ANY] * 10 + [VMEM],
        out_specs=[VMEM, VMEM],
        scratch_shapes=[
            pltpu.VMEM((rows + 2, channels, lanes), BF16),
            pltpu.SemaphoreType.DMA((rows // CHUNK, 8)),
        ],
        compiler_params=params(20),
        cost_estimate=cost(FLOPS, 5_000_000),
        name="forward",
    )(place, after, *blocks, weight)


def kernel_grad(place, live, rep, after, blocks, m, head):
    rows, width, lanes = m.shape
    channels = 8 * width
    return pl.pallas_call(
        kernel_grad_kernel,
        out_shape=[jax.ShapeDtypeStruct((2048, 128), F32)] * 2,
        in_specs=[SMEM] * 3 + [ANY] * 10 + [VMEM, VMEM],
        out_specs=[ANY, ANY],
        scratch_shapes=[
            pltpu.VMEM((rows + 2, channels, lanes), BF16),
            pltpu.VMEM((rows + 2, 3 * width, lanes + 256), BF16),
            pltpu.VMEM((3, 9 * width, channels), F32),
            pltpu.VMEM((4096, 128), F32),
            pltpu.SemaphoreType.DMA((rows // CHUNK, 8)),
            pltpu.SemaphoreType.DMA((2,)),
        ],
        compiler_params=params(20),
        cost_estimate=cost(FLOPS, 6_000_000),
        name="kernel_grad",
    )(place, live, rep, after, *blocks, m, head)


def to_rows(x):
    f, c, h, w = x.shape
    return x.transpose(2, 1, 0, 3).reshape(h, c, f * w)


def from_rows(x):
    h, c, lanes = x.shape
    return x.reshape(h, c, lanes // 128, 128).transpose(2, 1, 0, 3)


def core_swap(x):
    return lax.ppermute(x, "rep", [(0, 1), (1, 0)])


def exchange(x):
    return lax.all_to_all(x, "dp", 0, 0, tiled=True)


def asked_for(source):
    rep = lax.axis_index("rep")
    wanted = lax.dynamic_slice_in_dim(source, rep * 8, 8, 0)
    row = jnp.maximum(wanted, 0) % 8
    origin = jnp.where(wanted < 0, 0, jnp.where(wanted // 8 == rep, 1, 2)).astype(jnp.int32)
    return row, origin


def handed_on(own, source):
    row, origin = asked_for(source)
    return pick(row, origin, own, core_swap(own))


def first_exchange(mine, theirs, payload):
    pair = (mine + core_swap(theirs)).astype(BF16).reshape(8, 256, 128)
    return jnp.concatenate([pair, payload], 1)


def both_cores(spread):
    rep = lax.axis_index("rep")
    there = core_swap(spread)
    half, there = (x[:, :256].reshape(2048, 128) for x in (spread, there))
    low = jnp.where(rep == 0, half, there)
    high = jnp.where(rep == 0, there, half)
    return jnp.concatenate([low, high], 0)


def per_device(frames, weight, cotangent, prev_owner, lengths):
    seg_len, width, height, columns = frames.shape
    channels = weight.shape[4]
    rep, me = lax.axis_index("rep"), lax.axis_index("dp")
    member = rep * 8 + me
    tensor = Group("tensor", tensor_index, lambda i: (i // 2, i % 2))
    place = jnp.stack(tensor.absolute()).astype(jnp.int32)
    segments = jnp.arange(prev_owner.shape[0], dtype=jnp.int32)
    follows = prev_owner[None, :] == segments[:, None]
    follower = jnp.max(jnp.where(follows, segments[None, :], -1), 1)

    x = to_rows(frames)
    m = to_rows(cotangent)
    rows = weight.transpose(1, 2, 3, 0, 4)[:, ::-1].reshape(9, 3 * width, channels)

    payload, x = lax.optimization_barrier((m[:, :, :256], x))
    payload = exchange(payload)
    blocks = tensor.gather(x)
    payload, _ = lax.optimization_barrier((payload, (blocks[1], blocks[2])))
    head = exchange(handed_on(payload, follower))
    keep = jnp.arange(seg_len) < lengths[member]
    keep_head = jnp.arange(2) < lengths[jnp.maximum(follower[member], 0)]
    live = jnp.concatenate([keep, keep_head]).astype(jnp.int32)

    partials = input_partials(place, live, m, head, rows)
    partials, blocks = lax.optimization_barrier((partials, blocks))
    arrived = tensor.begin_sum(partials)
    mine, theirs = kernel_grad(place, live, rep.astype(jnp.int32)[None], partials[0], blocks, m, head)
    conv, carry = forward(place, theirs, blocks, rows)
    spread = first_exchange(mine, theirs, carry)
    arrived, spread = lax.optimization_barrier((arrived, spread))
    input_grad, spread = tensor.end_sum(partials, arrived, exchange(spread))
    input_grad = from_rows(input_grad)
    conv = conv.reshape(height, width, seg_len, columns).transpose(2, 1, 0, 3)

    cells = prev_owner.shape[0] * seg_len * height * columns
    row, origin = asked_for(prev_owner)
    spread = exchange(
        assemble(1.0 / math.sqrt(cells), row, origin, spread, core_swap(spread[:, 256:]))
    )
    received = spread[:, 256:]
    total = both_cores(spread)
    total = total[: 81 * width].reshape(3, 3, 3, 3, width, 128)
    weight_grad = total[:, :, ::-1].transpose(4, 0, 2, 3, 1, 5).reshape(weight.shape).astype(F32)

    received = received.reshape(height, 2, width, columns).transpose(1, 2, 0, 3).astype(F32)
    conv = conv + jnp.concatenate([received, jnp.zeros_like(received)], 0)
    output = jnp.where(keep[:, None, None, None], conv, 0.0).astype(BF16)
    return (output, input_grad, weight_grad)


def solution(mesh):
    split = P(("rep", "dp"), "tensor", None, None)
    kernel = P("tensor", None, None, None, None)
    return jax.shard_map(
        per_device,
        mesh=mesh,
        in_specs=(split, kernel, split, P(), P()),
        out_specs=(split, split, kernel),
        check_vma=False,
    )
```

```python
import functools
import math

import jax
import jax.numpy as jnp
from jax import lax
from jax.experimental import pallas as pl
from jax.experimental.pallas import tpu as pltpu
from jax.sharding import PartitionSpec as P

BF16 = jnp.bfloat16
F32 = jnp.float32
VMEM_LIMIT = 56 * 1024 * 1024
ANY = pl.BlockSpec(memory_space=pl.ANY)
VMEM = pl.BlockSpec(memory_space=pltpu.VMEM)
SMEM = pl.BlockSpec(memory_space=pltpu.SMEM)

PLACES = ((0, 0), (0, 1), (1, 0), (3, 0), (1, 1), (3, 1), (2, 0), (2, 1))


def tensor_index(ring, pair):
    return ring * 2 + pair


class Group:
    def __init__(self, name, index_of, coords):
        self.name = name
        self.index_of = index_of
        me = lax.axis_index(name)
        self.ring, self.pair = coords(me)
        cells = [(r, p) for r in range(4) for p in range(2)]
        self.perm_up = [(index_of(r, p), index_of((r + 1) % 4, p)) for r, p in cells]
        self.perm_down = [(index_of(r, p), index_of((r + 3) % 4, p)) for r, p in cells]
        self.perm_swap = [(index_of(r, p), index_of(r, 1 - p)) for r, p in cells]

    def up(self, x):
        return lax.ppermute(x, self.name, self.perm_up)

    def down(self, x):
        return lax.ppermute(x, self.name, self.perm_down)

    def swap(self, x):
        return lax.ppermute(x, self.name, self.perm_swap)

    def absolute(self):
        return [self.index_of((self.ring + dr) % 4, self.pair ^ dp) for dr, dp in PLACES]

    def gather(self, x):
        half = x.shape[0] // 2
        following, prev, pair = lax.optimization_barrier((self.down(x), self.up(x), self.swap(x)))
        pair_next = self.swap(following)
        pair_prev = self.up(pair)
        second = self.down(following)
        far_a = self.down(pair_next[:half])
        far_b = self.up(pair_prev[half:])
        return [x, pair, following, prev, pair_next, pair_prev, second, far_a, far_b]

    def begin_sum(self, parts):
        far_a, far_b = parts[7:]
        return self.up(far_a), self.down(far_b)

    def end_sum(self, parts, arrived):
        own, pair, following, prev, pair_next, pair_prev, second = parts[:7]
        in_a, in_b = arrived
        got_swap = self.swap(added(pair_next, jnp.concatenate([in_a, jnp.zeros_like(in_a)], 0)))
        got_down = self.down(added(pair_prev, jnp.concatenate([jnp.zeros_like(in_b), in_b], 0)))
        got_up, from_prev = self.up(second), self.down(prev)
        last_up = self.up(added(following, got_swap, got_up))
        last_swap = self.swap(added(pair, got_down))
        return sum(x.astype(F32) for x in (own, from_prev, last_up, last_swap))


def added(*terms):
    return sum(x.astype(F32) for x in terms).astype(BF16)


def shifted(x, by):
    lanes = x.shape[-1]
    column = lax.broadcasted_iota(jnp.int32, x.shape, x.ndim - 1) % 128
    rolled = pltpu.roll(x, by % lanes, x.ndim - 1)
    edge = 0 if by == 1 else 127
    return jnp.where(column == edge, 0.0, rolled)


def fill_taps(live_ref, m_ref, head_ref, taps):
    rows, width, lanes = m_ref.shape
    frames = taps.shape[2] // 128
    taps[0] = jnp.zeros(taps.shape[1:], BF16)
    taps[rows + 1] = jnp.zeros(taps.shape[1:], BF16)
    for h in range(rows):
        whole = jnp.concatenate([m_ref[h], head_ref[h]], 1).astype(F32)
        wide = jnp.concatenate(
            [
                jnp.where(live_ref[f] > 0, whole[:, f * 128 : f * 128 + 128], 0.0)
                for f in range(frames)
            ],
            1,
        )
        taps[h + 1, 0:width] = shifted(wide, -1).astype(BF16)
        taps[h + 1, width : 2 * width] = wide.astype(BF16)
        taps[h + 1, 2 * width : 3 * width] = shifted(wide, 1).astype(BF16)


def input_grad_kernel(place_ref, live_ref, m_ref, head_ref, w_ref, *rest):
    outs, (taps, wt, parts) = rest[:9], rest[9:]
    rows, width, lanes = m_ref.shape
    half = rows // 2
    fill_taps(live_ref, m_ref, head_ref, taps)
    depth = 3 * 3 * width
    for a in range(3):
        block = jnp.concatenate([w_ref[a * 3 + b] for b in range(3)], 0)
        wt[:, a * depth : (a + 1) * depth] = block.T

    for h in range(rows):
        stack = jnp.reshape(taps[h : h + 3], (depth, taps.shape[2]))
        for start in range(0, lanes, 256):
            rhs = jnp.concatenate(
                [stack[:, (2 - a) * 128 + start : (2 - a) * 128 + start + 256] for a in range(3)], 0
            )
            total = jnp.dot(wt[...], rhs, preferred_element_type=F32).astype(BF16)
            for t in range(8):
                parts[t, :, start : start + 256] = total[t * width : (t + 1) * width]
        for r in range(8):
            target = outs[r].at[h] if r < 7 else outs[7 + h // half].at[h % half]
            target[...] = parts[place_ref[r]]


def pick_kernel(row_ref, from_ref, own_ref, other_ref, out_ref):
    for d in range(out_ref.shape[0]):
        own, other = own_ref[row_ref[d]], other_ref[row_ref[d]]
        chosen = jnp.where(from_ref[d] == 1, own, other)
        out_ref[d] = jnp.where(from_ref[d] == 0, jnp.zeros_like(chosen), chosen)


def assemble_kernel(scale, row_ref, from_ref, own_ref, other_ref, out_ref):
    count, summed = own_ref.shape[0], own_ref.shape[1] - other_ref.shape[1]
    total = own_ref[0, :summed].astype(F32)
    for d in range(1, count):
        total = total + own_ref[d, :summed].astype(F32)
    share = (total * scale).astype(BF16)
    for d in range(count):
        out_ref[d, :summed] = share
        own, other = own_ref[row_ref[d], summed:], other_ref[row_ref[d]]
        chosen = jnp.where(from_ref[d] == 1, own, other)
        out_ref[d, summed:] = jnp.where(from_ref[d] == 0, jnp.zeros_like(chosen), chosen)


CHUNK = 2


def start_loads(place_ref, blocks, x, sems):
    rows, width = blocks[0].shape[0], blocks[0].shape[1]
    half = rows // 2
    x[0] = jnp.zeros(x.shape[1:], BF16)
    x[rows + 1] = jnp.zeros(x.shape[1:], BF16)
    lists = []
    for part in range(rows // CHUNK):
        first = part * CHUNK
        copies = []
        for r in range(8):
            channel = pl.ds(pl.multiple_of(place_ref[r] * width, 16), width)
            block, skip = (blocks[r], 0) if r < 7 else (blocks[7 + first // half], first // half * half)
            copies.append(
                pltpu.make_async_copy(
                    block.at[first - skip : first - skip + CHUNK],
                    x.at[first + 1 : first + 1 + CHUNK, channel],
                    sems.at[part, r],
                )
            )
            copies[-1].start()
        lists.append(copies)
    return lists


def wait_for(copies):
    for copy in copies:
        copy.wait()


def forward_kernel(place_ref, after_ref, *rest):
    del after_ref
    blocks, (w_ref, out_ref, carry_ref, x, sems) = rest[:9], rest[9:]
    rows, width, lanes = out_ref.shape
    loads = start_loads(place_ref, blocks, x, sems)
    lhs = jnp.concatenate(
        [jnp.concatenate([w_ref[a * 3 + 2 - b] for a in range(3)], 0) for b in range(3)], 1
    )
    wait_for(loads[0])
    for h in range(rows):
        if (h + 1) % CHUNK == 0 and h + 1 < rows:
            wait_for(loads[(h + 1) // CHUNK])
        stack = jnp.reshape(x[h : h + 3], (3 * x.shape[1], lanes))
        y = jnp.dot(lhs, stack, preferred_element_type=F32)
        sums = []
        for e in range(3):
            frames = []
            for g in range(lanes // 128 + 2):
                terms = []
                for a in range(3):
                    f = g + a - 2
                    if 0 <= f < lanes // 128:
                        row = (a * 3 + e) * width
                        terms.append(y[row : row + width, f * 128 : f * 128 + 128])
                total = terms[0]
                for term in terms[1:]:
                    total = total + term
                frames.append(total)
            sums.append(jnp.concatenate(frames, 1))
        result = sums[1] + shifted(sums[0], 1) + shifted(sums[2], -1)
        out_ref[h] = result[:, :lanes]
        carry_ref[h, :width] = result[:, lanes : lanes + 128].astype(BF16)
        carry_ref[h, width:] = result[:, lanes + 128 :].astype(BF16)


def kernel_grad_kernel(place_ref, live_ref, rep_ref, after_ref, *rest):
    del after_ref
    blocks, (m_ref, head_ref, mine_ref, theirs_ref, x, taps, total, result, sems, out_sems) = rest[:9], rest[9:]
    rows, width, lanes = m_ref.shape
    loads = start_loads(place_ref, blocks, x, sems)
    fill_taps(live_ref, m_ref, head_ref, taps)
    depth = 9 * width
    result[9 * depth :, :] = jnp.zeros((result.shape[0] - 9 * depth, 128), F32)
    for h in range(rows):
        if h % CHUNK == 0:
            wait_for(loads[h // CHUNK])
        stack = jnp.reshape(taps[h : h + 3], (depth, taps.shape[2]))
        right = x[h + 1]
        for a in range(3):
            left = stack[:, (2 - a) * 128 : (2 - a) * 128 + lanes]
            product = lax.dot_general(
                left, right, (((1,), (1,)), ((), ())), preferred_element_type=F32
            )
            if h == 0:
                total[a] = product
            elif h < rows - 1:
                total[a] += product
            else:
                product = total[a] + product
                for block in range(3):
                    row = (a * 3 + block) * depth
                    result[row : row + depth, :] = product[:, block * 128 : block * 128 + 128]
    half = result.shape[0] // 2
    copies = []
    for slot, (target, rep) in enumerate(((theirs_ref, 1 - rep_ref[0]), (mine_ref, rep_ref[0]))):
        source = result.at[pl.ds(pl.multiple_of(rep * half, 16), half)]
        copies.append(pltpu.make_async_copy(source, target, out_sems.at[slot]))
        copies[-1].start()
    wait_for(copies)


def params():
    return pltpu.CompilerParams(vmem_limit_bytes=VMEM_LIMIT)


def cost(flops, size):
    return pl.CostEstimate(flops=flops, bytes_accessed=size, transcendentals=0)


FLOPS = 2 * 27 * 48 * 384 * 4096


def input_partials(place, live, m, head, weight):
    rows, width, lanes = m.shape
    channels = weight.shape[2]
    whole = jax.ShapeDtypeStruct((rows, width, lanes), BF16)
    half = jax.ShapeDtypeStruct((rows // 2, width, lanes), BF16)
    return pl.pallas_call(
        input_grad_kernel,
        out_shape=[whole] * 7 + [half] * 2,
        in_specs=[SMEM, SMEM, VMEM, VMEM, VMEM],
        out_specs=[VMEM] * 9,
        scratch_shapes=[
            pltpu.VMEM((rows + 2, 3 * width, lanes + 256), BF16),
            pltpu.VMEM((channels, 27 * width), BF16),
            pltpu.VMEM((8, width, lanes), BF16),
        ],
        compiler_params=params(),
        cost_estimate=cost(FLOPS, 5_000_000),
        name="input_partials",
    )(place, live, m, head, weight)


def pick(row, origin, own, other):
    return pl.pallas_call(
        pick_kernel,
        out_shape=jax.ShapeDtypeStruct(own.shape, own.dtype),
        in_specs=[SMEM, SMEM, VMEM, VMEM],
        out_specs=VMEM,
        compiler_params=params(),
        name="pick",
    )(row, origin, own, other)


def assemble(scale, row, origin, own, other):
    return pl.pallas_call(
        functools.partial(assemble_kernel, scale),
        out_shape=jax.ShapeDtypeStruct(own.shape, own.dtype),
        in_specs=[SMEM, SMEM, VMEM, VMEM],
        out_specs=VMEM,
        compiler_params=params(),
        name="assemble",
    )(row, origin, own, other)


def forward(place, after, blocks, weight):
    rows, width, lanes = blocks[0].shape
    channels = weight.shape[2]
    return pl.pallas_call(
        forward_kernel,
        out_shape=[
            jax.ShapeDtypeStruct((rows, width, lanes), F32),
            jax.ShapeDtypeStruct((rows, 2 * width, 128), BF16),
        ],
        in_specs=[SMEM] + [ANY] * 10 + [VMEM],
        out_specs=[VMEM, VMEM],
        scratch_shapes=[
            pltpu.VMEM((rows + 2, channels, lanes), BF16),
            pltpu.SemaphoreType.DMA((rows // CHUNK, 8)),
        ],
        compiler_params=params(),
        cost_estimate=cost(FLOPS, 5_000_000),
        name="forward",
    )(place, after, *blocks, weight)


def kernel_grad(place, live, rep, after, blocks, m, head):
    rows, width, lanes = m.shape
    channels = 8 * width
    return pl.pallas_call(
        kernel_grad_kernel,
        out_shape=[jax.ShapeDtypeStruct((2048, 128), F32)] * 2,
        in_specs=[SMEM] * 3 + [ANY] * 10 + [VMEM, VMEM],
        out_specs=[ANY, ANY],
        scratch_shapes=[
            pltpu.VMEM((rows + 2, channels, lanes), BF16),
            pltpu.VMEM((rows + 2, 3 * width, lanes + 256), BF16),
            pltpu.VMEM((3, 9 * width, channels), F32),
            pltpu.VMEM((4096, 128), F32),
            pltpu.SemaphoreType.DMA((rows // CHUNK, 8)),
            pltpu.SemaphoreType.DMA((2,)),
        ],
        compiler_params=params(),
        cost_estimate=cost(FLOPS, 6_000_000),
        name="kernel_grad",
    )(place, live, rep, after, *blocks, m, head)


def to_rows(x):
    f, c, h, w = x.shape
    return x.transpose(2, 1, 0, 3).reshape(h, c, f * w)


def from_rows(x):
    h, c, lanes = x.shape
    return x.reshape(h, c, lanes // 128, 128).transpose(2, 1, 0, 3)


def core_swap(x):
    return lax.ppermute(x, "rep", [(0, 1), (1, 0)])


def exchange(x):
    return lax.all_to_all(x, "dp", 0, 0, tiled=True)


def asked_for(source):
    rep = lax.axis_index("rep")
    wanted = lax.dynamic_slice_in_dim(source, rep * 8, 8, 0)
    row = jnp.maximum(wanted, 0) % 8
    origin = jnp.where(wanted < 0, 0, jnp.where(wanted // 8 == rep, 1, 2)).astype(jnp.int32)
    return row, origin


def handed_on(own, source):
    row, origin = asked_for(source)
    return pick(row, origin, own, core_swap(own))


def first_exchange(mine, theirs, payload):
    pair = (mine + core_swap(theirs)).astype(BF16).reshape(8, 256, 128)
    return jnp.concatenate([pair, payload], 1)


def both_cores(half):
    rep = lax.axis_index("rep")
    there = core_swap(half)
    low = jnp.where(rep == 0, half, there)
    high = jnp.where(rep == 0, there, half)
    return jnp.concatenate([low, high], 0)


def per_device(frames, weight, cotangent, prev_owner, lengths):
    seg_len, width, height, columns = frames.shape
    channels = weight.shape[4]
    rep, me = lax.axis_index("rep"), lax.axis_index("dp")
    member = rep * 8 + me
    tensor = Group("tensor", tensor_index, lambda i: (i // 2, i % 2))
    place = jnp.stack(tensor.absolute()).astype(jnp.int32)
    segments = jnp.arange(prev_owner.shape[0], dtype=jnp.int32)
    follows = prev_owner[None, :] == segments[:, None]
    follower = jnp.max(jnp.where(follows, segments[None, :], -1), 1)

    x = to_rows(frames)
    m = to_rows(cotangent)
    rows = weight.transpose(1, 2, 3, 0, 4)[:, ::-1].reshape(9, 3 * width, channels)

    payload, x = lax.optimization_barrier((m[:, :, :256], x))
    payload = exchange(payload)
    blocks = tensor.gather(x)
    payload, _ = lax.optimization_barrier((payload, (blocks[1], blocks[2])))
    head = exchange(handed_on(payload, follower))
    keep = jnp.arange(seg_len) < lengths[member]
    keep_head = jnp.arange(2) < lengths[jnp.maximum(follower[member], 0)]
    live = jnp.concatenate([keep, keep_head]).astype(jnp.int32)

    partials = input_partials(place, live, m, head, rows)
    partials, blocks = lax.optimization_barrier((partials, blocks))
    arrived = tensor.begin_sum(partials)
    mine, theirs = kernel_grad(place, live, rep.astype(jnp.int32)[None], partials[0], blocks, m, head)
    conv, carry = forward(place, theirs, blocks, rows)
    spread = first_exchange(mine, theirs, carry)
    arrived, spread = lax.optimization_barrier((arrived, spread))
    input_grad = from_rows(tensor.end_sum(partials, arrived))
    conv = conv.reshape(height, width, seg_len, columns).transpose(2, 1, 0, 3)
    spread, conv = lax.optimization_barrier((exchange(spread), conv))

    cells = prev_owner.shape[0] * seg_len * height * columns
    row, origin = asked_for(prev_owner)
    spread = exchange(
        assemble(1.0 / math.sqrt(cells), row, origin, spread, core_swap(spread[:, 256:]))
    )
    received = spread[:, 256:]
    total = both_cores(spread[:, :256].reshape(2048, 128))
    total = total[: 81 * width].reshape(3, 3, 3, 3, width, 128)
    weight_grad = total[:, :, ::-1].transpose(4, 0, 2, 3, 1, 5).reshape(weight.shape).astype(F32)

    received = received.reshape(height, 2, width, columns).transpose(1, 2, 0, 3).astype(F32)
    conv = conv + jnp.concatenate([received, jnp.zeros_like(received)], 0)
    output = jnp.where(keep[:, None, None, None], conv, 0.0).astype(BF16)
    return (output, input_grad, weight_grad)


def solution(mesh):
    split = P(("rep", "dp"), "tensor", None, None)
    kernel = P("tensor", None, None, None, None)
    return jax.shard_map(
        per_device,
        mesh=mesh,
        in_specs=(split, kernel, split, P(), P()),
        out_specs=(split, split, kernel),
        check_vma=False,
    )
```

```python
import functools
import math

import jax
import jax.numpy as jnp
from jax import lax
from jax.experimental import pallas as pl
from jax.experimental.pallas import tpu as pltpu
from jax.sharding import PartitionSpec as P

BF16 = jnp.bfloat16
F32 = jnp.float32
MIB = 1024 * 1024
ANY = pl.BlockSpec(memory_space=pl.ANY)
VMEM = pl.BlockSpec(memory_space=pltpu.VMEM)
SMEM = pl.BlockSpec(memory_space=pltpu.SMEM)

PLACES = ((0, 0), (0, 1), (1, 0), (3, 0), (1, 1), (3, 1), (2, 0), (2, 1))


def tensor_index(ring, pair):
    return ring * 2 + pair


class Group:
    def __init__(self, name, index_of, coords):
        self.name = name
        self.index_of = index_of
        me = lax.axis_index(name)
        self.ring, self.pair = coords(me)
        cells = [(r, p) for r in range(4) for p in range(2)]
        self.perm_up = [(index_of(r, p), index_of((r + 1) % 4, p)) for r, p in cells]
        self.perm_down = [(index_of(r, p), index_of((r + 3) % 4, p)) for r, p in cells]
        self.perm_swap = [(index_of(r, p), index_of(r, 1 - p)) for r, p in cells]

    def up(self, x):
        return lax.ppermute(x, self.name, self.perm_up)

    def down(self, x):
        return lax.ppermute(x, self.name, self.perm_down)

    def swap(self, x):
        return lax.ppermute(x, self.name, self.perm_swap)

    def absolute(self):
        return [self.index_of((self.ring + dr) % 4, self.pair ^ dp) for dr, dp in PLACES]

    def gather(self, x):
        half = x.shape[0] // 2
        following, prev, pair = lax.optimization_barrier((self.down(x), self.up(x), self.swap(x)))
        pair_next = self.swap(following)
        pair_prev = self.up(pair)
        second = self.down(following)
        far_a = self.down(pair_next[:half])
        far_b = self.up(pair_prev[half:])
        return [x, pair, following, prev, pair_next, pair_prev, second, far_a, far_b]

    def begin_sum(self, parts):
        far_a, far_b = parts[7:]
        return self.up(far_a), self.down(far_b)

    def end_sum(self, parts, arrived):
        own, pair, following, prev, pair_next, pair_prev, second = parts[:7]
        in_a, in_b = arrived
        got_swap = self.swap(added(pair_next, jnp.concatenate([in_a, jnp.zeros_like(in_a)], 0)))
        got_down = self.down(added(pair_prev, jnp.concatenate([jnp.zeros_like(in_b), in_b], 0)))
        got_up = self.up(second)
        prev, _ = lax.optimization_barrier((prev, got_swap))
        from_prev = self.down(prev)
        last_up = self.up(added(following, got_swap, got_up))
        last_swap = self.swap(added(pair, got_down))
        return sum(x.astype(F32) for x in (own, from_prev, last_up, last_swap))


def added(*terms):
    return sum(x.astype(F32) for x in terms).astype(BF16)


def shifted(x, by):
    lanes = x.shape[-1]
    column = lax.broadcasted_iota(jnp.int32, x.shape, x.ndim - 1) % 128
    rolled = pltpu.roll(x, by % lanes, x.ndim - 1)
    edge = 0 if by == 1 else 127
    return jnp.where(column == edge, 0.0, rolled)


def fill_taps(live_ref, m_ref, head_ref, taps):
    rows, width, lanes = m_ref.shape
    frames = taps.shape[2] // 128
    taps[0] = jnp.zeros(taps.shape[1:], BF16)
    taps[rows + 1] = jnp.zeros(taps.shape[1:], BF16)
    for h in range(rows):
        whole = jnp.concatenate([m_ref[h], head_ref[h]], 1).astype(F32)
        wide = jnp.concatenate(
            [
                jnp.where(live_ref[f] > 0, whole[:, f * 128 : f * 128 + 128], 0.0)
                for f in range(frames)
            ],
            1,
        )
        taps[h + 1, 0:width] = shifted(wide, -1).astype(BF16)
        taps[h + 1, width : 2 * width] = wide.astype(BF16)
        taps[h + 1, 2 * width : 3 * width] = shifted(wide, 1).astype(BF16)


def input_grad_kernel(place_ref, live_ref, m_ref, head_ref, w_ref, *rest):
    outs, (taps, wt, parts) = rest[:9], rest[9:]
    rows, width, lanes = m_ref.shape
    half = rows // 2
    fill_taps(live_ref, m_ref, head_ref, taps)
    depth = 3 * 3 * width
    for a in range(3):
        block = jnp.concatenate([w_ref[a * 3 + b] for b in range(3)], 0)
        wt[:, a * depth : (a + 1) * depth] = block.T

    for h in range(rows):
        stack = jnp.reshape(taps[h : h + 3], (depth, taps.shape[2]))
        for start in range(0, lanes, 256):
            rhs = jnp.concatenate(
                [stack[:, (2 - a) * 128 + start : (2 - a) * 128 + start + 256] for a in range(3)], 0
            )
            total = jnp.dot(wt[...], rhs, preferred_element_type=F32).astype(BF16)
            for t in range(8):
                parts[t, :, start : start + 256] = total[t * width : (t + 1) * width]
        for r in range(8):
            target = outs[r].at[h] if r < 7 else outs[7 + h // half].at[h % half]
            target[...] = parts[place_ref[r]]


def pick_kernel(row_ref, from_ref, own_ref, other_ref, out_ref):
    for d in range(out_ref.shape[0]):
        own, other = own_ref[row_ref[d]], other_ref[row_ref[d]]
        chosen = jnp.where(from_ref[d] == 1, own, other)
        out_ref[d] = jnp.where(from_ref[d] == 0, jnp.zeros_like(chosen), chosen)


def assemble_kernel(scale, row_ref, from_ref, own_ref, other_ref, out_ref):
    count, summed = own_ref.shape[0], own_ref.shape[1] - other_ref.shape[1]
    total = own_ref[0, :summed].astype(F32)
    for d in range(1, count):
        total = total + own_ref[d, :summed].astype(F32)
    share = (total * scale).astype(BF16)
    for d in range(count):
        out_ref[d, :summed] = share
        own, other = own_ref[row_ref[d], summed:], other_ref[row_ref[d]]
        chosen = jnp.where(from_ref[d] == 1, own, other)
        out_ref[d, summed:] = jnp.where(from_ref[d] == 0, jnp.zeros_like(chosen), chosen)


CHUNK = 2


def start_loads(place_ref, blocks, x, sems):
    rows, width = blocks[0].shape[0], blocks[0].shape[1]
    half = rows // 2
    x[0] = jnp.zeros(x.shape[1:], BF16)
    x[rows + 1] = jnp.zeros(x.shape[1:], BF16)
    lists = []
    for part in range(rows // CHUNK):
        first = part * CHUNK
        copies = []
        for r in range(8):
            channel = pl.ds(pl.multiple_of(place_ref[r] * width, 16), width)
            block, skip = (blocks[r], 0) if r < 7 else (blocks[7 + first // half], first // half * half)
            copies.append(
                pltpu.make_async_copy(
                    block.at[first - skip : first - skip + CHUNK],
                    x.at[first + 1 : first + 1 + CHUNK, channel],
                    sems.at[part, r],
                )
            )
            copies[-1].start()
        lists.append(copies)
    return lists


def wait_for(copies):
    for copy in copies:
        copy.wait()


def forward_kernel(place_ref, after_ref, *rest):
    del after_ref
    blocks, (w_ref, out_ref, carry_ref, x, sems) = rest[:9], rest[9:]
    rows, width, lanes = out_ref.shape
    loads = start_loads(place_ref, blocks, x, sems)
    lhs = jnp.concatenate(
        [jnp.concatenate([w_ref[a * 3 + 2 - b] for a in range(3)], 0) for b in range(3)], 1
    )
    wait_for(loads[0])
    for h in range(rows):
        if (h + 1) % CHUNK == 0 and h + 1 < rows:
            wait_for(loads[(h + 1) // CHUNK])
        stack = jnp.reshape(x[h : h + 3], (3 * x.shape[1], lanes))
        y = jnp.dot(lhs, stack, preferred_element_type=F32)
        sums = []
        for e in range(3):
            frames = []
            for g in range(lanes // 128 + 2):
                terms = []
                for a in range(3):
                    f = g + a - 2
                    if 0 <= f < lanes // 128:
                        row = (a * 3 + e) * width
                        terms.append(y[row : row + width, f * 128 : f * 128 + 128])
                total = terms[0]
                for term in terms[1:]:
                    total = total + term
                frames.append(total)
            sums.append(jnp.concatenate(frames, 1))
        result = sums[1] + shifted(sums[0], 1) + shifted(sums[2], -1)
        out_ref[h] = result[:, :lanes]
        carry_ref[h, :width] = result[:, lanes : lanes + 128].astype(BF16)
        carry_ref[h, width:] = result[:, lanes + 128 :].astype(BF16)


def kernel_grad_kernel(place_ref, live_ref, rep_ref, after_ref, *rest):
    del after_ref
    blocks, (m_ref, head_ref, mine_ref, theirs_ref, x, taps, total, result, sems, out_sems) = rest[:9], rest[9:]
    rows, width, lanes = m_ref.shape
    loads = start_loads(place_ref, blocks, x, sems)
    fill_taps(live_ref, m_ref, head_ref, taps)
    depth = 9 * width
    result[9 * depth :, :] = jnp.zeros((result.shape[0] - 9 * depth, 128), F32)
    for h in range(rows):
        if h % CHUNK == 0:
            wait_for(loads[h // CHUNK])
        stack = jnp.reshape(taps[h : h + 3], (depth, taps.shape[2]))
        right = x[h + 1]
        for a in range(3):
            left = stack[:, (2 - a) * 128 : (2 - a) * 128 + lanes]
            product = lax.dot_general(
                left, right, (((1,), (1,)), ((), ())), preferred_element_type=F32
            )
            if h == 0:
                total[a] = product
            elif h < rows - 1:
                total[a] += product
            else:
                product = total[a] + product
                for block in range(3):
                    row = (a * 3 + block) * depth
                    result[row : row + depth, :] = product[:, block * 128 : block * 128 + 128]
    half = result.shape[0] // 2
    copies = []
    for slot, (target, rep) in enumerate(((theirs_ref, 1 - rep_ref[0]), (mine_ref, rep_ref[0]))):
        source = result.at[pl.ds(pl.multiple_of(rep * half, 16), half)]
        copies.append(pltpu.make_async_copy(source, target, out_sems.at[slot]))
        copies[-1].start()
    wait_for(copies)


def params(mib):
    return pltpu.CompilerParams(vmem_limit_bytes=mib * MIB)


def cost(flops, size):
    return pl.CostEstimate(flops=flops, bytes_accessed=size, transcendentals=0)


FLOPS = 2 * 27 * 48 * 384 * 4096


def input_partials(place, live, m, head, weight):
    rows, width, lanes = m.shape
    channels = weight.shape[2]
    whole = jax.ShapeDtypeStruct((rows, width, lanes), BF16)
    half = jax.ShapeDtypeStruct((rows // 2, width, lanes), BF16)
    return pl.pallas_call(
        input_grad_kernel,
        out_shape=[whole] * 7 + [half] * 2,
        in_specs=[SMEM, SMEM, VMEM, VMEM, VMEM],
        out_specs=[VMEM] * 9,
        scratch_shapes=[
            pltpu.VMEM((rows + 2, 3 * width, lanes + 256), BF16),
            pltpu.VMEM((channels, 27 * width), BF16),
            pltpu.VMEM((8, width, lanes), BF16),
        ],
        compiler_params=params(20),
        cost_estimate=cost(FLOPS, 5_000_000),
        name="input_partials",
    )(place, live, m, head, weight)


def pick(row, origin, own, other):
    return pl.pallas_call(
        pick_kernel,
        out_shape=jax.ShapeDtypeStruct(own.shape, own.dtype),
        in_specs=[SMEM, SMEM, VMEM, VMEM],
        out_specs=VMEM,
        compiler_params=params(4),
        name="pick",
    )(row, origin, own, other)


def assemble(scale, row, origin, own, other):
    return pl.pallas_call(
        functools.partial(assemble_kernel, scale),
        out_shape=jax.ShapeDtypeStruct(own.shape, own.dtype),
        in_specs=[SMEM, SMEM, VMEM, VMEM],
        out_specs=VMEM,
        compiler_params=params(6),
        name="assemble",
    )(row, origin, own, other)


def forward(place, after, blocks, weight):
    rows, width, lanes = blocks[0].shape
    channels = weight.shape[2]
    return pl.pallas_call(
        forward_kernel,
        out_shape=[
            jax.ShapeDtypeStruct((rows, width, lanes), F32),
            jax.ShapeDtypeStruct((rows, 2 * width, 128), BF16),
        ],
        in_specs=[SMEM] + [ANY] * 10 + [VMEM],
        out_specs=[VMEM, VMEM],
        scratch_shapes=[
            pltpu.VMEM((rows + 2, channels, lanes), BF16),
            pltpu.SemaphoreType.DMA((rows // CHUNK, 8)),
        ],
        compiler_params=params(20),
        cost_estimate=cost(FLOPS, 5_000_000),
        name="forward",
    )(place, after, *blocks, weight)


def kernel_grad(place, live, rep, after, blocks, m, head):
    rows, width, lanes = m.shape
    channels = 8 * width
    return pl.pallas_call(
        kernel_grad_kernel,
        out_shape=[jax.ShapeDtypeStruct((2048, 128), F32)] * 2,
        in_specs=[SMEM] * 3 + [ANY] * 10 + [VMEM, VMEM],
        out_specs=[ANY, ANY],
        scratch_shapes=[
            pltpu.VMEM((rows + 2, channels, lanes), BF16),
            pltpu.VMEM((rows + 2, 3 * width, lanes + 256), BF16),
            pltpu.VMEM((3, 9 * width, channels), F32),
            pltpu.VMEM((4096, 128), F32),
            pltpu.SemaphoreType.DMA((rows // CHUNK, 8)),
            pltpu.SemaphoreType.DMA((2,)),
        ],
        compiler_params=params(20),
        cost_estimate=cost(FLOPS, 6_000_000),
        name="kernel_grad",
    )(place, live, rep, after, *blocks, m, head)


def to_rows(x):
    f, c, h, w = x.shape
    return x.transpose(2, 1, 0, 3).reshape(h, c, f * w)


def from_rows(x):
    h, c, lanes = x.shape
    return x.reshape(h, c, lanes // 128, 128).transpose(2, 1, 0, 3)


def core_swap(x):
    return lax.ppermute(x, "rep", [(0, 1), (1, 0)])


def exchange(x):
    return lax.all_to_all(x, "dp", 0, 0, tiled=True)


def asked_for(source):
    rep = lax.axis_index("rep")
    wanted = lax.dynamic_slice_in_dim(source, rep * 8, 8, 0)
    row = jnp.maximum(wanted, 0) % 8
    origin = jnp.where(wanted < 0, 0, jnp.where(wanted // 8 == rep, 1, 2)).astype(jnp.int32)
    return row, origin


def handed_on(own, source):
    row, origin = asked_for(source)
    return pick(row, origin, own, core_swap(own))


def first_exchange(mine, theirs, payload):
    pair = (mine + core_swap(theirs)).astype(BF16).reshape(8, 256, 128)
    return jnp.concatenate([pair, payload], 1)


def both_cores(spread):
    rep = lax.axis_index("rep")
    there = core_swap(spread)
    half, there = (x[:, :256].reshape(2048, 128) for x in (spread, there))
    low = jnp.where(rep == 0, half, there)
    high = jnp.where(rep == 0, there, half)
    return jnp.concatenate([low, high], 0)


def per_device(frames, weight, cotangent, prev_owner, lengths):
    seg_len, width, height, columns = frames.shape
    channels = weight.shape[4]
    rep, me = lax.axis_index("rep"), lax.axis_index("dp")
    member = rep * 8 + me
    tensor = Group("tensor", tensor_index, lambda i: (i // 2, i % 2))
    place = jnp.stack(tensor.absolute()).astype(jnp.int32)
    segments = jnp.arange(prev_owner.shape[0], dtype=jnp.int32)
    follows = prev_owner[None, :] == segments[:, None]
    follower = jnp.max(jnp.where(follows, segments[None, :], -1), 1)

    x = to_rows(frames)
    m = to_rows(cotangent)
    rows = weight.transpose(1, 2, 3, 0, 4)[:, ::-1].reshape(9, 3 * width, channels)

    payload, x = lax.optimization_barrier((m[:, :, :256], x))
    payload = exchange(payload)
    blocks = tensor.gather(x)
    payload, _ = lax.optimization_barrier((payload, (blocks[1], blocks[2])))
    head = exchange(handed_on(payload, follower))
    keep = jnp.arange(seg_len) < lengths[member]
    keep_head = jnp.arange(2) < lengths[jnp.maximum(follower[member], 0)]
    live = jnp.concatenate([keep, keep_head]).astype(jnp.int32)

    partials = input_partials(place, live, m, head, rows)
    partials, blocks = lax.optimization_barrier((partials, blocks))
    arrived = tensor.begin_sum(partials)
    mine, theirs = kernel_grad(place, live, rep.astype(jnp.int32)[None], partials[0], blocks, m, head)
    conv, carry = forward(place, theirs, blocks, rows)
    spread = first_exchange(mine, theirs, carry)
    arrived, spread = lax.optimization_barrier((arrived, spread))
    input_grad = from_rows(tensor.end_sum(partials, arrived))
    conv = conv.reshape(height, width, seg_len, columns).transpose(2, 1, 0, 3)
    spread = exchange(spread)

    cells = prev_owner.shape[0] * seg_len * height * columns
    row, origin = asked_for(prev_owner)
    spread = exchange(
        assemble(1.0 / math.sqrt(cells), row, origin, spread, core_swap(spread[:, 256:]))
    )
    received = spread[:, 256:]
    total = both_cores(spread)
    total = total[: 81 * width].reshape(3, 3, 3, 3, width, 128)
    weight_grad = total[:, :, ::-1].transpose(4, 0, 2, 3, 1, 5).reshape(weight.shape).astype(F32)

    received = received.reshape(height, 2, width, columns).transpose(1, 2, 0, 3).astype(F32)
    conv = conv + jnp.concatenate([received, jnp.zeros_like(received)], 0)
    output = jnp.where(keep[:, None, None, None], conv, 0.0).astype(BF16)
    return (output, input_grad, weight_grad)


def solution(mesh):
    split = P(("rep", "dp"), "tensor", None, None)
    kernel = P("tensor", None, None, None, None)
    return jax.shard_map(
        per_device,
        mesh=mesh,
        in_specs=(split, kernel, split, P(), P()),
        out_specs=(split, split, kernel),
        check_vma=False,
    )
```
